32 devices in a mesh: dp: 32 (over z, y, x, core).
Axes of the slice: x: 2, y: 2, z: 4, core: 2. Of those that a mesh axis runs over, the one named last changes fastest.
Arguments:
- targets: bfloat16 [32768, 512], P('dp')
- memory: bfloat16 [32768, 512], P('dp'), may hold values from -6 to 6
- target_ids: int32 [32768], P('dp'), may hold values from 0 to 7, as said below
- memory_ids: int32 [32768], P('dp'), may hold values from 0 to 7, as said below
- cotangent: bfloat16 [32768, 512], P('dp'), may hold values from -6 to 6
- params: float32 [4203008], P('dp')
- first_moment: float32 [4203008], P('dp')
- second_moment: float32 [4203008], P('dp')
Outputs:
- layer_out: bfloat16 [32768, 512], P('dp')
- input_grad: bfloat16 [32768, 512], P('dp')
- memory_grad: bfloat16 [32768, 512], P('dp')
- grad_norm: float32 [], replicated
- param_grad: float32 [4203008], P('dp')
- vector_grad: float32 [8704], replicated
- new_params: float32 [4203008], P('dp')
- new_first: float32 [4203008], P('dp')
- new_second: float32 [4203008], P('dp')
- params_low: bfloat16 [4203008], P('dp')
The draws below stay inside these ranges and needn't reach their ends.
Inputs may be any that keep to these rules, and one draw needn't show every extreme that they name: `target_ids`: within each sequence of 1024 target tokens the ids start at 0 and rise by 0 or 1 from token to token; the same sequence's memory tokens carry exactly the same set of ids in the same way. `memory_ids`: within each sequence of 1024 memory tokens the ids start at 0 and rise by 0 or 1 from token to token, with the same set of ids as the sequence's target tokens.
All inputs are finite; a program needn't handle non-finite values.
Results may differ from the reference program's by a relative error of at most 0.018.
The reference program's roundings to bfloat16 on the way count: a program that leaves them out, or rounds other values in their place, can miss the bound.
Values may be sent and summed in bfloat16 or wider, within the bound.
No kernel may reach another device: no remote copies, remote signals or barrier semaphores. Data moves between devices by JAX's collectives and lax.ppermute only.
A program may use at most 192 MiB of HBM per device.

```python
import functools
import math
import jax
import jax.numpy as jnp
from jax import lax

D = 512
FF = 2048
HEADS = 8
LEN = 1024
MLEN = 1024
STEP = 10
TOKENS = 32768
MTOKENS = 32768
NPARAMS = 4203008


def draw_targets(key, part):
    column = jnp.arange(D, dtype=jnp.float32) / (D - 1)
    column_scale = jnp.exp(jnp.log(3.0) * (column - 0.5))
    base = jax.random.normal(key, (TOKENS, D), jnp.float32)
    return (base * column_scale[None, :]).astype(jnp.bfloat16)


def segment_pair(key):
    rows = TOKENS // LEN
    counts = jax.random.randint(jax.random.fold_in(key, 5), (rows,), 1, 9)
    counts = jnp.where(jnp.arange(rows) == 0, 8, counts)
    live = jnp.arange(7)[None, :] < (counts - 1)[:, None]

    def ids_for(sub_key, length):
        cuts = jax.vmap(lambda row_key: jax.random.permutation(row_key, length - 1)[:7] + 1)(jax.random.split(sub_key, rows))
        places = jnp.arange(length)
        above = (cuts[:, None, :] <= places[None, :, None]) & live[:, None, :]
        return jnp.sum(above.astype(jnp.int32), axis=2).reshape(rows * length).astype(jnp.int32)
    return (ids_for(jax.random.fold_in(key, 6), LEN), ids_for(jax.random.fold_in(key, 7), MLEN))


def draw_target_ids(key, part):
    return segment_pair(jax.random.fold_in(key, 11))[0]


def draw_memory_ids(key, part):
    return segment_pair(jax.random.fold_in(key, 11))[1]


def draw_params(key, part):
    square = D * D
    start_in = 8 * square
    start_out = start_in + D * FF
    start_vec = start_out + FF * D
    place = jnp.arange(NPARAMS)
    matrix = place // square
    base = jax.random.normal(jax.random.fold_in(key, 1), (NPARAMS,), jnp.float32)
    gains = jax.random.uniform(jax.random.fold_in(key, 2), (NPARAMS,), jnp.float32, 0.6, 1.4)
    attn_scale = jnp.where((matrix == 3) | (matrix == 7), 4.0, 1.0) / math.sqrt(D)
    scale = jnp.where(place < start_in, attn_scale, jnp.where(place < start_out, 1.0 / math.sqrt(D), jnp.where(place < start_vec, 1.5 / math.sqrt(FF), 0.2)))
    offset = place - start_vec
    is_gain = (place >= start_vec) & (offset < 6 * D) & (offset // D % 2 == 0)
    return jnp.where(is_gain, gains, base * scale).astype(jnp.float32)


def moment_scale():
    place = jnp.arange(NPARAMS)
    return jnp.where(place >= 8 * D * D + 2 * D * FF, 4.0, 1.0) / math.sqrt(NPARAMS)


def draw_first_moment(key, part):
    base = jax.random.normal(key, (NPARAMS,), jnp.float32)
    return (base * 0.11 * moment_scale()).astype(jnp.float32)


def draw_second_moment(key, part):
    factor = jnp.exp(jax.random.uniform(key, (NPARAMS,), jnp.float32, math.log(0.5), math.log(2.0)))
    grad_size = moment_scale()
    return (factor * 0.002 * grad_size * grad_size).astype(jnp.float32)


def level_of(stream_key, dims, cuts, least, largest):
    loudness, own = 1.0, jax.random.fold_in(stream_key, 6)
    for position, blocks in cuts:
        draws = jnp.exp(jax.random.uniform(jax.random.fold_in(own, position), (blocks,), jnp.float32, least / len(cuts), largest / len(cuts)))
        loudness = loudness * jnp.repeat(draws, dims[position] // blocks).reshape([-1 if axis == position else 1 for axis in range(len(dims))])
    return loudness


def normal_values(stream_key, shape, scale, reach, cuts=(), kind=jnp.bfloat16):
    values = jax.random.normal(stream_key, shape, jnp.float32) * scale
    if len(cuts) > 0:
        values = level_of(stream_key, shape, cuts, -0.22, 0.18) * values
    return jnp.clip(values, min=-reach, max=reach).astype(kind)


def setup_inputs(seed: int = 0) -> dict:
    key_list = jax.random.split(jax.random.key(seed), 9)
    targets = draw_targets(jax.random.fold_in(key_list[8], 71), 0)
    memory = normal_values(key_list[1], (MTOKENS, D), 1.0, 6.0, ((0, 32),))
    target_ids = draw_target_ids(jax.random.fold_in(key_list[8], 71), 0)
    memory_ids = draw_memory_ids(jax.random.fold_in(key_list[8], 71), 0)
    cotangent = normal_values(key_list[4], (TOKENS, D), 1.0, 6.0, ((0, 32),))
    params = draw_params(jax.random.fold_in(key_list[8], 71), 0)
    first_moment = draw_first_moment(jax.random.fold_in(key_list[8], 71), 0)
    second_moment = draw_second_moment(jax.random.fold_in(key_list[8], 71), 0)
    return {"targets": targets, "memory": memory, "target_ids": target_ids, "memory_ids": memory_ids, "cotangent": cotangent, "params": params, "first_moment": first_moment, "second_moment": second_moment}


@jax.custom_vjp
def low(v):
    return lax.optimization_barrier(v.astype(jnp.bfloat16)).astype(jnp.float32)

@jax.custom_vjp
def low_back(v):
    return v

def low_keep(v):
    return (low(v), None)

def low_pass(kept, grad):
    return (grad,)

def back_keep(v):
    return (v, None)

def back_low(kept, grad):
    return (low(grad),)
low.defvjp(low_keep, low_pass)
low_back.defvjp(back_keep, back_low)
eps_norm = 1e-05
beta_one = 0.9
beta_two = 0.999
adam_eps = 1e-08
step_rate = 0.05
weight_decay = 0.01
clip_limit = 1.0
masked_value = -1e+30
highest = lax.Precision.HIGHEST

def matmul(left_op, right_op):
    return jnp.dot(left_op, right_op, preferred_element_type=jnp.float32, precision=highest)

def layer_norm(residual, norm_gain, norm_shift):
    center = residual - lax.optimization_barrier(jnp.mean(residual, axis=1, keepdims=True))
    inv_std = lax.rsqrt(lax.optimization_barrier(jnp.mean(center * center, axis=1, keepdims=True)) + eps_norm)
    return center * inv_std * norm_gain + norm_shift

def attend(query_seq, key_seq, value_seq, query_ids, key_ids, causal):
    head_dim = D // HEADS
    query_len = query_seq.shape[0]
    key_len = key_seq.shape[0]
    query_heads = query_seq.reshape(query_len, HEADS, head_dim)
    key_heads = key_seq.reshape(key_len, HEADS, head_dim)
    value_heads = value_seq.reshape(key_len, HEADS, head_dim)
    raw_scores = jnp.einsum('qhd,khd->hqk', query_heads, key_heads, precision=highest) * head_dim ** (-0.5)
    scores = low_back(raw_scores)
    allowed = query_ids[:, None] == key_ids[None, :]
    if causal:
        allowed = allowed & (jnp.arange(key_len)[None, :] <= jnp.arange(query_len)[:, None])
    masked = jnp.where(allowed[None], scores, masked_value)
    row_max = lax.optimization_barrier(jnp.max(masked, axis=2, keepdims=True))
    exp_scores = jnp.exp(masked - row_max)
    weights = low(exp_scores / lax.optimization_barrier(jnp.sum(exp_scores, axis=2, keepdims=True)))
    mixed_rows = jnp.einsum('hqk,khd->qhd', weights, value_heads, precision=highest)
    return mixed_rows.reshape(query_len, D)

def layer_group(inputs, memory_rows, flat, target_ids, memory_ids):
    square = D * D
    start_in = 8 * square
    start_out = start_in + D * FF
    start_vec = start_out + FF * D
    weights = low(flat)
    matrices = weights[:start_in].reshape(8, D, D)
    w_in = weights[start_in:start_out].reshape(D, FF)
    w_out = weights[start_out:start_vec].reshape(FF, D)
    vec_rows = weights[start_vec:start_vec + 12 * D].reshape(12, D)
    bias_in = weights[start_vec + 12 * D:start_vec + 12 * D + FF]
    bias_out = weights[start_vec + 12 * D + FF:]
    seq_count = inputs.shape[0] // LEN

    def heads_all(query_rows, key_rows, value_rows, query_ids, key_ids, causal, key_len):
        attend_fn = jax.checkpoint(functools.partial(attend, causal=causal))
        mixed_rows = jax.vmap(attend_fn)(query_rows.reshape(seq_count, LEN, D), key_rows.reshape(seq_count, key_len, D), value_rows.reshape(seq_count, key_len, D), query_ids.reshape(seq_count, LEN), key_ids.reshape(seq_count, key_len))
        return mixed_rows.reshape(seq_count * LEN, D)
    self_query = low(low_back(matmul(inputs, matrices[0]) + vec_rows[6]))
    self_key = low(low_back(matmul(inputs, matrices[1])))
    self_value = low(low_back(matmul(inputs, matrices[2]) + vec_rows[7]))
    self_mixed = low(low_back(heads_all(self_query, self_key, self_value, target_ids, target_ids, True, LEN)))
    self_branch = low_back(matmul(self_mixed, matrices[3]) + vec_rows[8])
    first_norm = layer_norm(inputs + self_branch, vec_rows[0], vec_rows[1])
    first_low = low(first_norm)
    cross_query = low(low_back(matmul(first_low, matrices[4]) + vec_rows[9]))
    cross_key = low(low_back(matmul(memory_rows, matrices[5])))
    cross_value = low(low_back(matmul(memory_rows, matrices[6]) + vec_rows[10]))
    cross_mixed = low(low_back(heads_all(cross_query, cross_key, cross_value, target_ids, memory_ids, False, MLEN)))
    cross_branch = low_back(matmul(cross_mixed, matrices[7]) + vec_rows[11])
    second_norm = layer_norm(first_norm + cross_branch, vec_rows[2], vec_rows[3])
    second_low = low(second_norm)
    hidden_pre = low_back(matmul(second_low, w_in) + bias_in)
    hidden_low = low(jax.nn.silu(hidden_pre))
    ffn_branch = low_back(matmul(hidden_low, w_out) + bias_out)
    return layer_norm(second_norm + ffn_branch, vec_rows[4], vec_rows[5])

def reference(targets, memory, target_ids, memory_ids, cotangent, params, first_moment, second_moment):
    seqs_all = TOKENS // LEN
    group = math.gcd(seqs_all, max(1, 4096 // LEN))
    groups = seqs_all // group
    start_vec = 8 * D * D + 2 * D * FF

    def one_group(grad_sum, pieces):
        target_rows, memory_rows, target_seg, memory_seg, grad_rows = pieces

        def forward_fn(first_arg, second_arg, third_arg):
            return layer_group(first_arg, second_arg, third_arg, target_seg, memory_seg)
        output_rows, pullback = jax.vjp(forward_fn, target_rows, memory_rows, params)
        grad_target, grad_memory, grad_params = pullback(grad_rows)
        return (grad_sum + grad_params, (output_rows.astype(jnp.bfloat16), grad_target.astype(jnp.bfloat16), grad_memory.astype(jnp.bfloat16)))
    pieces = (targets.astype(jnp.float32).reshape(groups, group * LEN, D), memory.astype(jnp.float32).reshape(groups, group * MLEN, D), target_ids.reshape(groups, group * LEN), memory_ids.reshape(groups, group * MLEN), cotangent.astype(jnp.float32).reshape(groups, group * LEN, D))
    grad_total, (layer_rows, input_rows, memory_grad_rows) = lax.scan(one_group, jnp.zeros((NPARAMS,), jnp.float32), pieces)
    norm_value = jnp.sqrt(jnp.sum(grad_total * grad_total))
    factor = jnp.minimum(1.0, clip_limit / (norm_value + 1e-06))
    clipped = grad_total * factor
    new_first = beta_one * first_moment + (1.0 - beta_one) * clipped
    new_second = beta_two * second_moment + (1.0 - beta_two) * clipped * clipped
    first_hat = new_first / (1.0 - beta_one ** STEP)
    second_hat = new_second / (1.0 - beta_two ** STEP)
    new_params = params - step_rate * (first_hat / (jnp.sqrt(second_hat) + adam_eps) + weight_decay * params)
    return (layer_rows.reshape(TOKENS, D), input_rows.reshape(TOKENS, D), memory_grad_rows.reshape(MTOKENS, D), norm_value, grad_total, grad_total[start_vec:], new_params, new_first, new_second, new_params.astype(jnp.bfloat16))
```

```python
import functools
import jax
import jax.numpy as jnp
from jax import lax
from jax.experimental import pallas as pl
from jax.experimental.pallas import tpu as pltpu
from jax.sharding import PartitionSpec as P

D = 512
FF = 2048
HEADS = 8
LEN = 1024
STEP = 10
ROWS = 256
BLOCKS = LEN // ROWS
LANES = 128
PAIRS = D // LANES
MASK_LANE = 32

eps_norm = 1e-05
beta_one = 0.9
beta_two = 0.999
adam_eps = 1e-08
step_rate = 0.05
weight_decay = 0.01
clip_limit = 1.0
masked_value = -1e30
log2_e = 1.4426950408889634
query_scale = 0.125 * log2_e
key_scale = 1.0 / log2_e

BF = jnp.bfloat16
F32 = jnp.float32
VMEM_BYTES = 60 * 1024 * 1024


def nn(a, b):
    return jnp.dot(a, b, preferred_element_type=F32)


def nt(a, b):
    return lax.dot_general(a, b, (((1,), (1,)), ((), ())), preferred_element_type=F32)


def tn(a, b):
    return lax.dot_general(a, b, (((0,), (0,)), ((), ())), preferred_element_type=F32)


def layer_norm(resid):
    center = resid - jnp.mean(resid, axis=1, keepdims=True)
    inv_std = lax.rsqrt(jnp.mean(center * center, axis=1, keepdims=True) + eps_norm)
    return center * inv_std, inv_std


def norm_back(grad, normed, inv_std, gain):
    scaled = grad * gain
    return inv_std * (
        scaled
        - jnp.mean(scaled, axis=1, keepdims=True)
        - normed * jnp.mean(scaled * normed, axis=1, keepdims=True)
    )


def half_row(parity):
    lane = lax.broadcasted_iota(jnp.int32, (1, LANES), 1)
    inside = (lane // 64) == parity
    return jnp.where(inside, 1.0, 0.0).astype(BF)


def lane_row(first, count):
    lane = lax.broadcasted_iota(jnp.int32, (1, LANES), 1)
    inside = (lane >= first) & (lane < first + count)
    return jnp.where(inside, 1.0, 0.0).astype(BF)


def causal_bias(transposed):
    row = lax.broadcasted_iota(jnp.int32, (ROWS, ROWS), 0)
    col = lax.broadcasted_iota(jnp.int32, (ROWS, ROWS), 1)
    ok = (row <= col) if transposed else (col <= row)
    return jnp.where(ok, 0.0, masked_value)


def attend_forward(q_ref, k_ref, v_ref, qa_ref, ka_ref, o_ref, qal_ref, causal):
    lane = lax.broadcasted_iota(jnp.int32, (ROWS, LANES), 1)
    low = lane < 64
    bias = causal_bias(False) if causal else None
    for qb in range(BLOCKS):
        rows = pl.ds(qb * ROWS, ROWS)
        keys = (qb + 1) * ROWS if causal else LEN
        qa = qa_ref[rows, :]

        def one_pair(pair, lse_parts):
            lanes = pl.ds(pl.multiple_of(pair * LANES, LANES), LANES)
            q_pair = q_ref[rows, lanes]
            k_cat = jnp.concatenate([k_ref[:keys, lanes], ka_ref[:keys, :]], axis=1)
            v_pair = v_ref[:keys, lanes]
            outs = []
            for parity in range(2):
                half = half_row(parity)
                head = pair * 2 + parity
                q_cat = jnp.concatenate([q_pair * half, qa], axis=1)
                scores = nt(q_cat, k_cat)
                if causal:
                    diag = scores[:, keys - ROWS :] + bias
                    scores = (
                        jnp.concatenate([scores[:, : keys - ROWS], diag], axis=1) if qb else diag
                    )
                top = jnp.max(scores, axis=1, keepdims=True)
                probs = jnp.exp2(scores - top).astype(BF)
                mixed = nn(probs, v_pair * half + (1.0 - half).astype(BF))
                turned = pltpu.roll(mixed, 64, 1)
                outs.append(mixed / turned)
                total = turned if parity == 0 else mixed
                lse = -(top + jnp.log2(total))
                first = lse.astype(BF).astype(F32)
                rest = lse - first
                second = rest.astype(BF).astype(F32)
                base = head * 3
                lse_parts = jnp.where(lane == base, first, lse_parts)
                lse_parts = jnp.where(lane == base + 1, second, lse_parts)
                lse_parts = jnp.where(lane == base + 2, rest - second, lse_parts)
            o_ref[rows, lanes] = jnp.where(low, outs[0], outs[1]).astype(BF)
            return lse_parts

        lse_parts = lax.fori_loop(0, PAIRS, one_pair, jnp.zeros((ROWS, LANES), F32))
        qal_ref[rows, :] = (qa.astype(F32) + lse_parts).astype(BF)


def attend_backward(
    q_ref, k_ref, v_ref, do_ref, qal_ref, del_ref, ka_ref, dq_ref, dk_ref, dv_ref, p_ref, s_ref, causal
):
    bias = causal_bias(True) if causal else None

    def one_pair(pair, carry):
        lanes = pl.ds(pl.multiple_of(pair * LANES, LANES), LANES)
        k_pair = k_ref[:, lanes]
        k_turn = k_pair.T
        v_pair = v_ref[:, lanes]
        dq_parts = [[], []]
        for parity in range(2):
            head = pair * 2 + parity
            half = half_row(parity)
            k_cat = jnp.concatenate([k_pair * half, ka_ref[...] + lane_row(head * 3, 3)], axis=1)
            ones = jnp.broadcast_to(lane_row(head * 2, 2), (LEN, LANES))
            v_cat = jnp.concatenate([v_pair * half, ones], axis=1)
            for qb in range(BLOCKS):
                rows = pl.ds(qb * ROWS, ROWS)
                keys = (qb + 1) * ROWS if causal else LEN
                q_cat = jnp.concatenate([q_ref[rows, lanes], qal_ref[rows, :]], axis=1)
                do_cat = jnp.concatenate([do_ref[rows, lanes], del_ref[rows, :]], axis=1)
                scores = nt(k_cat[:keys], q_cat)
                if causal:
                    diag = scores[keys - ROWS :] + bias
                    scores = jnp.concatenate([scores[: keys - ROWS], diag], axis=0) if qb else diag
                probs = jnp.exp2(scores)
                p_ref[parity, :keys, rows] = probs.astype(BF)
                grads = (probs * nt(v_cat[:keys], do_cat)).astype(BF)
                s_ref[parity, :keys, rows] = grads
                dq_parts[parity].append(
                    nn(k_turn[parity * 64 : parity * 64 + 64, :keys], grads)
                )
        for qb in range(BLOCKS):
            rows = pl.ds(qb * ROWS, ROWS)
            dq = jnp.concatenate([dq_parts[0][qb], dq_parts[1][qb]], axis=0) * 0.125
            dq_ref[rows, lanes] = dq.T.astype(BF)
        for kb in range(BLOCKS):
            rows = pl.ds(kb * ROWS, ROWS)
            first = kb * ROWS if causal else 0
            tail = pl.ds(first, LEN - first)
            do_pair = do_ref[tail, lanes]
            q_pair = q_ref[tail, lanes]
            dv = nn(p_ref[0, rows, tail], do_pair * half_row(0))
            dv = dv + nn(p_ref[1, rows, tail], do_pair * half_row(1))
            dv_ref[rows, lanes] = dv.astype(BF)
            dk = nn(s_ref[0, rows, tail], q_pair * half_row(0))
            dk = dk + nn(s_ref[1, rows, tail], q_pair * half_row(1))
            dk_ref[rows, lanes] = (dk * key_scale).astype(BF)
        return carry

    lax.fori_loop(0, PAIRS, one_pair, 0)


def mix_gradient(g_ref, w_out, o_ref, do_ref, del_ref):
    lane = lax.broadcasted_iota(jnp.int32, (ROWS, LANES), 1)
    even = lane % 2 == 0
    col = lax.broadcasted_iota(jnp.int32, (D, LANES), 0) // 64
    pick = jnp.where(lax.broadcasted_iota(jnp.int32, (D, LANES), 1) // 2 == col, -1.0, 0.0).astype(BF)
    for qb in range(BLOCKS):
        rows = pl.ds(qb * ROWS, ROWS)
        do = nt(g_ref[rows, :], w_out).astype(BF)
        do_ref[rows, :] = do
        prod = do.astype(F32) * o_ref[rows, :].astype(F32)
        high = prod.astype(BF)
        inner = nn(high, pick) + nn((prod - high.astype(F32)).astype(BF), pick)
        first = inner.astype(BF).astype(F32)
        del_ref[rows, :] = jnp.where(even, first, inner - first).astype(BF)


def vec_row(vec_ref, index):
    return vec_ref[index : index + 1, :].astype(F32)


def self_forward_kernel(x_ref, w_ref, vec_ref, qa_ref, ka_ref, q_ref, k_ref, v_ref, o_ref, qal_ref, n_ref, r_ref):
    for qb in range(BLOCKS):
        rows = pl.ds(qb * ROWS, ROWS)
        x = x_ref[rows, :]
        q_ref[rows, :] = ((nn(x, w_ref[0]) + vec_row(vec_ref, 6)) * query_scale).astype(BF)
        k_ref[rows, :] = nn(x, w_ref[1]).astype(BF)
        v_ref[rows, :] = (nn(x, w_ref[2]) + vec_row(vec_ref, 7)).astype(BF)
    attend_forward(q_ref, k_ref, v_ref, qa_ref, ka_ref, o_ref, qal_ref, True)
    for qb in range(BLOCKS):
        rows = pl.ds(qb * ROWS, ROWS)
        resid = x_ref[rows, :].astype(F32) + nn(o_ref[rows, :], w_ref[3]) + vec_row(vec_ref, 8)
        normed, inv_std = layer_norm(resid)
        n_ref[rows, :] = normed
        r_ref[rows, :] = jnp.broadcast_to(inv_std, (ROWS, LANES))


def cross_forward_kernel(n1_ref, m_ref, w_ref, vec_ref, qa_ref, ka_ref, q_ref, k_ref, v_ref, o_ref, qal_ref, n_ref, r_ref):
    for qb in range(BLOCKS):
        rows = pl.ds(qb * ROWS, ROWS)
        h = (n1_ref[rows, :] * vec_row(vec_ref, 0) + vec_row(vec_ref, 1)).astype(BF)
        m = m_ref[rows, :]
        q_ref[rows, :] = ((nn(h, w_ref[0]) + vec_row(vec_ref, 9)) * query_scale).astype(BF)
        k_ref[rows, :] = nn(m, w_ref[1]).astype(BF)
        v_ref[rows, :] = (nn(m, w_ref[2]) + vec_row(vec_ref, 10)).astype(BF)
    attend_forward(q_ref, k_ref, v_ref, qa_ref, ka_ref, o_ref, qal_ref, False)
    for qb in range(BLOCKS):
        rows = pl.ds(qb * ROWS, ROWS)
        h = n1_ref[rows, :] * vec_row(vec_ref, 0) + vec_row(vec_ref, 1)
        resid = h + nn(o_ref[rows, :], w_ref[3]) + vec_row(vec_ref, 11)
        normed, inv_std = layer_norm(resid)
        n_ref[rows, :] = normed
        r_ref[rows, :] = jnp.broadcast_to(inv_std, (ROWS, LANES))


def col_sum(x):
    return jnp.sum(x.astype(F32), axis=0, keepdims=True)


def ffn_kernel(n2_ref, r2_ref, cot_ref, w1_ref, w2_ref, vec_ref, out_ref, dw1_ref, dw2_ref, dr_ref, vg_ref, u_ref, da_ref, h_ref, dz_ref, f_ref):
    def w1_block(j):
        return w1_ref[:, j].reshape(D, D)

    vg_ref[...] = jnp.zeros_like(vg_ref)

    def one_tile(tile, carry):
        rows = pl.ds(pl.multiple_of(tile * ROWS, ROWS), ROWS)
        n2 = n2_ref[rows, :]
        h2 = n2 * vec_row(vec_ref, 2) + vec_row(vec_ref, 3)
        h2_low = h2.astype(BF)
        h_ref[rows, :] = h2_low
        resid = h2 + vec_row(vec_ref, 16)
        for j in range(4):
            a = nn(h2_low, w1_block(j)) + vec_row(vec_ref, 12 + j)
            s = 0.5 * jnp.tanh(0.5 * a) + 0.5
            u = (a * s).astype(BF)
            u_ref[rows, j * D : (j + 1) * D] = u
            f_ref[:, j * D : (j + 1) * D] = s * (1.0 + a * (1.0 - s))
            resid = resid + nn(u, w2_ref[j * D : (j + 1) * D, :])
        n3, inv3 = layer_norm(resid)
        gain3 = vec_row(vec_ref, 4)
        out_ref[rows, :] = (n3 * gain3 + vec_row(vec_ref, 5)).astype(BF)
        cot = cot_ref[rows, :].astype(F32)
        dr3 = norm_back(cot, n3, inv3, gain3)
        dz = dr3.astype(BF)
        dz_ref[rows, :] = dz
        vg_ref[4:5, :] += col_sum(cot * n3)
        vg_ref[5:6, :] += col_sum(cot)
        vg_ref[16:17, :] += col_sum(dz)
        dh = dr3
        for j in range(4):
            da = (nt(dz, w2_ref[j * D : (j + 1) * D, :]) * f_ref[:, j * D : (j + 1) * D]).astype(BF)
            da_ref[rows, j * D : (j + 1) * D] = da
            vg_ref[12 + j : 13 + j, :] += col_sum(da)
            dh = dh + nt(da, w1_block(j))
        vg_ref[2:3, :] += col_sum(dh * n2)
        vg_ref[3:4, :] += col_sum(dh)
        dr2 = norm_back(dh, n2, r2_ref[rows, 0:1], vec_row(vec_ref, 2))
        dr_ref[rows, :] = dr2
        vg_ref[11:12, :] += col_sum(dr2.astype(BF))
        return carry

    lax.fori_loop(0, BLOCKS, one_tile, 0)
    h_turn = h_ref[...].T
    for j in range(4):
        cols = pl.ds(j * D, D)
        dw1 = nn(h_turn, da_ref[:, cols]).astype(BF)
        dw1_ref[:, j] = dw1.reshape(8, 64, D)
        dw2_ref[cols, :] = tn(u_ref[:, cols], dz_ref[...]).astype(BF)


def cross_backward_kernel(
    dr2_ref, w_ref, vec_ref, q_ref, k_ref, v_ref, o_ref, qal_ref, ka_ref, n1_ref, r1_ref, mt_ref,
    dw_ref, mg_ref, dr1_ref, vg_ref,
    g_ref, do_ref, del_ref, dq_ref, dk_ref, dv_ref, p_ref, s_ref, h_ref,
):
    for qb in range(BLOCKS):
        rows = pl.ds(qb * ROWS, ROWS)
        g_ref[rows, :] = dr2_ref[rows, :].astype(BF)
        h_ref[rows, :] = (n1_ref[rows, :] * vec_row(vec_ref, 0) + vec_row(vec_ref, 1)).astype(BF)
    mix_gradient(g_ref, w_ref[3], o_ref, do_ref, del_ref)
    dw_ref[3] = tn(o_ref[...], g_ref[...]).astype(BF)
    attend_backward(
        q_ref, k_ref, v_ref, do_ref, qal_ref, del_ref, ka_ref, dq_ref, dk_ref, dv_ref, p_ref, s_ref, False
    )
    dw_ref[0] = tn(h_ref[...], dq_ref[...]).astype(BF)
    dw_ref[1] = nn(mt_ref[...], dk_ref[...]).astype(BF)
    dw_ref[2] = nn(mt_ref[...], dv_ref[...]).astype(BF)
    vg_ref[...] = jnp.zeros_like(vg_ref)
    for qb in range(BLOCKS):
        rows = pl.ds(qb * ROWS, ROWS)
        dq = dq_ref[rows, :]
        dk = dk_ref[rows, :]
        dv = dv_ref[rows, :]
        mg_ref[rows, :] = (nt(dk, w_ref[1]) + nt(dv, w_ref[2])).astype(BF)
        vg_ref[9:10, :] += col_sum(dq)
        vg_ref[10:11, :] += col_sum(dv)
        dh = dr2_ref[rows, :] + nt(dq, w_ref[0])
        n1 = n1_ref[rows, :]
        vg_ref[0:1, :] += col_sum(dh * n1)
        vg_ref[1:2, :] += col_sum(dh)
        dr1 = norm_back(dh, n1, r1_ref[rows, 0:1], vec_row(vec_ref, 0))
        dr1_ref[rows, :] = dr1
        vg_ref[8:9, :] += col_sum(dr1.astype(BF))


def self_backward_kernel(
    dr1_ref, w_ref, q_ref, k_ref, v_ref, o_ref, qal_ref, ka_ref, xt_ref,
    dw_ref, ig_ref, vg_ref,
    g_ref, do_ref, del_ref, dq_ref, dk_ref, dv_ref, p_ref, s_ref,
):
    for qb in range(BLOCKS):
        rows = pl.ds(qb * ROWS, ROWS)
        g_ref[rows, :] = dr1_ref[rows, :].astype(BF)
    mix_gradient(g_ref, w_ref[3], o_ref, do_ref, del_ref)
    dw_ref[3] = tn(o_ref[...], g_ref[...]).astype(BF)
    attend_backward(
        q_ref, k_ref, v_ref, do_ref, qal_ref, del_ref, ka_ref, dq_ref, dk_ref, dv_ref, p_ref, s_ref, True
    )
    dw_ref[0] = nn(xt_ref[...], dq_ref[...]).astype(BF)
    dw_ref[1] = nn(xt_ref[...], dk_ref[...]).astype(BF)
    dw_ref[2] = nn(xt_ref[...], dv_ref[...]).astype(BF)
    vg_ref[...] = jnp.zeros_like(vg_ref)
    for qb in range(BLOCKS):
        rows = pl.ds(qb * ROWS, ROWS)
        dq = dq_ref[rows, :]
        dk = dk_ref[rows, :]
        dv = dv_ref[rows, :]
        ig_ref[rows, :] = (
            dr1_ref[rows, :] + nt(dq, w_ref[0]) + nt(dk, w_ref[1]) + nt(dv, w_ref[2])
        ).astype(BF)
        vg_ref[6:7, :] += col_sum(dq)
        vg_ref[7:8, :] += col_sum(dv)


def call(kernel, outs, scratch, flops, *args):
    sds = [jax.ShapeDtypeStruct(shape, dtype) for shape, dtype in outs]
    moved = sum(a.size * a.dtype.itemsize for a in args)
    return pl.pallas_call(
        kernel,
        out_shape=sds,
        scratch_shapes=[pltpu.VMEM(shape, dtype) for shape, dtype in scratch],
        compiler_params=pltpu.CompilerParams(vmem_limit_bytes=VMEM_BYTES),
        cost_estimate=pl.CostEstimate(flops=flops, bytes_accessed=moved, transcendentals=0),
    )(*args)


TOK = (LEN, D)
STAT = (LEN, LANES)
unit = 2 * LEN * D * D


def self_forward(x, w, vec, qa, ka):
    outs = [(TOK, BF)] * 4 + [(STAT, BF), (TOK, F32), (STAT, F32)]
    return call(self_forward_kernel, outs, [], 20 * unit, x, w, vec, qa, ka)


def cross_forward(n1, m, w, vec, qa, ka):
    outs = [(TOK, BF)] * 4 + [(STAT, BF), (TOK, F32), (STAT, F32)]
    return call(cross_forward_kernel, outs, [], 25 * unit, n1, m, w, vec, qa, ka)


def ffn(n2, r2, cot, w1, w2, vec):
    outs = [(TOK, BF), ((8, 4, 64, D), BF), ((FF, D), BF), (TOK, F32), ((32, D), F32)]
    scratch = [((LEN, FF), BF), ((LEN, FF), BF), (TOK, BF), (TOK, BF), ((ROWS, FF), F32)]
    return call(ffn_kernel, outs, scratch, 26 * unit, n2, r2, cot, w1, w2, vec)


ATT_SCRATCH = [(TOK, BF), (TOK, BF), (STAT, BF), (TOK, BF), (TOK, BF), (TOK, BF), ((2, LEN, LEN), BF), ((2, LEN, LEN), BF)]


def cross_backward(*args):
    outs = [((4, D, D), BF), (TOK, BF), (TOK, F32), ((32, D), F32)]
    return call(cross_backward_kernel, outs, ATT_SCRATCH + [(TOK, BF)], 50 * unit, *args)


def self_backward(*args):
    outs = [((4, D, D), BF), (TOK, BF), ((32, D), F32)]
    return call(self_backward_kernel, outs, ATT_SCRATCH, 40 * unit, *args)


SQUARES = 8 * D * D
FULL_ROWS = 8192
VEC_ROWS = 17
VEC_LEN = VEC_ROWS * D


def groups_xy():
    return [[z * 8 + c * 2 + core for c in range(4)] for z in range(4) for core in range(2)]


def groups_z():
    return [[z * 8 + p for z in range(4)] for p in range(8)]


def swap(x, bit):
    return lax.ppermute(x, "dp", [(i, i ^ bit) for i in range(32)])


def turn_w1(chunk, here, out_first):
    if out_first:
        alt = chunk.reshape(64, 4, D).transpose(1, 0, 2).reshape(ROWS, D)
    else:
        alt = chunk.reshape(4, 64, D).transpose(1, 0, 2).reshape(ROWS, D)
    return jnp.where(here, alt, chunk)


def gather_blocks(params, index):
    low = params.astype(BF)
    share = low.shape[0]
    shift = share - ROWS * D
    prev = lax.ppermute(low[share - VEC_LEN :], "dp", [(i, (i + 1) % 32) for i in range(32)])
    flat = lax.dynamic_slice(jnp.concatenate([prev, low]), (VEC_LEN - shift * index,), (ROWS * D,))
    chunk = turn_w1(flat.reshape(ROWS, D), index // 8 == 2, True)
    vec = jnp.pad(prev.reshape(VEC_ROWS, D), ((0, 15), (0, 0)))
    both = lax.all_gather(jnp.concatenate([chunk, vec]), "dp", axis=0)
    main = both[:, :ROWS]
    return (
        main[:8].reshape(4, D, D),
        main[8:16].reshape(4, D, D),
        main[16:24].reshape(8, 4, 64, D),
        main[24:].reshape(FF, D),
        both[0, ROWS:].astype(F32),
    )


def gather_plain(params):
    flat = lax.all_gather(params.astype(BF), "dp", axis=0, tiled=True)
    mats = flat[:SQUARES].reshape(8, D, D)
    w1 = flat[SQUARES : SQUARES + D * FF].reshape(8, 64, 4, D).transpose(0, 2, 1, 3)
    w2 = flat[SQUARES + D * FF : SQUARES + 2 * D * FF].reshape(FF, D)
    vec = flat[SQUARES + 2 * D * FF :].reshape(VEC_ROWS, D).astype(F32)
    return mats[:4], mats[4:], w1, w2, jnp.pad(vec, ((0, 15), (0, 0)))


def plane_sum(grads, core):
    other = lax.dynamic_index_in_dim(grads, 1 - core, 1, keepdims=False)
    mine = lax.dynamic_index_in_dim(grads, core, 1, keepdims=False)
    pair = (mine.astype(F32) + swap(other, 1).astype(F32)).astype(BF)
    parts = lax.all_to_all(pair, "dp", 0, 0, tiled=True, axis_index_groups=groups_xy())
    return jnp.sum(parts.astype(F32), axis=0)


def share_blocks(dws, dwc, dw1, dw2, vec, index):
    core = index % 2
    ffn_part = plane_sum(
        jnp.concatenate([dw1.reshape(4, 2, ROWS, D), dw2.reshape(4, 2, ROWS, D)], axis=2), core
    )
    cross_part = plane_sum(dwc.reshape(4, 2, ROWS, D), core)
    self_part = plane_sum(dws.reshape(4, 2, ROWS, D), core)
    stack = jnp.stack([self_part, cross_part, ffn_part[:ROWS], ffn_part[ROWS:]]).astype(BF)
    chunk = jnp.sum(
        lax.all_to_all(stack, "dp", 0, 0, tiled=True, axis_index_groups=groups_z()).astype(F32), axis=0
    )
    for bit in (1, 2, 4, 8, 16):
        vec = vec + swap(vec, bit)
    total = jnp.full((8, LANES), jnp.sum(chunk * chunk))
    for bit in (1, 2, 4, 8, 16):
        total = total + swap(total, bit)
    vec = vec[:VEC_ROWS].reshape(VEC_LEN)
    square = total[0, 0] + jnp.sum(vec * vec)
    chunk = turn_w1(chunk, index // 8 == 2, False)
    flat = chunk.reshape(ROWS * D)
    after = lax.ppermute(flat[:VEC_LEN], "dp", [(i + 1, i) for i in range(31)])
    after = jnp.where(index == 31, vec, after)
    share = lax.dynamic_slice(jnp.concatenate([flat, after]), (272 * index,), (ROWS * D + 272,))
    return share, vec, square


def share_plain(dws, dwc, dw1, dw2, vec, index, share_len):
    flat = jnp.concatenate(
        [
            dws.reshape(-1),
            dwc.reshape(-1),
            dw1.transpose(0, 2, 1, 3).reshape(-1),
            dw2.reshape(-1),
        ]
    ).astype(F32)
    flat = lax.psum(jnp.concatenate([flat, vec[:VEC_ROWS].reshape(-1)]), "dp")
    share = lax.dynamic_slice(flat, (index * share_len,), (share_len,))
    return share, flat[-VEC_LEN:], jnp.sum(flat * flat)


def shards(count, targets, memory, target_ids, memory_ids, cotangent, params, first_moment, second_moment):
    index = lax.axis_index("dp")
    blocked = count == 32
    ws, wc, w1, w2, vec = gather_blocks(params, index) if blocked else gather_plain(params)
    lane = jnp.arange(LANES)[None, :] - MASK_LANE
    live = (lane >= 0) & (lane < 8)
    same_t = lane == target_ids[:, None]
    same_m = lane == memory_ids[:, None]
    qa = jnp.where(live & ~same_t, masked_value, 0.0).astype(BF)
    ka_self = jnp.where(same_t, 1.0, 0.0).astype(BF)
    ka_cross = jnp.where(same_m, 1.0, 0.0).astype(BF)
    qs, ks, vs, os, qal_s, n1, r1 = self_forward(targets, ws, vec, qa, ka_self)
    qc, kc, vc, oc, qal_c, n2, r2 = cross_forward(n1, memory, wc, vec, qa, ka_cross)
    out, dw1, dw2, dr2, vg_f = ffn(n2, r2, cotangent, w1, w2, vec)
    dwc, memory_grad, dr1, vg_c = cross_backward(
        dr2, wc, vec, qc, kc, vc, oc, qal_c, ka_cross, n1, r1, memory.T
    )
    dws, input_grad, vg_s = self_backward(dr1, ws, qs, ks, vs, os, qal_s, ka_self, targets.T)
    vec_grad = vg_f + vg_c + vg_s
    if blocked:
        grad, vec_total, square = share_blocks(dws, dwc, dw1, dw2, vec_grad, index)
    else:
        grad, vec_total, square = share_plain(dws, dwc, dw1, dw2, vec_grad, index, params.shape[0])
    norm_value = jnp.sqrt(square)
    factor = jnp.minimum(1.0, clip_limit / (norm_value + 1e-06))
    clipped = grad * factor
    new_first = beta_one * first_moment + (1.0 - beta_one) * clipped
    new_second = beta_two * second_moment + (1.0 - beta_two) * clipped * clipped
    first_hat = new_first / (1.0 - beta_one**STEP)
    second_hat = new_second / (1.0 - beta_two**STEP)
    new_params = params - step_rate * (
        first_hat / (jnp.sqrt(second_hat) + adam_eps) + weight_decay * params
    )
    return (
        out,
        input_grad,
        memory_grad,
        norm_value,
        grad,
        vec_total,
        new_params,
        new_first,
        new_second,
        new_params.astype(BF),
    )


def solution(mesh):
    rows, flat = P("dp", None), P("dp")
    return jax.shard_map(
        functools.partial(shards, mesh.shape["dp"]),
        mesh=mesh,
        in_specs=(rows, rows, flat, flat, rows, flat, flat, flat),
        out_specs=(rows, rows, rows, P(), flat, P(), flat, flat, flat, flat),
        check_vma=False,
    )
```

```python
import functools
import jax
import jax.numpy as jnp
from jax import lax
from jax.experimental import pallas as pl
from jax.experimental.pallas import tpu as pltpu
from jax.sharding import PartitionSpec as P

D = 512
FF = 2048
HEADS = 8
LEN = 1024
STEP = 10
ROWS = 256
BLOCKS = LEN // ROWS
LANES = 128
PAIRS = D // LANES
MASK_LANE = 32
EARLY_PAIRS = 3

eps_norm = 1e-05
beta_one = 0.9
beta_two = 0.999
adam_eps = 1e-08
step_rate = 0.05
weight_decay = 0.01
clip_limit = 1.0
masked_value = -1e30
log2_e = 1.4426950408889634
query_scale = 0.125 * log2_e
key_scale = 1.0 / log2_e

BF = jnp.bfloat16
F32 = jnp.float32
VMEM_BYTES = 60 * 1024 * 1024


def nn(a, b):
    return jnp.dot(a, b, preferred_element_type=F32)


def nt(a, b):
    return lax.dot_general(a, b, (((1,), (1,)), ((), ())), preferred_element_type=F32)


def tn(a, b):
    return lax.dot_general(a, b, (((0,), (0,)), ((), ())), preferred_element_type=F32)


def layer_norm(resid):
    center = resid - jnp.mean(resid, axis=1, keepdims=True)
    inv_std = lax.rsqrt(jnp.mean(center * center, axis=1, keepdims=True) + eps_norm)
    return center * inv_std, inv_std


def norm_back(grad, normed, inv_std, gain):
    scaled = grad * gain
    return inv_std * (
        scaled
        - jnp.mean(scaled, axis=1, keepdims=True)
        - normed * jnp.mean(scaled * normed, axis=1, keepdims=True)
    )


def half_row(parity):
    lane = lax.broadcasted_iota(jnp.int32, (1, LANES), 1)
    inside = (lane // 64) == parity
    return jnp.where(inside, 1.0, 0.0).astype(BF)


def lane_row(first, count):
    lane = lax.broadcasted_iota(jnp.int32, (1, LANES), 1)
    inside = (lane >= first) & (lane < first + count)
    return jnp.where(inside, 1.0, 0.0).astype(BF)


def causal_bias(transposed):
    row = lax.broadcasted_iota(jnp.int32, (ROWS, ROWS), 0)
    col = lax.broadcasted_iota(jnp.int32, (ROWS, ROWS), 1)
    ok = (row <= col) if transposed else (col <= row)
    return jnp.where(ok, 0.0, masked_value)


def attend_forward(q_ref, k_ref, v_ref, qa_ref, ka_ref, o_ref, qal_ref, causal):
    lane = lax.broadcasted_iota(jnp.int32, (ROWS, LANES), 1)
    low = lane < 64
    bias = causal_bias(False) if causal else None
    for qb in range(BLOCKS):
        rows = pl.ds(qb * ROWS, ROWS)
        keys = (qb + 1) * ROWS if causal else LEN
        qa = qa_ref[rows, :]

        def one_pair(pair, lse_parts):
            lanes = pl.ds(pl.multiple_of(pair * LANES, LANES), LANES)
            q_pair = q_ref[rows, lanes]
            k_cat = jnp.concatenate([k_ref[:keys, lanes], ka_ref[:keys, :]], axis=1)
            v_pair = v_ref[:keys, lanes]
            outs = []
            for parity in range(2):
                half = half_row(parity)
                head = pair * 2 + parity
                q_cat = jnp.concatenate([q_pair * half, qa], axis=1)
                scores = nt(q_cat, k_cat)
                if causal:
                    diag = scores[:, keys - ROWS :] + bias
                    scores = (
                        jnp.concatenate([scores[:, : keys - ROWS], diag], axis=1) if qb else diag
                    )
                top = jnp.max(scores, axis=1, keepdims=True)
                probs = jnp.exp2(scores - top).astype(BF)
                mixed = nn(probs, v_pair * half + (1.0 - half).astype(BF))
                turned = pltpu.roll(mixed, 64, 1)
                outs.append(mixed / turned)
                total = turned if parity == 0 else mixed
                lse = -(top + jnp.log2(total))
                first = lse.astype(BF).astype(F32)
                rest = lse - first
                second = rest.astype(BF).astype(F32)
                base = head * 3
                lse_parts = jnp.where(lane == base, first, lse_parts)
                lse_parts = jnp.where(lane == base + 1, second, lse_parts)
                lse_parts = jnp.where(lane == base + 2, rest - second, lse_parts)
            o_ref[rows, lanes] = jnp.where(low, outs[0], outs[1]).astype(BF)
            return lse_parts

        lse_parts = lax.fori_loop(0, PAIRS, one_pair, jnp.zeros((ROWS, LANES), F32))
        qal_ref[rows, :] = (qa.astype(F32) + lse_parts).astype(BF)


def attend_backward(
    q_ref, k_ref, v_ref, do_ref, qal_ref, del_ref, ka_ref, dq_ref, dk_ref, dv_ref, p_ref, s_ref, causal,
    span=(0, PAIRS),
):
    bias = causal_bias(True) if causal else None

    def one_pair(pair, carry):
        lanes = pl.ds(pl.multiple_of(pair * LANES, LANES), LANES)
        k_pair = k_ref[:, lanes]
        k_turn = k_pair.T
        v_pair = v_ref[:, lanes]
        dq_parts = [[], []]
        for parity in range(2):
            head = pair * 2 + parity
            half = half_row(parity)
            k_cat = jnp.concatenate([k_pair * half, ka_ref[...] + lane_row(head * 3, 3)], axis=1)
            ones = jnp.broadcast_to(lane_row(head * 2, 2), (LEN, LANES))
            v_cat = jnp.concatenate([v_pair * half, ones], axis=1)
            for qb in range(BLOCKS):
                rows = pl.ds(qb * ROWS, ROWS)
                keys = (qb + 1) * ROWS if causal else LEN
                q_cat = jnp.concatenate([q_ref[rows, lanes], qal_ref[rows, :]], axis=1)
                do_cat = jnp.concatenate([do_ref[rows, lanes], del_ref[rows, :]], axis=1)
                scores = nt(k_cat[:keys], q_cat)
                if causal:
                    diag = scores[keys - ROWS :] + bias
                    scores = jnp.concatenate([scores[: keys - ROWS], diag], axis=0) if qb else diag
                probs = jnp.exp2(scores)
                p_ref[parity, :keys, rows] = probs.astype(BF)
                grads = (probs * nt(v_cat[:keys], do_cat)).astype(BF)
                s_ref[parity, :keys, rows] = grads
                dq_parts[parity].append(
                    nn(k_turn[parity * 64 : parity * 64 + 64, :keys], grads)
                )
        for qb in range(BLOCKS):
            rows = pl.ds(qb * ROWS, ROWS)
            dq = jnp.concatenate([dq_parts[0][qb], dq_parts[1][qb]], axis=0) * 0.125
            dq_ref[rows, lanes] = dq.T.astype(BF)
        for kb in range(BLOCKS):
            rows = pl.ds(kb * ROWS, ROWS)
            first = kb * ROWS if causal else 0
            tail = pl.ds(first, LEN - first)
            do_pair = do_ref[tail, lanes]
            q_pair = q_ref[tail, lanes]
            dv = nn(p_ref[0, rows, tail], do_pair * half_row(0))
            dv = dv + nn(p_ref[1, rows, tail], do_pair * half_row(1))
            dv_ref[rows, lanes] = dv.astype(BF)
            dk = nn(s_ref[0, rows, tail], q_pair * half_row(0))
            dk = dk + nn(s_ref[1, rows, tail], q_pair * half_row(1))
            dk_ref[rows, lanes] = (dk * key_scale).astype(BF)
        return carry

    lax.fori_loop(span[0], span[1], one_pair, 0)


def mix_gradient(g_ref, w_out, o_ref, do_ref, del_ref):
    lane = lax.broadcasted_iota(jnp.int32, (ROWS, LANES), 1)
    even = lane % 2 == 0
    col = lax.broadcasted_iota(jnp.int32, (D, LANES), 0) // 64
    pick = jnp.where(lax.broadcasted_iota(jnp.int32, (D, LANES), 1) // 2 == col, -1.0, 0.0).astype(BF)
    for qb in range(BLOCKS):
        rows = pl.ds(qb * ROWS, ROWS)
        do = nt(g_ref[rows, :], w_out).astype(BF)
        do_ref[rows, :] = do
        prod = do.astype(F32) * o_ref[rows, :].astype(F32)
        high = prod.astype(BF)
        inner = nn(high, pick) + nn((prod - high.astype(F32)).astype(BF), pick)
        first = inner.astype(BF).astype(F32)
        del_ref[rows, :] = jnp.where(even, first, inner - first).astype(BF)


def vec_row(vec_ref, index):
    return vec_ref[index : index + 1, :]


def fetch(all_ref, block, w_ref, sem):
    copy = pltpu.make_async_copy(all_ref.at[pl.ds(8 * block, 8)], w_ref, sem)
    copy.start()
    return copy


def square(w_ref, matrix):
    return w_ref[2 * matrix : 2 * matrix + 2].reshape(D, D)


def put_square(mine_ref, other_ref, core, matrix, turned_ref, grad):
    for ref, half in ((mine_ref, core), (other_ref, 1 - core)):
        rows = turned_ref[pl.ds(pl.multiple_of(half * ROWS, ROWS), ROWS), :]
        ref[matrix, :ROWS, :] = nn(rows, grad).astype(BF)


def put_square_tn(mine_ref, other_ref, core, matrix, left_ref, grad):
    for ref, half in ((mine_ref, core), (other_ref, 1 - core)):
        cols = left_ref[:, pl.ds(pl.multiple_of(half * ROWS, ROWS), ROWS)]
        ref[matrix, :ROWS, :] = tn(cols, grad).astype(BF)


def self_forward_kernel(
    core_ref, own_ref, other_ref, x_ref, vec_ref, qa_ref, ka_ref,
    q_ref, k_ref, v_ref, o_ref, qal_ref, n_ref, r_ref,
    w_ref, sems,
):
    core, place_xy = core_ref[0], core_ref[1]
    copies = []
    for matrix in range(4):
        for half, source in enumerate((own_ref, other_ref)):
            place = 2 * matrix + (core if half == 0 else 1 - core)
            copies.append(
                pltpu.make_async_copy(
                    source.at[matrix ^ place_xy, pl.ds(0, ROWS)], w_ref.at[place], sems.at[2 * matrix + half]
                )
            )
    for copy in copies:
        copy.start()
    for copy in copies[:6]:
        copy.wait()
    for qb in range(BLOCKS):
        rows = pl.ds(qb * ROWS, ROWS)
        x = x_ref[rows, :]
        q_ref[rows, :] = ((nn(x, square(w_ref, 0)) + vec_row(vec_ref, 6)) * query_scale).astype(BF)
        k_ref[rows, :] = nn(x, square(w_ref, 1)).astype(BF)
        v_ref[rows, :] = (nn(x, square(w_ref, 2)) + vec_row(vec_ref, 7)).astype(BF)
    attend_forward(q_ref, k_ref, v_ref, qa_ref, ka_ref, o_ref, qal_ref, True)
    for copy in copies[6:]:
        copy.wait()
    for qb in range(BLOCKS):
        rows = pl.ds(qb * ROWS, ROWS)
        resid = x_ref[rows, :].astype(F32) + nn(o_ref[rows, :], square(w_ref, 3)) + vec_row(vec_ref, 8)
        normed, inv_std = layer_norm(resid)
        n_ref[rows, :] = normed
        r_ref[rows, :] = jnp.broadcast_to(inv_std, (ROWS, LANES))


def cross_forward_kernel(
    all_ref, n1_ref, m_ref, vec_ref, qa_ref, ka_ref,
    q_ref, k_ref, v_ref, o_ref, qal_ref, n_ref, r_ref,
    w_ref, sem,
):
    fetch(all_ref, 1, w_ref, sem).wait()
    for qb in range(BLOCKS):
        rows = pl.ds(qb * ROWS, ROWS)
        h = (n1_ref[rows, :] * vec_row(vec_ref, 0) + vec_row(vec_ref, 1)).astype(BF)
        m = m_ref[rows, :]
        q_ref[rows, :] = ((nn(h, square(w_ref, 0)) + vec_row(vec_ref, 9)) * query_scale).astype(BF)
        k_ref[rows, :] = nn(m, square(w_ref, 1)).astype(BF)
        v_ref[rows, :] = (nn(m, square(w_ref, 2)) + vec_row(vec_ref, 10)).astype(BF)
    attend_forward(q_ref, k_ref, v_ref, qa_ref, ka_ref, o_ref, qal_ref, False)
    for qb in range(BLOCKS):
        rows = pl.ds(qb * ROWS, ROWS)
        h = n1_ref[rows, :] * vec_row(vec_ref, 0) + vec_row(vec_ref, 1)
        resid = h + nn(o_ref[rows, :], square(w_ref, 3)) + vec_row(vec_ref, 11)
        normed, inv_std = layer_norm(resid)
        n_ref[rows, :] = normed
        r_ref[rows, :] = jnp.broadcast_to(inv_std, (ROWS, LANES))


def col_sum(x):
    return jnp.sum(x.astype(F32), axis=0, keepdims=True)


def ffn_kernel(
    core_ref, all_ref, n2_ref, r2_ref, cot_ref, vec_ref,
    out_ref, mine_ref, other_ref, dr_ref, vg_ref,
    w1_ref, w2_ref, u_ref, da_ref, h_ref, dz_ref, f_ref, ht_ref, sem1, sem2,
):
    copy1 = fetch(all_ref, 2, w1_ref, sem1)
    copy2 = fetch(all_ref, 3, w2_ref, sem2)
    copy1.wait()
    copy2.wait()

    def w1_block(j):
        return w1_ref[:, 64 * j : 64 * j + 64].reshape(D, D)

    def w2_block(j):
        return square(w2_ref, j)

    vg_ref[...] = jnp.zeros_like(vg_ref)

    def one_tile(tile, carry):
        rows = pl.ds(pl.multiple_of(tile * ROWS, ROWS), ROWS)
        n2 = n2_ref[rows, :]
        h2 = n2 * vec_row(vec_ref, 2) + vec_row(vec_ref, 3)
        h2_low = h2.astype(BF)
        h_ref[rows, :] = h2_low
        resid = h2 + vec_row(vec_ref, 16)
        for j in range(4):
            a = nn(h2_low, w1_block(j)) + vec_row(vec_ref, 12 + j)
            s = 0.5 * jnp.tanh(0.5 * a) + 0.5
            u = (a * s).astype(BF)
            u_ref[rows, j * D : (j + 1) * D] = u
            f_ref[:, j * D : (j + 1) * D] = s * (1.0 + a * (1.0 - s))
            resid = resid + nn(u, w2_block(j))
        n3, inv3 = layer_norm(resid)
        gain3 = vec_row(vec_ref, 4)
        out_ref[rows, :] = (n3 * gain3 + vec_row(vec_ref, 5)).astype(BF)
        cot = cot_ref[rows, :].astype(F32)
        dr3 = norm_back(cot, n3, inv3, gain3)
        dz = dr3.astype(BF)
        dz_ref[rows, :] = dz
        vg_ref[4:5, :] += col_sum(cot * n3)
        vg_ref[5:6, :] += col_sum(cot)
        vg_ref[16:17, :] += col_sum(dz)
        dh = dr3
        for j in range(4):
            da = (nt(dz, w2_block(j)) * f_ref[:, j * D : (j + 1) * D]).astype(BF)
            da_ref[rows, j * D : (j + 1) * D] = da
            vg_ref[12 + j : 13 + j, :] += col_sum(da)
            dh = dh + nt(da, w1_block(j))
        vg_ref[2:3, :] += col_sum(dh * n2)
        vg_ref[3:4, :] += col_sum(dh)
        dr2 = norm_back(dh, n2, r2_ref[rows, 0:1], vec_row(vec_ref, 2))
        dr_ref[rows, :] = dr2
        vg_ref[11:12, :] += col_sum(dr2.astype(BF))
        return carry

    lax.fori_loop(0, BLOCKS, one_tile, 0)
    core = core_ref[0]
    ht_ref[...] = jnp.swapaxes(h_ref[...].T.reshape(4, 2, 64, LEN), 0, 1).reshape(2, ROWS, LEN)
    for j in range(4):
        da = da_ref[:, j * D : (j + 1) * D]
        dz = dz_ref[...]
        for ref, half in ((mine_ref, core), (other_ref, 1 - core)):
            dw1 = nn(ht_ref[half], da).astype(BF)
            ref[:, 64 * j : 64 * j + 64, :] = dw1.reshape(4, 64, D)
            cols = pl.ds(pl.multiple_of(j * D + half * ROWS, ROWS), ROWS)
            ref[j, ROWS:, :] = tn(u_ref[:, cols], dz).astype(BF)


def cross_backward_kernel(
    core_ref, all_ref, dr2_ref, vec_ref, q_ref, k_ref, v_ref, o_ref, qal_ref, ka_ref, n1_ref, r1_ref, mt_ref, vf_ref,
    mine_ref, other_ref, mg_ref, dr1_ref,
    g_ref, do_ref, del_ref, dq_ref, dk_ref, dv_ref, p_ref, s_ref, h_ref, w_ref, vg_ref, sem,
):
    core = core_ref[0]
    copy = fetch(all_ref, 1, w_ref, sem)
    for qb in range(BLOCKS):
        rows = pl.ds(qb * ROWS, ROWS)
        g_ref[rows, :] = dr2_ref[rows, :].astype(BF)
        h_ref[rows, :] = (n1_ref[rows, :] * vec_row(vec_ref, 0) + vec_row(vec_ref, 1)).astype(BF)
    copy.wait()
    mix_gradient(g_ref, square(w_ref, 3), o_ref, do_ref, del_ref)
    put_square_tn(mine_ref, other_ref, core, 3, o_ref, g_ref[...])
    attend_backward(
        q_ref, k_ref, v_ref, do_ref, qal_ref, del_ref, ka_ref, dq_ref, dk_ref, dv_ref, p_ref, s_ref, False
    )
    put_square_tn(mine_ref, other_ref, core, 0, h_ref, dq_ref[...])
    put_square(mine_ref, other_ref, core, 1, mt_ref, dk_ref[...])
    put_square(mine_ref, other_ref, core, 2, mt_ref, dv_ref[...])
    vg_ref[...] = vf_ref[...]
    for qb in range(BLOCKS):
        rows = pl.ds(qb * ROWS, ROWS)
        dq = dq_ref[rows, :]
        dk = dk_ref[rows, :]
        dv = dv_ref[rows, :]
        mg_ref[rows, :] = (nt(dk, square(w_ref, 1)) + nt(dv, square(w_ref, 2))).astype(BF)
        vg_ref[9:10, :] += col_sum(dq)
        vg_ref[10:11, :] += col_sum(dv)
        dh = dr2_ref[rows, :] + nt(dq, square(w_ref, 0))
        n1 = n1_ref[rows, :]
        vg_ref[0:1, :] += col_sum(dh * n1)
        vg_ref[1:2, :] += col_sum(dh)
        dr1 = norm_back(dh, n1, r1_ref[rows, 0:1], vec_row(vec_ref, 0))
        dr1_ref[rows, :] = dr1
        vg_ref[8:9, :] += col_sum(dr1.astype(BF))
    blank = jnp.zeros((12, D), F32)
    for ref, half in ((mine_ref, core), (other_ref, 1 - core)):
        for xy in range(4):
            low, high = vg_ref[8 * xy : 8 * xy + 4, :], vg_ref[8 * xy + 4 : 8 * xy + 8, :]
            rows = jnp.where(half == 0, low, high)
            ref[xy, ROWS:, :] = jnp.concatenate([rows, blank], axis=0).astype(BF)


def self_backward_start_kernel(
    all_ref, dr1_ref, q_ref, k_ref, v_ref, o_ref, qal_ref, ka_ref,
    do_ref, del_ref, dq_ref, dk_ref, dv_ref,
    g_ref, p_ref, s_ref, w_ref, sem,
):
    copy = fetch(all_ref, 0, w_ref, sem)
    for qb in range(BLOCKS):
        rows = pl.ds(qb * ROWS, ROWS)
        g_ref[rows, :] = dr1_ref[rows, :].astype(BF)
    copy.wait()
    mix_gradient(g_ref, square(w_ref, 3), o_ref, do_ref, del_ref)
    attend_backward(
        q_ref, k_ref, v_ref, do_ref, qal_ref, del_ref, ka_ref, dq_ref, dk_ref, dv_ref, p_ref, s_ref, True,
        (0, EARLY_PAIRS),
    )


def self_backward_end_kernel(
    core_ref, all_ref, dr1_ref, q_ref, k_ref, v_ref, o_ref, qal_ref, ka_ref, xt_ref,
    do_ref, del_ref, dqe_ref, dke_ref, dve_ref,
    mine_ref, other_ref, ig_ref,
    g_ref, dq_ref, dk_ref, dv_ref, p_ref, s_ref, w_ref, late_ref, sem,
):
    core = core_ref[0]
    copy = fetch(all_ref, 0, w_ref, sem)
    for qb in range(BLOCKS):
        rows = pl.ds(qb * ROWS, ROWS)
        g_ref[rows, :] = dr1_ref[rows, :].astype(BF)
    early = EARLY_PAIRS * LANES
    for ref, source in ((dq_ref, dqe_ref), (dk_ref, dke_ref), (dv_ref, dve_ref)):
        ref[:, :early] = source[:, :early]
    attend_backward(
        q_ref, k_ref, v_ref, do_ref, qal_ref, del_ref, ka_ref, dq_ref, dk_ref, dv_ref, p_ref, s_ref, True,
        (EARLY_PAIRS, PAIRS),
    )
    copy.wait()
    put_square_tn(mine_ref, other_ref, core, 3, o_ref, g_ref[...])
    put_square(mine_ref, other_ref, core, 0, xt_ref, dq_ref[...])
    put_square(mine_ref, other_ref, core, 1, xt_ref, dk_ref[...])
    put_square(mine_ref, other_ref, core, 2, xt_ref, dv_ref[...])
    late_ref[...] = jnp.zeros_like(late_ref)
    for qb in range(BLOCKS):
        rows = pl.ds(qb * ROWS, ROWS)
        dq = dq_ref[rows, :]
        dk = dk_ref[rows, :]
        dv = dv_ref[rows, :]
        ig_ref[rows, :] = (
            dr1_ref[rows, :]
            + nt(dq, square(w_ref, 0))
            + nt(dk, square(w_ref, 1))
            + nt(dv, square(w_ref, 2))
        ).astype(BF)
        late_ref[0:1, :] += col_sum(dq)
        late_ref[1:2, :] += col_sum(dv)
    for ref, half in ((mine_ref, core), (other_ref, 1 - core)):
        for xy in range(4):
            place = pl.multiple_of((2 * (xy % 2) + half) * LANES, LANES)
            piece = late_ref[xy // 2 : xy // 2 + 1, pl.ds(place, LANES)]
            ref[xy, ROWS:, :] = jnp.zeros((16, D), BF)
            ref[xy, ROWS:, :LANES] = jnp.broadcast_to(piece, (16, LANES)).astype(BF)


def call(kernel, outs, scratch, flops, args, remote=(), sems=1):
    sds = [jax.ShapeDtypeStruct(shape, dtype) for shape, dtype in outs]
    moved = sum(a.size * a.dtype.itemsize for a in args)
    spaces = {"a": pl.ANY, "s": pltpu.SMEM, "v": pltpu.VMEM}
    kinds = dict(remote)
    memory = [pltpu.VMEM(shape, dtype) for shape, dtype in scratch]
    memory += [pltpu.SemaphoreType.DMA] * sems if sems < 8 else [pltpu.SemaphoreType.DMA((sems,))]
    return pl.pallas_call(
        kernel,
        out_shape=sds,
        in_specs=[
            pl.BlockSpec(memory_space=spaces[kinds.get(i, "v")]) for i in range(len(args))
        ],
        scratch_shapes=memory,
        compiler_params=pltpu.CompilerParams(vmem_limit_bytes=VMEM_BYTES),
        cost_estimate=pl.CostEstimate(flops=flops, bytes_accessed=moved, transcendentals=0),
    )(*args)


TOK = (LEN, D)
STAT = (LEN, LANES)
OCT = (8, ROWS, D)
unit = 2 * LEN * D * D
FORWARD_OUTS = [(TOK, BF)] * 4 + [(STAT, BF), (TOK, F32), (STAT, F32)]
HALVES = ((4, ROWS + 16, D), BF)
TOKB = (TOK, BF)
PROBS = ((2, LEN, LEN), BF)


def self_forward(*args):
    kinds = ((0, "s"), (1, "a"), (2, "a"))
    return call(self_forward_kernel, FORWARD_OUTS, [(OCT, BF)], 20 * unit, args, kinds, 8)


def cross_forward(*args):
    return call(cross_forward_kernel, FORWARD_OUTS, [(OCT, BF)], 25 * unit, args, ((0, "a"),))


KINDS = ((0, "s"), (1, "a"))


def ffn(*args):
    outs = [TOKB, ((4, 2 * ROWS, D), BF), ((4, 2 * ROWS, D), BF), (TOK, F32), ((32, D), F32)]
    scratch = [(OCT, BF), (OCT, BF), ((LEN, FF), BF), ((LEN, FF), BF), TOKB, TOKB]
    scratch += [((ROWS, FF), F32), ((2, ROWS, LEN), BF)]
    return call(ffn_kernel, outs, scratch, 26 * unit, args, KINDS, 2)


def cross_backward(*args):
    outs = [HALVES, HALVES, TOKB, (TOK, F32)]
    scratch = [TOKB, TOKB, (STAT, BF), TOKB, TOKB, TOKB, PROBS, PROBS, TOKB, (OCT, BF), ((32, D), F32)]
    return call(cross_backward_kernel, outs, scratch, 50 * unit, args, KINDS)


def self_backward_start(*args):
    outs = [TOKB, (STAT, BF), TOKB, TOKB, TOKB]
    scratch = [TOKB, PROBS, PROBS, (OCT, BF)]
    return call(self_backward_start_kernel, outs, scratch, 25 * unit, args, ((0, "a"),))


def self_backward_end(*args):
    outs = [HALVES, HALVES, TOKB]
    scratch = [TOKB, TOKB, TOKB, TOKB, PROBS, PROBS, (OCT, BF), ((8, D), F32)]
    return call(self_backward_end_kernel, outs, scratch, 2 * unit, args, KINDS)


SQUARES = 8 * D * D
VEC_ROWS = 17
VEC_LEN = VEC_ROWS * D


def groups_xy():
    return [[z * 8 + c * 2 + core for c in range(4)] for z in range(4) for core in range(2)]


def groups_z():
    return [[z * 8 + p for z in range(4)] for p in range(8)]


def swap(x, bit):
    return lax.ppermute(x, "dp", [(i, i ^ bit) for i in range(32)])


def turn_w1(chunk, here, out_first):
    if out_first:
        alt = chunk.reshape(64, 4, D).transpose(1, 0, 2).reshape(ROWS, D)
    else:
        alt = chunk.reshape(4, 64, D).transpose(1, 0, 2).reshape(ROWS, D)
    return jnp.where(here, alt, chunk)


def gather_first(buf, index):
    z = index // 8
    far = lax.ppermute(buf, "dp", [(p, 16 + p) for p in range(8)])
    held = jnp.where(z == 2, far, buf)
    near = lax.ppermute(held, "dp", [(z0 * 8 + p, z0 * 8 + 8 + p) for z0 in (0, 2) for p in range(8)])
    held = jnp.where(z % 2 == 1, near, held)
    side, up = swap(held, 2), swap(held, 4)
    half = held.shape[0] // 2
    corner = [swap(up[:half], 2), swap(side[half:], 4)]
    own = jnp.concatenate([held, side, up] + corner).reshape((4,) + held.shape)
    other = swap(own, 1)
    place = index % 8 // 2
    source = jnp.where(
        index % 2 == 0,
        lax.dynamic_index_in_dim(own, place, 0, keepdims=False)[ROWS:],
        lax.dynamic_index_in_dim(other, place, 0, keepdims=False)[ROWS:],
    )
    return own, other, source.astype(F32)


def gather_blocks(params, index):
    low = params.astype(BF)
    share = low.shape[0]
    shift = share - ROWS * D
    prev = lax.ppermute(low[share - VEC_LEN :], "dp", [(i, (i + 1) % 32) for i in range(32)])
    flat = lax.dynamic_slice(jnp.concatenate([prev, low]), (VEC_LEN - shift * index,), (ROWS * D,))
    chunk = turn_w1(flat.reshape(ROWS, D), index // 8 == 2, True)
    everything = lax.all_gather(chunk, "dp", axis=0)
    vec = jnp.pad(prev.reshape(VEC_ROWS, D), ((0, 15), (0, 0)))
    own, other, vec = gather_first(jnp.concatenate([chunk, vec]), index)
    return own, other, everything.reshape(32, ROWS, D), vec


def gather_plain(params, index):
    flat = lax.all_gather(params.astype(BF), "dp", axis=0, tiled=True)
    end = SQUARES + D * FF
    w1 = flat[SQUARES:end].reshape(8, 64, 4, D).transpose(0, 2, 1, 3).reshape(8, ROWS, D)
    mats = flat[:SQUARES].reshape(16, ROWS, D)
    w2 = flat[end : end + D * FF].reshape(8, ROWS, D)
    vec = flat[end + D * FF :].reshape(VEC_ROWS, D).astype(F32)
    pairs = mats[:8].reshape(4, 2, ROWS, D)
    own = lax.dynamic_index_in_dim(pairs, index % 2, 1, keepdims=False)
    other = lax.dynamic_index_in_dim(pairs, 1 - index % 2, 1, keepdims=False)
    return own, other, jnp.concatenate([mats, w1, w2]), jnp.pad(vec, ((0, 15), (0, 0)))


def plane_sum(mine, other):
    pair = (mine.astype(F32) + swap(other, 1).astype(F32)).astype(BF)
    parts = lax.all_to_all(pair, "dp", 0, 0, tiled=True, axis_index_groups=groups_xy())
    return jnp.sum(parts.astype(F32), axis=0).astype(BF)


def column_sum(part_c, part_f):
    rows = ROWS + 16
    blocks = jnp.stack([jnp.zeros((ROWS, D), BF), part_c[:ROWS], part_f[:ROWS], part_f[ROWS:]])
    extra = jnp.pad(part_c[ROWS : ROWS + 4].reshape(4, 1, D), ((0, 0), (0, 15), (0, 0)))
    stack = jnp.concatenate([blocks, extra], axis=1).reshape(4 * rows, D)
    return lax.psum_scatter(
        stack, "dp", scatter_dimension=0, tiled=True, axis_index_groups=groups_z()
    ).astype(F32)


def finish_blocks(mine, other, rest, index):
    z = index // 8
    part = plane_sum(mine, other)
    sent = [lax.ppermute(part, "dp", [(8 * k + p, p) for p in range(8)]) for k in (1, 2, 3)]
    own = part.astype(F32)
    for piece in sent:
        own = own + piece.astype(F32)
    chunk = jnp.where(z == 0, own[:ROWS], rest[:ROWS])
    flat = turn_w1(chunk, z == 2, False).reshape(ROWS * D)
    after = lax.ppermute(flat[:VEC_LEN], "dp", [(i + 1, i) for i in range(31)])
    pieces = jnp.concatenate(
        [
            rest[ROWS].reshape(4, LANES),
            own[ROWS : ROWS + 1, :LANES],
            jnp.full((3, LANES), jnp.sum(chunk * chunk)),
        ]
    )
    pieces = jnp.broadcast_to(pieces[None], (32, 8, LANES))
    pieces = lax.all_to_all(pieces, "dp", 0, 0, tiled=True)
    vec = pieces[:, :4].reshape(4, 8, D).transpose(1, 0, 2).reshape(32, D)
    late = jnp.pad(pieces[:8, 4].reshape(2, D), ((6, 9), (0, 0)))
    vec = (vec[:VEC_ROWS] + late).reshape(VEC_LEN)
    square = jnp.sum(pieces[:, 5, 0]) + jnp.sum(vec * vec)
    after = jnp.where(index == 31, vec, after)
    share = lax.dynamic_slice(jnp.concatenate([flat, after]), (272 * index,), (ROWS * D + 272,))
    return share, vec, square


def share_plain(pairs, index, share_len):
    def joined(mine, other):
        low = jnp.where(index % 2 == 0, mine, other).astype(F32)
        return jnp.stack([low, jnp.where(index % 2 == 0, other, mine).astype(F32)], axis=1)

    self_g, cross_g, ffn_g = (joined(*pair) for pair in pairs)
    dw1 = ffn_g[:, :, :ROWS].reshape(8, 4, 64, D).transpose(0, 2, 1, 3)
    vec = cross_g[:, :, ROWS : ROWS + 4].reshape(32, D)
    late = jnp.pad(self_g[:, :, ROWS, :LANES].reshape(2, D), ((6, 9), (0, 0)))
    vec = vec[:VEC_ROWS] + late
    parts = (self_g[:, :, :ROWS], cross_g[:, :, :ROWS], dw1, ffn_g[:, :, ROWS:], vec)
    flat = lax.psum(jnp.concatenate([g.reshape(-1) for g in parts]), "dp")
    share = lax.dynamic_slice(flat, (index * share_len,), (share_len,))
    return share, flat[-VEC_LEN:], jnp.sum(flat * flat)


def shards(count, targets, memory, target_ids, memory_ids, cotangent, params, first_moment, second_moment):
    index = lax.axis_index("dp")
    blocked = count == 32
    gather = gather_blocks if blocked else gather_plain
    own, other, weights, vec = gather(params, index)
    place = jnp.where(blocked, index % 8 // 2, 0)
    core = jnp.stack([index % 2, place]).astype(jnp.int32)
    lane = jnp.arange(LANES)[None, :] - MASK_LANE
    live = (lane >= 0) & (lane < 8)
    same_t = lane == target_ids[:, None]
    same_m = lane == memory_ids[:, None]
    qa = jnp.where(live & ~same_t, masked_value, 0.0).astype(BF)
    ka_self = jnp.where(same_t, 1.0, 0.0).astype(BF)
    ka_cross = jnp.where(same_m, 1.0, 0.0).astype(BF)
    memory_turn, targets_turn = memory.T, targets.T
    qa, ka_self, ka_cross, memory_turn, targets_turn, vec = lax.optimization_barrier(
        (qa, ka_self, ka_cross, memory_turn, targets_turn, vec)
    )
    qs, ks, vs, os, qal_s, n1, r1 = self_forward(
        core, own, other, targets, vec, qa, ka_self
    )
    qc, kc, vc, oc, qal_c, n2, r2 = cross_forward(
        weights, n1, memory, vec, qa, ka_cross
    )
    out, mine_f, other_f, dr2, vg_f = ffn(core, weights, n2, r2, cotangent, vec)
    mine_c, other_c, memory_grad, dr1 = cross_backward(
        core, weights, dr2, vec, qc, kc, vc, oc, qal_c, ka_cross, n1, r1, memory_turn, vg_f
    )
    if blocked:
        part_f = plane_sum(mine_f, other_f)
        part_f, mine_c, other_c, dr1 = lax.optimization_barrier((part_f, mine_c, other_c, dr1))
        part_c = plane_sum(mine_c, other_c)
    early = self_backward_start(weights, dr1, qs, ks, vs, os, qal_s, ka_self)
    if blocked:
        part_c, early = lax.optimization_barrier((part_c, early))
        rest = column_sum(part_c, part_f)
    mine_s, other_s, input_grad = self_backward_end(
        core, weights, dr1, qs, ks, vs, os, qal_s, ka_self, targets_turn, *early
    )
    if blocked:
        grad, vec_total, square = finish_blocks(mine_s, other_s, rest, index)
    else:
        pairs = ((mine_s, other_s), (mine_c, other_c), (mine_f, other_f))
        grad, vec_total, square = share_plain(pairs, index, params.shape[0])
    norm_value = jnp.sqrt(square)
    factor = jnp.minimum(1.0, clip_limit / (norm_value + 1e-06))
    clipped = grad * factor
    new_first = beta_one * first_moment + (1.0 - beta_one) * clipped
    new_second = beta_two * second_moment + (1.0 - beta_two) * clipped * clipped
    first_hat = new_first / (1.0 - beta_one**STEP)
    second_hat = new_second / (1.0 - beta_two**STEP)
    new_params = params - step_rate * (
        first_hat / (jnp.sqrt(second_hat) + adam_eps) + weight_decay * params
    )
    return (
        out,
        input_grad,
        memory_grad,
        norm_value,
        grad,
        vec_total,
        new_params,
        new_first,
        new_second,
        new_params.astype(BF),
    )


def solution(mesh):
    rows, flat = P("dp", None), P("dp")
    return jax.shard_map(
        functools.partial(shards, mesh.shape["dp"]),
        mesh=mesh,
        in_specs=(rows, rows, flat, flat, rows, flat, flat, flat),
        out_specs=(rows, rows, rows, P(), flat, P(), flat, flat, flat, flat),
        check_vma=False,
    )
```

```python
import functools
import jax
import jax.numpy as jnp
from jax import lax
from jax.experimental import pallas as pl
from jax.experimental.pallas import tpu as pltpu
from jax.sharding import PartitionSpec as P

D = 512
FF = 2048
HEADS = 8
LEN = 1024
STEP = 10
ROWS = 256
BLOCKS = LEN // ROWS
LANES = 128
PAIRS = D // LANES
MASK_LANE = 32
EARLY_PAIRS = 3
FIRST_ROWS = ROWS + 32

eps_norm = 1e-05
beta_one = 0.9
beta_two = 0.999
adam_eps = 1e-08
step_rate = 0.05
weight_decay = 0.01
clip_limit = 1.0
masked_value = -1e30
log2_e = 1.4426950408889634
query_scale = 0.125 * log2_e
key_scale = 1.0 / log2_e

BF = jnp.bfloat16
F32 = jnp.float32
VMEM_BYTES = 60 * 1024 * 1024


def nn(a, b):
    return jnp.dot(a, b, preferred_element_type=F32)


def nt(a, b):
    return lax.dot_general(a, b, (((1,), (1,)), ((), ())), preferred_element_type=F32)


def tn(a, b):
    return lax.dot_general(a, b, (((0,), (0,)), ((), ())), preferred_element_type=F32)


def layer_norm(resid):
    center = resid - jnp.mean(resid, axis=1, keepdims=True)
    inv_std = lax.rsqrt(jnp.mean(center * center, axis=1, keepdims=True) + eps_norm)
    return center * inv_std, inv_std


def norm_back(grad, normed, inv_std, gain):
    scaled = grad * gain
    return inv_std * (
        scaled
        - jnp.mean(scaled, axis=1, keepdims=True)
        - normed * jnp.mean(scaled * normed, axis=1, keepdims=True)
    )


def half_row(parity):
    lane = lax.broadcasted_iota(jnp.int32, (1, LANES), 1)
    inside = (lane // 64) == parity
    return jnp.where(inside, 1.0, 0.0).astype(BF)


def lane_row(first, count):
    lane = lax.broadcasted_iota(jnp.int32, (1, LANES), 1)
    inside = (lane >= first) & (lane < first + count)
    return jnp.where(inside, 1.0, 0.0).astype(BF)


def causal_bias(transposed):
    row = lax.broadcasted_iota(jnp.int32, (ROWS, ROWS), 0)
    col = lax.broadcasted_iota(jnp.int32, (ROWS, ROWS), 1)
    ok = (row <= col) if transposed else (col <= row)
    return jnp.where(ok, 0.0, masked_value)


def attend_forward(q_ref, k_ref, v_ref, qa_ref, ka_ref, o_ref, qal_ref, kt_ref, kat_ref, causal):
    size, depth = (ROWS, 2) if causal else (2 * ROWS, 1)
    lane = lax.broadcasted_iota(jnp.int32, (size, LANES), 1)
    low = lane < 64
    bias = causal_bias(False) if causal else None
    kt_ref[...] = k_ref[...].T
    kat_ref[...] = ka_ref[...].T

    def score(block, head):
        rows = pl.ds(block * size, size)
        lanes = pl.ds(head // 2 * LANES, LANES)
        keys = (block + 1) * size if causal else LEN
        q_cat = jnp.concatenate([q_ref[rows, lanes] * half_row(head % 2), qa_ref[rows, :]], axis=1)
        k_cat = jnp.concatenate([kt_ref[lanes, :keys], kat_ref[:, :keys]], axis=0)
        scores = nn(q_cat, k_cat)
        if causal:
            diag = scores[:, keys - size :] + bias
            scores = jnp.concatenate([scores[:, : keys - size], diag], axis=1) if block else diag
        return scores

    def finish(head, scores, lse_parts):
        half = half_row(head % 2)
        top = jnp.max(scores, axis=1, keepdims=True)
        probs = jnp.exp2(scores - top).astype(BF)
        values = v_ref[: scores.shape[1], pl.ds(head // 2 * LANES, LANES)]
        mixed = nn(probs, values * half + (1.0 - half).astype(BF))
        turned = pltpu.roll(mixed, 64, 1)
        lse = -(top + jnp.log2(turned if head % 2 == 0 else mixed))
        first = lse.astype(BF).astype(F32)
        rest = lse - first
        second = rest.astype(BF).astype(F32)
        for place, part in enumerate((first, second, rest - second)):
            lse_parts = jnp.where(lane == head * 3 + place, part, lse_parts)
        return mixed / turned, lse_parts

    for block in range(LEN // size):
        rows = pl.ds(block * size, size)
        waiting, outs = [], []
        lse_parts = jnp.zeros((size, LANES), F32)
        for step in range(HEADS + depth):
            if step < HEADS:
                waiting.append(score(block, step))
            if step >= depth:
                head = step - depth
                out, lse_parts = finish(head, waiting.pop(0), lse_parts)
                outs.append(out)
                if head % 2:
                    lanes = pl.ds(head // 2 * LANES, LANES)
                    o_ref[rows, lanes] = jnp.where(low, outs[-2], outs[-1]).astype(BF)
        qal_ref[rows, :] = (qa_ref[rows, :].astype(F32) + lse_parts).astype(BF)


def attend_backward(
    q_ref, k_ref, v_ref, do_ref, qal_ref, del_ref, ka_ref, dq_ref, dk_ref, dv_ref, p_ref, s_ref, kt_ref, dqt_ref,
    causal, span=(0, PAIRS),
):
    bias = causal_bias(True) if causal else None
    kt_ref[...] = k_ref[...].T

    def score(head, block):
        lanes = pl.ds(head // 2 * LANES, LANES)
        half = half_row(head % 2)
        rows = pl.ds(block * ROWS, ROWS)
        keys = (block + 1) * ROWS if causal else LEN
        marks = ka_ref[:keys, :] + lane_row(head * 3, 3)
        k_cat = jnp.concatenate([k_ref[:keys, lanes] * half, marks], axis=1)
        ones = jnp.broadcast_to(lane_row(head * 2, 2), (keys, LANES))
        v_cat = jnp.concatenate([v_ref[:keys, lanes] * half, ones], axis=1)
        q_cat = jnp.concatenate([q_ref[rows, lanes], qal_ref[rows, :]], axis=1)
        do_cat = jnp.concatenate([do_ref[rows, lanes], del_ref[rows, :]], axis=1)
        return nt(k_cat, q_cat), nt(v_cat, do_cat)

    def finish(head, block, scores, grads):
        rows = pl.ds(block * ROWS, ROWS)
        keys = scores.shape[0]
        if causal:
            diag = scores[keys - ROWS :] + bias
            scores = jnp.concatenate([scores[: keys - ROWS], diag], axis=0) if block else diag
        probs = jnp.exp2(scores)
        p_ref[head % 2, :keys, rows] = probs.astype(BF)
        inner = (probs * grads).astype(BF)
        s_ref[head % 2, :keys, rows] = inner
        own = pl.ds(head * 64, 64)
        dqt_ref[own, rows] = nn(kt_ref[own, :keys], inner)

    def pair_end(pair):
        lanes = pl.ds(pair * LANES, LANES)
        for kb in range(BLOCKS):
            rows = pl.ds(kb * ROWS, ROWS)
            first = kb * ROWS if causal else 0
            tail = pl.ds(first, LEN - first)
            do_pair = do_ref[tail, lanes]
            q_pair = q_ref[tail, lanes]
            dv = nn(p_ref[0, rows, tail], do_pair * half_row(0))
            dv = dv + nn(p_ref[1, rows, tail], do_pair * half_row(1))
            dv_ref[rows, lanes] = dv.astype(BF)
            dk = nn(s_ref[0, rows, tail], q_pair * half_row(0))
            dk = dk + nn(s_ref[1, rows, tail], q_pair * half_row(1))
            dk_ref[rows, lanes] = (dk * key_scale).astype(BF)

    steps = [(h, b) for h in range(2 * span[0], 2 * span[1]) for b in range(BLOCKS)]
    waiting = score(*steps[0])
    for place, (head, block) in enumerate(steps):
        current = waiting
        if place + 1 < len(steps):
            waiting = score(*steps[place + 1])
        finish(head, block, *current)
        if head % 2 and block == BLOCKS - 1:
            pair_end(head // 2)
    cols = pl.ds(span[0] * LANES, (span[1] - span[0]) * LANES)
    for block in range(BLOCKS):
        rows = pl.ds(block * ROWS, ROWS)
        dq_ref[rows, cols] = (dqt_ref[cols, rows] * 0.125).T.astype(BF)


def mix_gradient(g_ref, w_out, o_ref, do_ref, del_ref):
    lane = lax.broadcasted_iota(jnp.int32, (ROWS, LANES), 1)
    even = lane % 2 == 0
    col = lax.broadcasted_iota(jnp.int32, (D, LANES), 0) // 64
    pick = jnp.where(lax.broadcasted_iota(jnp.int32, (D, LANES), 1) // 2 == col, -1.0, 0.0).astype(BF)
    for qb in range(BLOCKS):
        rows = pl.ds(qb * ROWS, ROWS)
        do = nt(g_ref[rows, :], w_out).astype(BF)
        do_ref[rows, :] = do
        prod = do.astype(F32) * o_ref[rows, :].astype(F32)
        high = prod.astype(BF)
        inner = nn(high, pick) + nn((prod - high.astype(F32)).astype(BF), pick)
        first = inner.astype(BF).astype(F32)
        del_ref[rows, :] = jnp.where(even, first, inner - first).astype(BF)


def vec_row(vec_ref, index):
    return vec_ref[index : index + 1, :]


def fetch(core_ref, parts, w_ref, sems, rows=ROWS, first=0):
    core, chip = core_ref[0], core_ref[1]
    near, far = chip ^ (1 + core), chip ^ (2 - core)
    own, other = core, 1 - core
    moves = (
        (0, 0, chip, own),
        (1, 0, chip, other),
        (2, 0, near, own),
        (2, rows, near, other),
        (3, 0, far, other),
        (3, rows, far, own),
        (4, 0, chip ^ 3, own),
        (5, 0, chip ^ 3, other),
    )
    copies = []
    for i, (part, start, place, half) in enumerate(moves):
        source = parts[part].at[pl.ds(start + first, ROWS)]
        copies.append(pltpu.make_async_copy(source, w_ref.at[2 * place + half], sems.at[i]))
    for copy in copies:
        copy.start()
    return copies


def wait_all(copies):
    for copy in copies:
        copy.wait()


def square(w_ref, matrix):
    return w_ref[2 * matrix : 2 * matrix + 2].reshape(D, D)


def put_square(mine_ref, other_ref, core, matrix, turned_ref, grad, place=0):
    for ref, half in ((mine_ref, core), (other_ref, 1 - core)):
        rows = turned_ref[pl.ds(pl.multiple_of(half * ROWS, ROWS), ROWS), :]
        ref[matrix ^ place, :ROWS, :] = nn(rows, grad).astype(BF)


def put_square_tn(mine_ref, other_ref, core, matrix, left_ref, grad, place=0):
    for ref, half in ((mine_ref, core), (other_ref, 1 - core)):
        cols = left_ref[:, pl.ds(pl.multiple_of(half * ROWS, ROWS), ROWS)]
        ref[matrix ^ place, :ROWS, :] = tn(cols, grad).astype(BF)


def self_forward_kernel(
    core_ref, parts, x_ref, vec_ref, qa_ref, ka_ref,
    q_ref, k_ref, v_ref, o_ref, qal_ref, n_ref, r_ref,
    w_ref, kt_ref, kat_ref, sems,
):
    copies = fetch(core_ref, parts, w_ref, sems, FIRST_ROWS)
    wait_all(copies)
    for qb in range(BLOCKS):
        rows = pl.ds(qb * ROWS, ROWS)
        x = x_ref[rows, :]
        q_ref[rows, :] = ((nn(x, square(w_ref, 0)) + vec_row(vec_ref, 6)) * query_scale).astype(BF)
        k_ref[rows, :] = nn(x, square(w_ref, 1)).astype(BF)
        v_ref[rows, :] = (nn(x, square(w_ref, 2)) + vec_row(vec_ref, 7)).astype(BF)
    attend_forward(q_ref, k_ref, v_ref, qa_ref, ka_ref, o_ref, qal_ref, kt_ref, kat_ref, True)
    for qb in range(BLOCKS):
        rows = pl.ds(qb * ROWS, ROWS)
        resid = x_ref[rows, :].astype(F32) + nn(o_ref[rows, :], square(w_ref, 3)) + vec_row(vec_ref, 8)
        normed, inv_std = layer_norm(resid)
        n_ref[rows, :] = normed
        r_ref[rows, :] = jnp.broadcast_to(inv_std, (ROWS, LANES))


def cross_forward_kernel(
    core_ref, parts, n1_ref, m_ref, vec_ref, qa_ref, ka_ref,
    q_ref, k_ref, v_ref, o_ref, qal_ref, n_ref, r_ref,
    w_ref, kt_ref, kat_ref, sems,
):
    wait_all(fetch(core_ref, parts, w_ref, sems))
    for qb in range(BLOCKS):
        rows = pl.ds(qb * ROWS, ROWS)
        h = (n1_ref[rows, :] * vec_row(vec_ref, 0) + vec_row(vec_ref, 1)).astype(BF)
        m = m_ref[rows, :]
        q_ref[rows, :] = ((nn(h, square(w_ref, 0)) + vec_row(vec_ref, 9)) * query_scale).astype(BF)
        k_ref[rows, :] = nn(m, square(w_ref, 1)).astype(BF)
        v_ref[rows, :] = (nn(m, square(w_ref, 2)) + vec_row(vec_ref, 10)).astype(BF)
    attend_forward(q_ref, k_ref, v_ref, qa_ref, ka_ref, o_ref, qal_ref, kt_ref, kat_ref, False)
    for qb in range(BLOCKS):
        rows = pl.ds(qb * ROWS, ROWS)
        h = n1_ref[rows, :] * vec_row(vec_ref, 0) + vec_row(vec_ref, 1)
        resid = h + nn(o_ref[rows, :], square(w_ref, 3)) + vec_row(vec_ref, 11)
        normed, inv_std = layer_norm(resid)
        n_ref[rows, :] = normed
        r_ref[rows, :] = jnp.broadcast_to(inv_std, (ROWS, LANES))


def col_sum(x):
    return jnp.sum(x.astype(F32), axis=0, keepdims=True)


def ffn_kernel(
    core_ref, parts, n2_ref, r2_ref, cot_ref, vec_ref,
    out_ref, mine_ref, other_ref, dr_ref, vg_ref,
    w1_ref, w2_ref, u_ref, da_ref, h_ref, dz_ref, f_ref, ht_ref, sems1, sems2,
):
    copies = fetch(core_ref, parts, w1_ref, sems1, 2 * ROWS)
    copies += fetch(core_ref, parts, w2_ref, sems2, 2 * ROWS, ROWS)
    wait_all(copies)

    def w1_block(j):
        return w1_ref[:, 64 * j : 64 * j + 64].reshape(D, D)

    def w2_block(j):
        return square(w2_ref, j)

    vg_ref[...] = jnp.zeros_like(vg_ref)

    def one_tile(tile, carry):
        rows = pl.ds(pl.multiple_of(tile * ROWS, ROWS), ROWS)
        n2 = n2_ref[rows, :]
        h2 = n2 * vec_row(vec_ref, 2) + vec_row(vec_ref, 3)
        h2_low = h2.astype(BF)
        h_ref[rows, :] = h2_low
        resid = h2 + vec_row(vec_ref, 16)
        for j in range(4):
            a = nn(h2_low, w1_block(j)) + vec_row(vec_ref, 12 + j)
            s = 0.5 * jnp.tanh(0.5 * a) + 0.5
            u = (a * s).astype(BF)
            u_ref[rows, j * D : (j + 1) * D] = u
            f_ref[:, j * D : (j + 1) * D] = s * (1.0 + a * (1.0 - s))
            resid = resid + nn(u, w2_block(j))
        n3, inv3 = layer_norm(resid)
        gain3 = vec_row(vec_ref, 4)
        out_ref[rows, :] = (n3 * gain3 + vec_row(vec_ref, 5)).astype(BF)
        cot = cot_ref[rows, :].astype(F32)
        dr3 = norm_back(cot, n3, inv3, gain3)
        dz = dr3.astype(BF)
        dz_ref[rows, :] = dz
        vg_ref[4:5, :] += col_sum(cot * n3)
        vg_ref[5:6, :] += col_sum(cot)
        vg_ref[16:17, :] += col_sum(dz)
        dh = dr3
        for j in range(4):
            da = (nt(dz, w2_block(j)) * f_ref[:, j * D : (j + 1) * D]).astype(BF)
            da_ref[rows, j * D : (j + 1) * D] = da
            vg_ref[12 + j : 13 + j, :] += col_sum(da)
            dh = dh + nt(da, w1_block(j))
        vg_ref[2:3, :] += col_sum(dh * n2)
        vg_ref[3:4, :] += col_sum(dh)
        dr2 = norm_back(dh, n2, r2_ref[rows, 0:1], vec_row(vec_ref, 2))
        dr_ref[rows, :] = dr2
        vg_ref[11:12, :] += col_sum(dr2.astype(BF))
        return carry

    lax.fori_loop(0, BLOCKS, one_tile, 0)
    core = core_ref[0]
    ht_ref[...] = jnp.swapaxes(h_ref[...].T.reshape(4, 2, 64, LEN), 0, 1).reshape(2, ROWS, LEN)
    for j in range(4):
        da = da_ref[:, j * D : (j + 1) * D]
        dz = dz_ref[...]
        for ref, half in ((mine_ref, core), (other_ref, 1 - core)):
            dw1 = nn(ht_ref[half], da).astype(BF)
            ref[:, 64 * j : 64 * j + 64, :] = dw1.reshape(4, 64, D)
            cols = pl.ds(pl.multiple_of(j * D + half * ROWS, ROWS), ROWS)
            ref[j, ROWS:, :] = tn(u_ref[:, cols], dz).astype(BF)


def cross_backward_kernel(
    core_ref, parts, dr2_ref, vec_ref, q_ref, k_ref, v_ref, o_ref, qal_ref, ka_ref, n1_ref, r1_ref, mt_ref, vf_ref,
    mine_ref, other_ref, dr1_ref, dk_ref, dv_ref,
    g_ref, do_ref, del_ref, dq_ref, p_ref, s_ref, h_ref, w_ref, vg_ref, kt_ref, dqt_ref, sems,
):
    core = core_ref[0]
    copies = fetch(core_ref, parts, w_ref, sems)
    for qb in range(BLOCKS):
        rows = pl.ds(qb * ROWS, ROWS)
        g_ref[rows, :] = dr2_ref[rows, :].astype(BF)
        h_ref[rows, :] = (n1_ref[rows, :] * vec_row(vec_ref, 0) + vec_row(vec_ref, 1)).astype(BF)
    wait_all(copies)
    mix_gradient(g_ref, square(w_ref, 3), o_ref, do_ref, del_ref)
    put_square_tn(mine_ref, other_ref, core, 3, o_ref, g_ref[...])
    attend_backward(
        q_ref, k_ref, v_ref, do_ref, qal_ref, del_ref, ka_ref, dq_ref, dk_ref, dv_ref, p_ref, s_ref, kt_ref, dqt_ref, False
    )
    put_square_tn(mine_ref, other_ref, core, 0, h_ref, dq_ref[...])
    put_square(mine_ref, other_ref, core, 1, mt_ref, dk_ref[...])
    put_square(mine_ref, other_ref, core, 2, mt_ref, dv_ref[...])
    vg_ref[...] = vf_ref[...]
    for qb in range(BLOCKS):
        rows = pl.ds(qb * ROWS, ROWS)
        dq = dq_ref[rows, :]
        dv = dv_ref[rows, :]
        vg_ref[9:10, :] += col_sum(dq)
        vg_ref[10:11, :] += col_sum(dv)
        dh = dr2_ref[rows, :] + nt(dq, square(w_ref, 0))
        n1 = n1_ref[rows, :]
        vg_ref[0:1, :] += col_sum(dh * n1)
        vg_ref[1:2, :] += col_sum(dh)
        dr1 = norm_back(dh, n1, r1_ref[rows, 0:1], vec_row(vec_ref, 0))
        dr1_ref[rows, :] = dr1
        vg_ref[8:9, :] += col_sum(dr1.astype(BF))
    blank = jnp.zeros((12, D), F32)
    for ref, half in ((mine_ref, core), (other_ref, 1 - core)):
        for xy in range(4):
            low, high = vg_ref[8 * xy : 8 * xy + 4, :], vg_ref[8 * xy + 4 : 8 * xy + 8, :]
            rows = jnp.where(half == 0, low, high)
            ref[xy, ROWS:, :] = jnp.concatenate([rows, blank], axis=0).astype(BF)


def self_backward_start_kernel(
    core_ref, parts, dr1_ref, q_ref, k_ref, v_ref, o_ref, qal_ref, ka_ref,
    do_ref, del_ref, dq_ref, dk_ref, dv_ref,
    g_ref, p_ref, s_ref, w_ref, kt_ref, dqt_ref, sems,
):
    copies = fetch(core_ref, parts, w_ref, sems, FIRST_ROWS)
    for qb in range(BLOCKS):
        rows = pl.ds(qb * ROWS, ROWS)
        g_ref[rows, :] = dr1_ref[rows, :].astype(BF)
    wait_all(copies)
    mix_gradient(g_ref, square(w_ref, 3), o_ref, do_ref, del_ref)
    attend_backward(
        q_ref, k_ref, v_ref, do_ref, qal_ref, del_ref, ka_ref, dq_ref, dk_ref, dv_ref, p_ref, s_ref, kt_ref, dqt_ref, True,
        (0, EARLY_PAIRS),
    )


def self_backward_end_kernel(
    core_ref, dr1_ref, q_ref, k_ref, v_ref, o_ref, qal_ref, ka_ref, xt_ref,
    do_ref, del_ref, dqe_ref, dke_ref, dve_ref,
    mine_ref, other_ref, dq_ref, dk_ref, dv_ref,
    g_ref, p_ref, s_ref, late_ref, kt_ref, dqt_ref,
):
    core, chip = core_ref[0], core_ref[1]
    for qb in range(BLOCKS):
        rows = pl.ds(qb * ROWS, ROWS)
        g_ref[rows, :] = dr1_ref[rows, :].astype(BF)
    early = EARLY_PAIRS * LANES
    for ref, source in ((dq_ref, dqe_ref), (dk_ref, dke_ref), (dv_ref, dve_ref)):
        ref[:, :early] = source[:, :early]
    attend_backward(
        q_ref, k_ref, v_ref, do_ref, qal_ref, del_ref, ka_ref, dq_ref, dk_ref, dv_ref, p_ref, s_ref, kt_ref, dqt_ref, True,
        (EARLY_PAIRS, PAIRS),
    )
    put_square_tn(mine_ref, other_ref, core, 3, o_ref, g_ref[...], chip)
    put_square(mine_ref, other_ref, core, 0, xt_ref, dq_ref[...], chip)
    put_square(mine_ref, other_ref, core, 1, xt_ref, dk_ref[...], chip)
    put_square(mine_ref, other_ref, core, 2, xt_ref, dv_ref[...], chip)
    late_ref[...] = jnp.zeros_like(late_ref)
    for qb in range(BLOCKS):
        rows = pl.ds(qb * ROWS, ROWS)
        dq = dq_ref[rows, :]
        dv = dv_ref[rows, :]
        late_ref[0:1, :] += col_sum(dq)
        late_ref[1:2, :] += col_sum(dv)
    for ref, half in ((mine_ref, core), (other_ref, 1 - core)):
        for xy in range(4):
            place = pl.multiple_of((2 * (xy % 2) + half) * LANES, LANES)
            piece = late_ref[xy // 2 : xy // 2 + 1, pl.ds(place, LANES)]
            after = lax.broadcasted_iota(jnp.int32, (16, LANES), 0) >= 4
            ref[xy ^ chip, ROWS:, :] = jnp.zeros((16, D), BF)
            ref[xy ^ chip, ROWS:, :LANES] = jnp.where(after, piece, 0.0).astype(BF)


def input_grads_kernel(
    core_ref, parts, parts2, dr1_ref, dqs_ref, dks_ref, dvs_ref, dkc_ref, dvc_ref,
    ig_ref, mg_ref,
    w_ref, wc_ref, sems1, sems2,
):
    copies = fetch(core_ref, parts, w_ref, sems1, FIRST_ROWS)
    copies += fetch(core_ref, parts2, wc_ref, sems2)
    wait_all(copies)
    for qb in range(BLOCKS):
        rows = pl.ds(qb * ROWS, ROWS)
        total = dr1_ref[rows, :] + nt(dqs_ref[rows, :], square(w_ref, 0))
        total = total + nt(dks_ref[rows, :], square(w_ref, 1))
        ig_ref[rows, :] = (total + nt(dvs_ref[rows, :], square(w_ref, 2))).astype(BF)
        total = nt(dkc_ref[rows, :], square(wc_ref, 1))
        mg_ref[rows, :] = (total + nt(dvc_ref[rows, :], square(wc_ref, 2))).astype(BF)


def call(kernel, outs, scratch, flops, core, parts, args, sems=1):
    sds = [jax.ShapeDtypeStruct(shape, dtype) for shape, dtype in outs]
    arrays = [block for group in parts for block in group]
    moved = sum(a.size * a.dtype.itemsize for a in arrays + list(args))
    spaces = [pltpu.SMEM] + [pl.ANY] * len(arrays) + [pltpu.VMEM] * len(args)
    memory = [pltpu.VMEM(shape, dtype) for shape, dtype in scratch]
    memory += [pltpu.SemaphoreType.DMA((8,))] * sems

    def body(core_ref, *refs):
        groups = [refs[6 * i : 6 * i + 6] for i in range(len(parts))]
        kernel(core_ref, *groups, *refs[6 * len(parts) :])

    return pl.pallas_call(
        body,
        out_shape=sds,
        in_specs=[pl.BlockSpec(memory_space=space) for space in spaces],
        scratch_shapes=memory,
        compiler_params=pltpu.CompilerParams(vmem_limit_bytes=VMEM_BYTES),
        cost_estimate=pl.CostEstimate(flops=flops, bytes_accessed=moved, transcendentals=0),
    )(core, *arrays, *args)


TOK = (LEN, D)
STAT = (LEN, LANES)
OCT = (8, ROWS, D)
unit = 2 * LEN * D * D
FORWARD_OUTS = [(TOK, BF)] * 4 + [(STAT, BF), (TOK, F32), (STAT, F32)]
HALVES = ((4, ROWS + 16, D), BF)
TOKB = (TOK, BF)
PROBS = ((2, LEN, LEN), BF)
TURN = ((D, LEN), BF)
TURN32 = ((D, LEN), F32)
FORWARD_SCRATCH = [(OCT, BF), TURN, ((LANES, LEN), BF)]


def self_forward(core, w, *args):
    return call(self_forward_kernel, FORWARD_OUTS, FORWARD_SCRATCH, 20 * unit, core, [w], args)


def cross_forward(core, w, *args):
    return call(cross_forward_kernel, FORWARD_OUTS, FORWARD_SCRATCH, 25 * unit, core, [w], args)


def ffn(core, w, *args):
    outs = [TOKB, ((4, 2 * ROWS, D), BF), ((4, 2 * ROWS, D), BF), (TOK, F32), ((32, D), F32)]
    scratch = [(OCT, BF), (OCT, BF), ((LEN, FF), BF), ((LEN, FF), BF), TOKB, TOKB]
    scratch += [((ROWS, FF), F32), ((2, ROWS, LEN), BF)]
    return call(ffn_kernel, outs, scratch, 26 * unit, core, [w], args, 2)


def cross_backward(core, w, *args):
    outs = [HALVES, HALVES, (TOK, F32), TOKB, TOKB]
    scratch = [TOKB, TOKB, (STAT, BF), TOKB, PROBS, PROBS, TOKB, (OCT, BF), ((32, D), F32), TURN, TURN32]
    return call(cross_backward_kernel, outs, scratch, 50 * unit, core, [w], args)


def self_backward_start(core, w, *args):
    outs = [TOKB, (STAT, BF), TOKB, TOKB, TOKB]
    scratch = [TOKB, PROBS, PROBS, (OCT, BF), TURN, TURN32]
    return call(self_backward_start_kernel, outs, scratch, 25 * unit, core, [w], args)


def self_backward_end(core, *args):
    outs = [HALVES, HALVES, TOKB, TOKB, TOKB]
    scratch = [TOKB, PROBS, PROBS, ((8, D), F32), TURN, TURN32]
    return call(self_backward_end_kernel, outs, scratch, 12 * unit, core, [], args, 0)


def input_grads(core, ws, wc, *args):
    scratch = [(OCT, BF), (OCT, BF)]
    return call(input_grads_kernel, [TOKB, TOKB], scratch, 6 * unit, core, [ws, wc], args, 2)


SQUARES = 8 * D * D
VEC_ROWS = 17
VEC_LEN = VEC_ROWS * D


def groups_xy():
    return [[z * 8 + c * 2 + core for c in range(4)] for z in range(4) for core in range(2)]


def groups_z():
    return [[z * 8 + p for z in range(4)] for p in range(8)]


def swap(x, bit):
    return lax.ppermute(x, "dp", [(i, i ^ bit) for i in range(32)])


def turn_w1(chunk, here, out_first):
    if out_first:
        alt = chunk.reshape(64, 4, D).transpose(1, 0, 2).reshape(ROWS, D)
    else:
        alt = chunk.reshape(4, 64, D).transpose(1, 0, 2).reshape(ROWS, D)
    return jnp.where(here, alt, chunk)


def along_z(x, moves):
    return lax.ppermute(x, "dp", [(8 * a + p, 8 * b + p) for a, b in moves for p in range(8)])


def gather_blocks(params, index, others):
    low = params.astype(BF)
    share = low.shape[0]
    shift = share - ROWS * D
    z = index // 8
    prev = lax.ppermute(low[share - VEC_LEN :], "dp", [(i, (i + 1) % 32) for i in range(32)])
    flat = lax.dynamic_slice(jnp.concatenate([prev, low]), (VEC_LEN - shift * index,), (ROWS * D,))
    chunk = turn_w1(flat.reshape(ROWS, D), z == 2, True)
    vec = jnp.pad(prev.reshape(VEC_ROWS, D), ((0, 15), (0, 0)))
    mine = jnp.concatenate([chunk, vec])
    first = along_z(mine, ((0, 2), (1, 0), (2, 3), (3, 1)))
    first, others = lax.optimization_barrier((first, others))
    second = along_z(jnp.where(z == 2, first, mine), ((0, 1), (1, 2), (2, 3)))
    third = along_z(jnp.where(z == 1, first, mine)[:ROWS], ((3, 2), (2, 1), (1, 0)))
    second, third = lax.optimization_barrier((second, third))
    block0 = jnp.where(z == 0, mine, jnp.where(z == 2, first, second))
    fourth = along_z(jnp.where(z == 1, third, second[:ROWS]), ((1, 0), (2, 3)))
    pair0, near0 = to_sides(block0)
    near0, fourth = lax.optimization_barrier((near0, fourth))
    first, second = first[:ROWS], second[:ROWS]

    def pick(*blocks):
        return jnp.where(z < 2, jnp.where(z == 0, *blocks[:2]), jnp.where(z == 2, *blocks[2:]))

    block1 = pick(first, chunk, second, fourth)
    block2 = pick(fourth, third, chunk, first)
    block3 = pick(third, first, third, chunk)
    across0 = to_corners(near0)
    pair1, near1 = to_sides(block1)
    across0, near1 = lax.optimization_barrier((across0, near1))
    part0 = finish_block(pair0, near0, across0)
    across1 = to_corners(near1)
    pair2, near2 = to_sides(jnp.concatenate([block2, block3]))
    core, chip = index % 2, index % 8 // 2
    rows = [part0[0], part0[1], part0[2], part0[2], part0[3], part0[3], part0[4], part0[5]]
    starts = [ROWS, ROWS, ROWS, 2 * ROWS + 32, ROWS, 2 * ROWS + 32, ROWS, ROWS]
    rows = jnp.stack([lax.slice_in_dim(a, s, s + 32) for a, s in zip(rows, starts)])
    place = jnp.where(chip == 0, core, jnp.where(chip == 3, 6 + core, jnp.where(chip == 1 + core, 2 + core, 5 - core)))
    source = lax.dynamic_index_in_dim(rows, place, 0, keepdims=False)
    return part0, (pair1, near1, across1), (pair2, near2), source.astype(F32), others


def sides(first, second):
    return [(i, i ^ (first if i % 2 == 0 else second)) for i in range(32)]


def to_sides(block):
    pair = (block, swap(block, 1))
    return pair, lax.ppermute(jnp.concatenate(pair), "dp", sides(2, 4))


def to_corners(near):
    return lax.ppermute(near[: near.shape[0] // 2], "dp", sides(4, 2))


def finish_block(pair, near, across):
    return [*pair, near, swap(near, 1), across, swap(across, 1)]


def gather_plain(params, index, others):
    flat = lax.all_gather(params.astype(BF), "dp", axis=0, tiled=True)
    end = SQUARES + D * FF
    w1 = flat[SQUARES:end].reshape(8, 64, 4, D).transpose(0, 2, 1, 3).reshape(8, ROWS, D)
    w2 = flat[end : end + D * FF].reshape(8, ROWS, D)
    vec = flat[end + D * FF :].reshape(VEC_ROWS, D).astype(F32)
    mats = flat[:SQUARES].reshape(2, 4, 2, ROWS, D)

    core = index % 2

    def parts(pairs, rows):
        pairs = jnp.pad(pairs, ((0, 0), (0, 0), (0, rows - pairs.shape[2]), (0, 0)))
        own = lax.dynamic_index_in_dim(pairs, core, 1, keepdims=False)
        other = lax.dynamic_index_in_dim(pairs, 1 - core, 1, keepdims=False)
        one, two = jnp.concatenate([own, other], axis=1), jnp.concatenate([other, own], axis=1)
        near = lax.dynamic_index_in_dim(one, 1 + core, 0, keepdims=False)
        far = lax.dynamic_index_in_dim(two, 2 - core, 0, keepdims=False)
        return [own[0], other[0], near, far, own[3], other[3]]

    vec = jnp.pad(vec, ((0, 15), (0, 0)))
    wide = jnp.concatenate([w1.reshape(4, 2, ROWS, D), w2.reshape(4, 2, ROWS, D)], axis=2)
    return parts(mats[0], FIRST_ROWS), parts(mats[1], ROWS), parts(wide, 2 * ROWS), vec, others


def plane_sum(mine, other):
    pair = (mine.astype(F32) + swap(other, 1).astype(F32)).astype(BF)
    parts = lax.all_to_all(pair, "dp", 0, 0, tiled=True, axis_index_groups=groups_xy())
    return jnp.sum(parts.astype(F32), axis=0).astype(BF)


def add(a, b):
    return (a.astype(F32) + b.astype(F32)).astype(BF)


def first_round(part_c, part_f, z):
    extra = part_c[ROWS:]
    part_1 = jnp.concatenate([part_f[:ROWS], extra])
    part_2 = jnp.concatenate([part_f[ROWS:], extra])
    return part_c, part_1, part_2, along_z(jnp.where(z == 0, part_1, part_c), ((0, 1), (3, 2)))


def finish_blocks(mine, other, blocks, index):
    z = index // 8
    got = swap(other, 1)
    pairs = [(mine[j].astype(F32) + got[j].astype(F32)).astype(BF) for j in range(4)]
    part_c, part_1, part_2, early = blocks
    part = pairs[0].astype(F32) + swap(pairs[1], 2).astype(F32) + swap(pairs[2], 4).astype(F32)
    part = part + swap(pairs[3], 6).astype(F32)
    part = (part + jnp.pad(part_c[ROWS:].astype(F32), ((ROWS, 0), (0, 0)))).astype(BF)
    left = jnp.where(z == 2, add(part_c, early), part)
    right = jnp.where(z == 1, add(part_1, early), part_2)
    got_left = along_z(left, ((1, 0), (2, 1), (3, 2)))
    got_right = along_z(right, ((0, 1), (1, 2), (2, 3)))
    last = jnp.where(z < 2, jnp.where(z == 0, part_c, add(part_2, got_right)), jnp.where(z == 2, add(part, got_left), part_1))
    got = along_z(last, ((2, 0), (0, 1), (3, 2), (1, 3)))
    own = jnp.where(z < 2, jnp.where(z == 0, part, part_c), jnp.where(z == 2, part_1, part_2)).astype(F32)
    own = own + jnp.where(z < 2, got_left, got_right).astype(F32) + got.astype(F32)
    chunk = own[:ROWS]
    flat = turn_w1(chunk, z == 2, False).reshape(ROWS * D)
    after = lax.ppermute(flat[:VEC_LEN], "dp", [(i + 1, i) for i in range(31)])
    pieces = jnp.concatenate(
        [
            lax.dynamic_index_in_dim(own[ROWS : ROWS + 4], z, 0, keepdims=False).reshape(4, LANES),
            own[ROWS + 4 : ROWS + 5, :LANES],
            jnp.full((3, LANES), jnp.sum(chunk * chunk)),
        ]
    )
    pieces = jnp.broadcast_to(pieces[None], (32, 8, LANES))
    pieces = lax.all_to_all(pieces, "dp", 0, 0, tiled=True)
    vec = pieces[:, :4].reshape(4, 8, D).transpose(1, 0, 2).reshape(32, D)
    late = jnp.pad(pieces[:8, 4].reshape(2, D), ((6, 9), (0, 0)))
    vec = (vec[:VEC_ROWS] + late).reshape(VEC_LEN)
    square = jnp.sum(pieces[:, 5, 0]) + jnp.sum(vec * vec)
    after = jnp.where(index == 31, vec, after)
    share = lax.dynamic_slice(jnp.concatenate([flat, after]), (272 * index,), (ROWS * D + 272,))
    return share, vec, square


def share_plain(pairs, index, share_len):
    def joined(mine, other):
        low = jnp.where(index % 2 == 0, mine, other).astype(F32)
        return jnp.stack([low, jnp.where(index % 2 == 0, other, mine).astype(F32)], axis=1)

    self_g, cross_g, ffn_g = (joined(*pair) for pair in pairs)
    dw1 = ffn_g[:, :, :ROWS].reshape(8, 4, 64, D).transpose(0, 2, 1, 3)
    vec = cross_g[:, :, ROWS : ROWS + 4].reshape(32, D)
    late = jnp.pad(self_g[:, :, ROWS + 4, :LANES].reshape(2, D), ((6, 9), (0, 0)))
    vec = vec[:VEC_ROWS] + late
    parts = (self_g[:, :, :ROWS], cross_g[:, :, :ROWS], dw1, ffn_g[:, :, ROWS:], vec)
    flat = lax.psum(jnp.concatenate([g.reshape(-1) for g in parts]), "dp")
    share = lax.dynamic_slice(flat, (index * share_len,), (share_len,))
    return share, flat[-VEC_LEN:], jnp.sum(flat * flat)


def shards(count, targets, memory, target_ids, memory_ids, cotangent, params, first_moment, second_moment):
    index = lax.axis_index("dp")
    blocked = count == 32
    place = jnp.where(blocked, index % 8 // 2, 0)
    core = jnp.stack([index % 2, place]).astype(jnp.int32)
    lane = jnp.arange(LANES)[None, :] - MASK_LANE
    live = (lane >= 0) & (lane < 8)
    same_t = lane == target_ids[:, None]
    same_m = lane == memory_ids[:, None]
    others = (
        jnp.where(live & ~same_t, masked_value, 0.0).astype(BF),
        jnp.where(same_t, 1.0, 0.0).astype(BF),
        jnp.where(same_m, 1.0, 0.0).astype(BF),
        memory.T,
        targets.T,
        core,
    )
    gather = gather_blocks if blocked else gather_plain
    ws, wc, wide, vec, others = gather(params, index, others)
    qa, ka_self, ka_cross, memory_turn, targets_turn, core = others
    qs, ks, vs, os, qal_s, n1, r1 = self_forward(core, ws, targets, vec, qa, ka_self)
    if blocked:
        wc, wide, n1 = lax.optimization_barrier((wc, wide, n1))
        wc = finish_block(*wc)
        across = to_corners(wide[1])
    qc, kc, vc, oc, qal_c, n2, r2 = cross_forward(core, wc, n1, memory, vec, qa, ka_cross)
    if blocked:
        across, n2 = lax.optimization_barrier((across, n2))
        wide = finish_block(*wide, across)
    out, mine_f, other_f, dr2, vg_f = ffn(core, wide, n2, r2, cotangent, vec)
    mine_c, other_c, dr1, dkc, dvc = cross_backward(
        core, wc, dr2, vec, qc, kc, vc, oc, qal_c, ka_cross, n1, r1, memory_turn, vg_f
    )
    if blocked:
        part_f = plane_sum(mine_f, other_f)
        part_f, mine_c, other_c, dr1 = lax.optimization_barrier((part_f, mine_c, other_c, dr1))
        part_c = plane_sum(mine_c, other_c)
    early = self_backward_start(core, ws, dr1, qs, ks, vs, os, qal_s, ka_self)
    if blocked:
        part_c, early = lax.optimization_barrier((part_c, early))
        blocks = first_round(part_c, part_f, index // 8)
    mine_s, other_s, dqs, dks, dvs = self_backward_end(
        core, dr1, qs, ks, vs, os, qal_s, ka_self, targets_turn, *early
    )
    input_grad, memory_grad = input_grads(core, ws, wc, dr1, dqs, dks, dvs, dkc, dvc)
    if blocked:
        blocks, mine_s, other_s = lax.optimization_barrier((blocks, mine_s, other_s))
        grad, vec_total, square = finish_blocks(mine_s, other_s, blocks, index)
    else:
        pairs = ((mine_s, other_s), (mine_c, other_c), (mine_f, other_f))
        grad, vec_total, square = share_plain(pairs, index, params.shape[0])
    norm_value = jnp.sqrt(square)
    factor = jnp.minimum(1.0, clip_limit / (norm_value + 1e-06))
    clipped = grad * factor
    new_first = beta_one * first_moment + (1.0 - beta_one) * clipped
    new_second = beta_two * second_moment + (1.0 - beta_two) * clipped * clipped
    first_hat = new_first / (1.0 - beta_one**STEP)
    second_hat = new_second / (1.0 - beta_two**STEP)
    new_params = params - step_rate * (
        first_hat / (jnp.sqrt(second_hat) + adam_eps) + weight_decay * params
    )
    return (
        out,
        input_grad,
        memory_grad,
        norm_value,
        grad,
        vec_total,
        new_params,
        new_first,
        new_second,
        new_params.astype(BF),
    )


def solution(mesh):
    rows, flat = P("dp", None), P("dp")
    return jax.shard_map(
        functools.partial(shards, mesh.shape["dp"]),
        mesh=mesh,
        in_specs=(rows, rows, flat, flat, rows, flat, flat, flat),
        out_specs=(rows, rows, rows, P(), flat, P(), flat, flat, flat, flat),
        check_vma=False,
    )
```

```python
import functools
import jax
import jax.numpy as jnp
from jax import lax
from jax.experimental import pallas as pl
from jax.experimental.pallas import tpu as pltpu
from jax.sharding import PartitionSpec as P

D = 512
FF = 2048
HEADS = 8
LEN = 1024
STEP = 10
ROWS = 256
BLOCKS = LEN // ROWS
TALL = 512
TALLS = LEN // TALL
LANES = 128
PAIRS = D // LANES
MASK_LANE = 32
EARLY_PAIRS = 3
FIRST_ROWS = ROWS + 32

eps_norm = 1e-05
beta_one = 0.9
beta_two = 0.999
adam_eps = 1e-08
step_rate = 0.05
weight_decay = 0.01
clip_limit = 1.0
masked_value = -1e30
log2_e = 1.4426950408889634
query_scale = 0.125 * log2_e
key_scale = 1.0 / log2_e

BF = jnp.bfloat16
F32 = jnp.float32
VMEM_BYTES = 60 * 1024 * 1024


def nn(a, b):
    return jnp.dot(a, b, preferred_element_type=F32)


def nt(a, b):
    return lax.dot_general(a, b, (((1,), (1,)), ((), ())), preferred_element_type=F32)


def tn(a, b):
    return lax.dot_general(a, b, (((0,), (0,)), ((), ())), preferred_element_type=F32)


def layer_norm(resid):
    center = resid - jnp.mean(resid, axis=1, keepdims=True)
    inv_std = lax.rsqrt(jnp.mean(center * center, axis=1, keepdims=True) + eps_norm)
    return center * inv_std, inv_std


def norm_back(grad, normed, inv_std, gain):
    scaled = grad * gain
    return inv_std * (
        scaled
        - jnp.mean(scaled, axis=1, keepdims=True)
        - normed * jnp.mean(scaled * normed, axis=1, keepdims=True)
    )


def half_row(parity):
    lane = lax.broadcasted_iota(jnp.int32, (1, LANES), 1)
    inside = (lane // 64) == parity
    return jnp.where(inside, 1.0, 0.0).astype(BF)


def lane_row(first, count):
    lane = lax.broadcasted_iota(jnp.int32, (1, LANES), 1)
    inside = (lane >= first) & (lane < first + count)
    return jnp.where(inside, 1.0, 0.0).astype(BF)


def causal_bias(transposed):
    row = lax.broadcasted_iota(jnp.int32, (ROWS, ROWS), 0)
    col = lax.broadcasted_iota(jnp.int32, (ROWS, ROWS), 1)
    ok = (row <= col) if transposed else (col <= row)
    return jnp.where(ok, 0.0, masked_value)


def attend_forward(moves, q_ref, k_ref, v_ref, qa_ref, ka_ref, o_ref, qal_ref, kt_ref, kat_ref, causal):
    size, depth = (ROWS, 2) if causal else (2 * ROWS, 1)
    lane = lax.broadcasted_iota(jnp.int32, (size, LANES), 1)
    low = lane < 64
    bias = causal_bias(False) if causal else None
    kt_ref[...] = k_ref[...].T
    kat_ref[...] = ka_ref[...].T

    def score(block, head):
        rows = pl.ds(block * size, size)
        lanes = pl.ds(head // 2 * LANES, LANES)
        keys = (block + 1) * size if causal else LEN
        q_cat = jnp.concatenate([q_ref[rows, lanes] * half_row(head % 2), qa_ref[rows, :]], axis=1)
        k_cat = jnp.concatenate([kt_ref[lanes, :keys], kat_ref[:, :keys]], axis=0)
        scores = nn(q_cat, k_cat)
        if causal:
            diag = scores[:, keys - size :] + bias
            scores = jnp.concatenate([scores[:, : keys - size], diag], axis=1) if block else diag
        return scores

    def finish(head, scores, lse_parts):
        half = half_row(head % 2)
        top = jnp.max(scores, axis=1, keepdims=True)
        probs = jnp.exp2(scores - top).astype(BF)
        values = v_ref[: scores.shape[1], pl.ds(head // 2 * LANES, LANES)]
        mixed = nn(probs, values * half + (1.0 - half).astype(BF))
        turned = pltpu.roll(mixed, 64, 1)
        lse = -(top + jnp.log2(turned if head % 2 == 0 else mixed))
        first = lse.astype(BF).astype(F32)
        rest = lse - first
        second = rest.astype(BF).astype(F32)
        for place, part in enumerate((first, second, rest - second)):
            lse_parts = jnp.where(lane == head * 3 + place, part, lse_parts)
        return mixed / turned, lse_parts

    for block in range(LEN // size):
        rows = pl.ds(block * size, size)
        waiting, outs = [], []
        lse_parts = jnp.zeros((size, LANES), F32)
        for step in range(HEADS + depth):
            if step < HEADS:
                waiting.append(score(block, step))
            if step >= depth:
                head = step - depth
                out, lse_parts = finish(head, waiting.pop(0), lse_parts)
                outs.append(out)
                if head % 2:
                    lanes = pl.ds(head // 2 * LANES, LANES)
                    o_ref[rows, lanes] = jnp.where(low, outs[-2], outs[-1]).astype(BF)
        qal_ref[rows, :] = (qa_ref[rows, :].astype(F32) + lse_parts).astype(BF)
        moves.done(o_ref, rows)
        moves.done(qal_ref, rows)


def attend_backward(
    q_ref, k_ref, v_ref, do_ref, qal_ref, del_ref, ka_ref, dq_ref, dk_ref, dv_ref, p_ref, s_ref, kt_ref, dqt_ref,
    causal, span=(0, PAIRS),
):
    bias = causal_bias(True) if causal else None
    cols = pl.ds(span[0] * LANES, (span[1] - span[0]) * LANES)
    kt_ref[cols, :] = k_ref[:, cols].T

    def score(head, block):
        lanes = pl.ds(head // 2 * LANES, LANES)
        half = half_row(head % 2)
        rows = pl.ds(block * ROWS, ROWS)
        keys = (block + 1) * ROWS if causal else LEN
        marks = ka_ref[:keys, :] + lane_row(head * 3, 3)
        k_cat = jnp.concatenate([k_ref[:keys, lanes] * half, marks], axis=1)
        ones = jnp.broadcast_to(lane_row(head * 2, 2), (keys, LANES))
        v_cat = jnp.concatenate([v_ref[:keys, lanes] * half, ones], axis=1)
        q_cat = jnp.concatenate([q_ref[rows, lanes], qal_ref[rows, :]], axis=1)
        do_cat = jnp.concatenate([do_ref[rows, lanes], del_ref[rows, :]], axis=1)
        return nt(k_cat, q_cat), nt(v_cat, do_cat)

    def finish(head, block, scores, grads):
        rows = pl.ds(block * ROWS, ROWS)
        keys = scores.shape[0]
        if causal:
            diag = scores[keys - ROWS :] + bias
            scores = jnp.concatenate([scores[: keys - ROWS], diag], axis=0) if block else diag
        probs = jnp.exp2(scores)
        p_ref[head % 2, :keys, rows] = probs.astype(BF)
        inner = (probs * grads).astype(BF)
        s_ref[head % 2, :keys, rows] = inner
        own = pl.ds(head * 64, 64)
        dqt_ref[own, rows] = nn(kt_ref[own, :keys], inner)

    def pair_end(pair):
        lanes = pl.ds(pair * LANES, LANES)
        for kb in range(BLOCKS):
            rows = pl.ds(kb * ROWS, ROWS)
            first = kb * ROWS if causal else 0
            tail = pl.ds(first, LEN - first)
            do_pair = do_ref[tail, lanes]
            q_pair = q_ref[tail, lanes]
            dv = nn(p_ref[0, rows, tail], do_pair * half_row(0))
            dv = dv + nn(p_ref[1, rows, tail], do_pair * half_row(1))
            dv_ref[rows, lanes] = dv.astype(BF)
            dk = nn(s_ref[0, rows, tail], q_pair * half_row(0))
            dk = dk + nn(s_ref[1, rows, tail], q_pair * half_row(1))
            dk_ref[rows, lanes] = (dk * key_scale).astype(BF)

    steps = [(h, b) for h in range(2 * span[0], 2 * span[1]) for b in range(BLOCKS)]
    waiting = score(*steps[0])
    for place, (head, block) in enumerate(steps):
        current = waiting
        if place + 1 < len(steps):
            waiting = score(*steps[place + 1])
        finish(head, block, *current)
        if head % 2 and block == BLOCKS - 1:
            pair_end(head // 2)
    for block in range(BLOCKS):
        rows = pl.ds(block * ROWS, ROWS)
        dq_ref[rows, cols] = (dqt_ref[cols, rows] * 0.125).T.astype(BF)


def mix_gradient(g_ref, w_out, o_ref, do_ref, del_ref):
    lane = lax.broadcasted_iota(jnp.int32, (TALL, LANES), 1)
    even = lane % 2 == 0
    col = lax.broadcasted_iota(jnp.int32, (D, LANES), 0) // 64
    pick = jnp.where(lax.broadcasted_iota(jnp.int32, (D, LANES), 1) // 2 == col, -1.0, 0.0).astype(BF)
    for qb in range(TALLS):
        rows = pl.ds(qb * TALL, TALL)
        do = nt(g_ref[rows, :], w_out).astype(BF)
        do_ref[rows, :] = do
        prod = do.astype(F32) * o_ref[rows, :].astype(F32)
        high = prod.astype(BF)
        inner = nn(high, pick) + nn((prod - high.astype(F32)).astype(BF), pick)
        first = inner.astype(BF).astype(F32)
        del_ref[rows, :] = jnp.where(even, first, inner - first).astype(BF)


def vec_row(vec_ref, index):
    return vec_ref[index : index + 1, :]


class Moves:
    def __init__(self, sems):
        self.sems, self.used = sems, 0
        self.inward, self.outward = {}, []

    def copy(self, source, target):
        move = pltpu.make_async_copy(source, target, self.sems.at[self.used])
        self.used += 1
        move.start()
        return move

    def bring(self, source, target, key):
        self.inward.setdefault(id(key), []).append(self.copy(source, target))

    def need(self, *refs):
        for ref in refs:
            for move in self.inward.pop(id(ref), []):
                move.wait()

    def pair(self, scratch, out):
        self.outs = getattr(self, "outs", {})
        self.outs[id(scratch)] = out

    def done(self, ref, *where):
        out = self.outs[id(ref)]
        if where:
            ref, out = ref.at[where], out.at[where]
        self.outward.append(self.copy(ref, out))

    def finish(self):
        for moves in self.inward.values():
            for move in moves:
                move.wait()
        for move in self.outward:
            move.wait()


def fetch(moves, core_ref, parts, w_ref, rows=ROWS, first=0):
    core, chip = core_ref[0], core_ref[1]
    near, far = chip ^ (1 + core), chip ^ (2 - core)
    own, other = core, 1 - core
    places = (
        (0, 0, chip, own),
        (1, 0, chip, other),
        (2, 0, near, own),
        (2, rows, near, other),
        (3, 0, far, other),
        (3, rows, far, own),
        (4, 0, chip ^ 3, own),
        (5, 0, chip ^ 3, other),
    )
    for part, start, place, half in places:
        source = parts[part].at[pl.ds(start + first, ROWS)]
        moves.bring(source, w_ref.at[2 * place + half], w_ref)


def square(w_ref, matrix):
    return w_ref[2 * matrix : 2 * matrix + 2].reshape(D, D)


def put_square(mine_ref, other_ref, core, matrix, turned_ref, grad, place=0):
    halves = [turned_ref[pl.ds(pl.multiple_of(h * ROWS, ROWS), ROWS), :] for h in (core, 1 - core)]
    both = nn(jnp.concatenate(halves, axis=0), grad).astype(BF)
    mine_ref[matrix ^ place, :ROWS, :] = both[:ROWS]
    other_ref[matrix ^ place, :ROWS, :] = both[ROWS:]


def put_square_tn(mine_ref, other_ref, core, matrix, left_ref, grad, place=0):
    halves = [left_ref[:, pl.ds(pl.multiple_of(h * ROWS, ROWS), ROWS)] for h in (core, 1 - core)]
    both = tn(jnp.concatenate(halves, axis=1), grad).astype(BF)
    mine_ref[matrix ^ place, :ROWS, :] = both[:ROWS]
    other_ref[matrix ^ place, :ROWS, :] = both[ROWS:]


def self_forward_kernel(
    moves, core_ref, parts, x_ref, vec_ref, qa_ref, ka_ref,
    q_ref, k_ref, v_ref, o_ref, qal_ref, n_ref, r_ref,
    w_ref, kt_ref, kat_ref,
):
    fetch(moves, core_ref, parts, w_ref, FIRST_ROWS)
    moves.need(x_ref, vec_ref, w_ref)
    for qb in range(TALLS):
        rows = pl.ds(qb * TALL, TALL)
        x = x_ref[rows, :]
        q_ref[rows, :] = ((nn(x, square(w_ref, 0)) + vec_row(vec_ref, 6)) * query_scale).astype(BF)
        k_ref[rows, :] = nn(x, square(w_ref, 1)).astype(BF)
        v_ref[rows, :] = (nn(x, square(w_ref, 2)) + vec_row(vec_ref, 7)).astype(BF)
    moves.need(qa_ref, ka_ref)
    for ref in (q_ref, k_ref, v_ref):
        moves.done(ref)
    attend_forward(moves, q_ref, k_ref, v_ref, qa_ref, ka_ref, o_ref, qal_ref, kt_ref, kat_ref, True)
    for qb in range(TALLS):
        rows = pl.ds(qb * TALL, TALL)
        resid = x_ref[rows, :].astype(F32) + nn(o_ref[rows, :], square(w_ref, 3)) + vec_row(vec_ref, 8)
        normed, inv_std = layer_norm(resid)
        n_ref[rows, :] = normed
        r_ref[rows, :] = jnp.broadcast_to(inv_std, (TALL, LANES))
        moves.done(n_ref, rows)
    moves.done(r_ref)


def cross_forward_kernel(
    moves, core_ref, parts, n1_ref, vec_ref, m_ref, qa_ref, ka_ref,
    q_ref, k_ref, v_ref, o_ref, qal_ref, n_ref, r_ref,
    w_ref, kt_ref, kat_ref,
):
    fetch(moves, core_ref, parts, w_ref)
    moves.need(m_ref, vec_ref, w_ref)
    for qb in range(TALLS):
        rows = pl.ds(qb * TALL, TALL)
        m = m_ref[rows, :]
        k_ref[rows, :] = nn(m, square(w_ref, 1)).astype(BF)
        v_ref[rows, :] = (nn(m, square(w_ref, 2)) + vec_row(vec_ref, 10)).astype(BF)
    moves.need(n1_ref)
    for qb in range(TALLS):
        rows = pl.ds(qb * TALL, TALL)
        h = (n1_ref[rows, :] * vec_row(vec_ref, 0) + vec_row(vec_ref, 1)).astype(BF)
        q_ref[rows, :] = ((nn(h, square(w_ref, 0)) + vec_row(vec_ref, 9)) * query_scale).astype(BF)
    moves.need(qa_ref, ka_ref)
    for ref in (q_ref, k_ref, v_ref):
        moves.done(ref)
    attend_forward(moves, q_ref, k_ref, v_ref, qa_ref, ka_ref, o_ref, qal_ref, kt_ref, kat_ref, False)
    for qb in range(TALLS):
        rows = pl.ds(qb * TALL, TALL)
        h = n1_ref[rows, :] * vec_row(vec_ref, 0) + vec_row(vec_ref, 1)
        resid = h + nn(o_ref[rows, :], square(w_ref, 3)) + vec_row(vec_ref, 11)
        normed, inv_std = layer_norm(resid)
        n_ref[rows, :] = normed
        r_ref[rows, :] = jnp.broadcast_to(inv_std, (TALL, LANES))
        moves.done(n_ref, rows)
    moves.done(r_ref)


def col_sum(x):
    return jnp.sum(x.astype(F32), axis=0, keepdims=True)


def ffn_kernel(
    moves, core_ref, parts, n2_ref, vec_ref, cot_ref, r2_ref,
    out_ref, mine_ref, other_ref, dr_ref, vg_ref,
    w1_ref, w2_ref, u_ref, da_ref, h_ref, dz_ref, f_ref, ht_ref,
):
    fetch(moves, core_ref, parts, w1_ref, 2 * ROWS)
    fetch(moves, core_ref, parts, w2_ref, 2 * ROWS, ROWS)

    def w1_block(j):
        return w1_ref[:, 64 * j : 64 * j + 64].reshape(D, D)

    def w2_block(j):
        return square(w2_ref, j)

    vg_ref[...] = jnp.zeros_like(vg_ref)
    moves.need(n2_ref, vec_ref, w1_ref)
    for tile in range(TALLS):
        rows = pl.ds(tile * TALL, TALL)
        n2 = n2_ref[rows, :]
        h2 = n2 * vec_row(vec_ref, 2) + vec_row(vec_ref, 3)
        h2_low = h2.astype(BF)
        h_ref[rows, :] = h2_low
        resid = h2 + vec_row(vec_ref, 16)
        for j in range(4):
            a = nn(h2_low, w1_block(j)) + vec_row(vec_ref, 12 + j)
            s = 0.5 * jnp.tanh(0.5 * a) + 0.5
            u = (a * s).astype(BF)
            u_ref[rows, j * D : (j + 1) * D] = u
            f_ref[:, j * D : (j + 1) * D] = s * (1.0 + a * (1.0 - s))
            moves.need(w2_ref)
            resid = resid + nn(u, w2_block(j))
        n3, inv3 = layer_norm(resid)
        gain3 = vec_row(vec_ref, 4)
        out_ref[rows, :] = (n3 * gain3 + vec_row(vec_ref, 5)).astype(BF)
        moves.done(out_ref, rows)
        moves.need(cot_ref)
        cot = cot_ref[rows, :].astype(F32)
        dr3 = norm_back(cot, n3, inv3, gain3)
        dz = dr3.astype(BF)
        dz_ref[rows, :] = dz
        vg_ref[4:5, :] += col_sum(cot * n3)
        vg_ref[5:6, :] += col_sum(cot)
        vg_ref[16:17, :] += col_sum(dz)
        dh = dr3
        for j in range(4):
            da = (nt(dz, w2_block(j)) * f_ref[:, j * D : (j + 1) * D]).astype(BF)
            da_ref[rows, j * D : (j + 1) * D] = da
            vg_ref[12 + j : 13 + j, :] += col_sum(da)
            dh = dh + nt(da, w1_block(j))
        vg_ref[2:3, :] += col_sum(dh * n2)
        vg_ref[3:4, :] += col_sum(dh)
        moves.need(r2_ref)
        dr2 = norm_back(dh, n2, r2_ref[rows, 0:1], vec_row(vec_ref, 2))
        dr_ref[rows, :] = dr2
        moves.done(dr_ref, rows)
        vg_ref[11:12, :] += col_sum(dr2.astype(BF))
    moves.done(vg_ref)
    core = core_ref[0]
    ht_ref[...] = jnp.swapaxes(h_ref[...].T.reshape(4, 2, 64, LEN), 0, 1).reshape(2, ROWS, LEN)
    dz = dz_ref[...]
    turned = jnp.concatenate([ht_ref[1 - core], ht_ref[core]], axis=0)
    for j in range(4):
        starts = [pl.multiple_of(j * D + h * ROWS, ROWS) for h in (1 - core, core)]
        cols = jnp.concatenate([u_ref[:, pl.ds(start, ROWS)] for start in starts], axis=1)
        dw1 = nn(turned, da_ref[:, j * D : (j + 1) * D]).astype(BF)
        dw2 = tn(cols, dz).astype(BF)
        for place, ref in enumerate((other_ref, mine_ref)):
            half = slice(place * ROWS, place * ROWS + ROWS)
            ref[:, 64 * j : 64 * j + 64, :] = dw1[half].reshape(4, 64, D)
            ref[j, ROWS:, :] = dw2[half]
            moves.done(ref, j, pl.ds(ROWS, ROWS))
    for j in range(4):
        for ref in (other_ref, mine_ref):
            moves.done(ref, j, pl.ds(0, ROWS))


def cross_backward_kernel(
    moves, core_ref, parts, dr2_ref, o_ref, q_ref, k_ref, v_ref, qal_ref, ka_ref, mt_ref, n1_ref, vec_ref, vf_ref, r1_ref,
    mine_ref, other_ref, dr1_ref, dk_ref, dv_ref,
    g_ref, do_ref, del_ref, dq_ref, p_ref, s_ref, h_ref, w_ref, vg_ref, kt_ref, dqt_ref,
):
    core = core_ref[0]
    fetch(moves, core_ref, parts, w_ref)
    moves.need(dr2_ref)
    for qb in range(TALLS):
        rows = pl.ds(qb * TALL, TALL)
        g_ref[rows, :] = dr2_ref[rows, :].astype(BF)
    moves.need(w_ref, o_ref)
    mix_gradient(g_ref, square(w_ref, 3), o_ref, do_ref, del_ref)
    put_square_tn(mine_ref, other_ref, core, 3, o_ref, g_ref[...])
    moves.need(q_ref, k_ref, v_ref, qal_ref, ka_ref)
    attend_backward(
        q_ref, k_ref, v_ref, do_ref, qal_ref, del_ref, ka_ref, dq_ref, dk_ref, dv_ref, p_ref, s_ref, kt_ref, dqt_ref, False
    )
    moves.done(dk_ref)
    moves.done(dv_ref)
    moves.need(n1_ref, vec_ref, vf_ref, r1_ref, mt_ref)
    vg_ref[...] = vf_ref[...]
    for qb in range(TALLS):
        rows = pl.ds(qb * TALL, TALL)
        dq = dq_ref[rows, :]
        vg_ref[9:10, :] += col_sum(dq)
        vg_ref[10:11, :] += col_sum(dv_ref[rows, :])
        dh = dr2_ref[rows, :] + nt(dq, square(w_ref, 0))
        n1 = n1_ref[rows, :]
        vg_ref[0:1, :] += col_sum(dh * n1)
        vg_ref[1:2, :] += col_sum(dh)
        dr1 = norm_back(dh, n1, r1_ref[rows, 0:1], vec_row(vec_ref, 0))
        dr1_ref[rows, :] = dr1
        moves.done(dr1_ref, rows)
        vg_ref[8:9, :] += col_sum(dr1.astype(BF))
        h_ref[rows, :] = (n1 * vec_row(vec_ref, 0) + vec_row(vec_ref, 1)).astype(BF)
    blank = jnp.zeros((12, D), F32)
    for ref, half in ((mine_ref, core), (other_ref, 1 - core)):
        for xy in range(4):
            low, high = vg_ref[8 * xy : 8 * xy + 4, :], vg_ref[8 * xy + 4 : 8 * xy + 8, :]
            rows = jnp.where(half == 0, low, high)
            ref[xy, ROWS:, :] = jnp.concatenate([rows, blank], axis=0).astype(BF)
        moves.done(ref, 3)
    put_square(mine_ref, other_ref, core, 1, mt_ref, dk_ref[...])
    put_square(mine_ref, other_ref, core, 2, mt_ref, dv_ref[...])
    for ref in (mine_ref, other_ref):
        moves.done(ref, 1)
        moves.done(ref, 2)
    put_square_tn(mine_ref, other_ref, core, 0, h_ref, dq_ref[...])
    for ref in (mine_ref, other_ref):
        moves.done(ref, 0)


EARLY = pl.ds(0, EARLY_PAIRS * LANES)
LATE = pl.ds(EARLY_PAIRS * LANES, (PAIRS - EARLY_PAIRS) * LANES)
EVERY = slice(None)


def self_backward_start_kernel(
    moves, core_ref, parts, dr1_ref, o_ref, q_ref, k_ref, v_ref, qal_ref, ka_ref,
    do_ref, del_ref, dq_ref, dk_ref, dv_ref, so_ref,
    g_ref, p_ref, s_ref, w_ref, kt_ref, dqt_ref,
):
    core = core_ref[0]
    fetch(moves, core_ref, parts, w_ref, FIRST_ROWS)
    moves.need(dr1_ref)
    for qb in range(TALLS):
        rows = pl.ds(qb * TALL, TALL)
        g_ref[rows, :] = dr1_ref[rows, :].astype(BF)
    moves.need(w_ref, o_ref)
    mix_gradient(g_ref, square(w_ref, 3), o_ref, do_ref, del_ref)
    moves.done(do_ref, EVERY, LATE)
    moves.done(del_ref)
    halves = [o_ref[:, pl.ds(pl.multiple_of(h * ROWS, ROWS), ROWS)] for h in (core, 1 - core)]
    so_ref[...] = tn(jnp.concatenate(halves, axis=1), g_ref[...]).astype(BF).reshape(2, ROWS, D)
    moves.done(so_ref)
    moves.need(q_ref, k_ref, v_ref, qal_ref, ka_ref)
    attend_backward(
        q_ref, k_ref, v_ref, do_ref, qal_ref, del_ref, ka_ref, dq_ref, dk_ref, dv_ref, p_ref, s_ref, kt_ref, dqt_ref, True,
        (0, EARLY_PAIRS),
    )
    for ref in (dq_ref, dk_ref, dv_ref):
        moves.done(ref, EVERY, EARLY)


def self_backward_end_kernel(
    moves, core_ref, q_ref, k_ref, v_ref, do_ref, qal_ref, del_ref, ka_ref, dqe_ref, dke_ref, dve_ref, xt_ref, so_ref,
    mine_ref, other_ref, dq_ref, dk_ref, dv_ref,
    p_ref, s_ref, late_ref, kt_ref, dqt_ref,
):
    core, chip = core_ref[0], core_ref[1]
    moves.need(q_ref, k_ref, v_ref, do_ref, qal_ref, del_ref, ka_ref)
    attend_backward(
        q_ref, k_ref, v_ref, do_ref, qal_ref, del_ref, ka_ref, dq_ref, dk_ref, dv_ref, p_ref, s_ref, kt_ref, dqt_ref, True,
        (EARLY_PAIRS, PAIRS),
    )
    for ref, source in ((dq_ref, dqe_ref), (dk_ref, dke_ref), (dv_ref, dve_ref)):
        moves.need(source)
        ref[:, EARLY] = source[:, EARLY]
        moves.done(ref)
    moves.need(xt_ref, so_ref)
    mine_ref[3 ^ chip, :ROWS, :] = so_ref[0]
    other_ref[3 ^ chip, :ROWS, :] = so_ref[1]
    late_ref[0:1, :] = col_sum(dq_ref[...])
    late_ref[1:2, :] = col_sum(dv_ref[...])
    for ref, half in ((mine_ref, core), (other_ref, 1 - core)):
        for xy in range(4):
            place = pl.multiple_of((2 * (xy % 2) + half) * LANES, LANES)
            piece = late_ref[xy // 2 : xy // 2 + 1, pl.ds(place, LANES)]
            after = lax.broadcasted_iota(jnp.int32, (16, LANES), 0) >= 4
            ref[xy ^ chip, ROWS:, :] = jnp.zeros((16, D), BF)
            ref[xy ^ chip, ROWS:, :LANES] = jnp.where(after, piece, 0.0).astype(BF)
        moves.done(ref, 3 ^ chip)
    for matrix, source in ((0, dq_ref), (1, dk_ref), (2, dv_ref)):
        put_square(mine_ref, other_ref, core, matrix, xt_ref, source[...], chip)
        moves.done(mine_ref, matrix ^ chip)
        moves.done(other_ref, matrix ^ chip)


def input_grads_kernel(
    moves, core_ref, parts, parts2, dr1_ref, dqs_ref, dks_ref, dvs_ref, dkc_ref, dvc_ref,
    ig_ref, mg_ref,
    w_ref, wc_ref,
):
    fetch(moves, core_ref, parts, w_ref, FIRST_ROWS)
    fetch(moves, core_ref, parts2, wc_ref)
    moves.need(w_ref, dr1_ref, dqs_ref, dks_ref, dvs_ref)
    for qb in range(TALLS):
        rows = pl.ds(qb * TALL, TALL)
        total = dr1_ref[rows, :] + nt(dqs_ref[rows, :], square(w_ref, 0))
        total = total + nt(dks_ref[rows, :], square(w_ref, 1))
        ig_ref[rows, :] = (total + nt(dvs_ref[rows, :], square(w_ref, 2))).astype(BF)
        moves.done(ig_ref, rows)
    moves.need(wc_ref, dkc_ref, dvc_ref)
    for qb in range(TALLS):
        rows = pl.ds(qb * TALL, TALL)
        total = nt(dkc_ref[rows, :], square(wc_ref, 1))
        mg_ref[rows, :] = (total + nt(dvc_ref[rows, :], square(wc_ref, 2))).astype(BF)
        moves.done(mg_ref, rows)


def call(kernel, outs, scratch, flops, core, parts, args, views=None):
    views = views or {}
    sds = [jax.ShapeDtypeStruct(shape, dtype) for shape, dtype in outs]
    arrays = [block for group in parts for block in group]
    moved = sum(a.size * a.dtype.itemsize for a in arrays + list(args))
    spaces = [pltpu.SMEM] + [pl.ANY] * (len(arrays) + len(args))
    memory = [pltpu.VMEM(a.shape, a.dtype) for a in args]
    memory += [pltpu.VMEM(shape, dtype) for shape, dtype in list(outs) + scratch]
    memory += [pltpu.SemaphoreType.DMA((64,))]

    def body(core_ref, *refs):
        groups = [refs[6 * i : 6 * i + 6] for i in range(len(parts))]
        refs = refs[6 * len(parts) :]
        given, refs = refs[: len(args)], refs[len(args) :]
        results, refs = refs[: len(outs)], refs[len(outs) :]
        held, refs = refs[: len(args)], refs[len(args) :]
        moves = Moves(refs[-1])
        for i, (source, target) in enumerate(zip(given, held)):
            if i in views:
                moves.bring(source.at[views[i]], target.at[views[i]], target)
            else:
                moves.bring(source, target, target)
        for place, result in zip(refs, results):
            moves.pair(place, result)
        kernel(moves, core_ref, *groups, *held, *refs[:-1])
        moves.finish()

    return pl.pallas_call(
        body,
        out_shape=sds,
        in_specs=[pl.BlockSpec(memory_space=space) for space in spaces],
        out_specs=[pl.BlockSpec(memory_space=pl.ANY)] * len(outs),
        scratch_shapes=memory,
        compiler_params=pltpu.CompilerParams(vmem_limit_bytes=VMEM_BYTES),
        cost_estimate=pl.CostEstimate(flops=flops, bytes_accessed=moved, transcendentals=0),
    )(core, *arrays, *args)


TOK = (LEN, D)
STAT = (LEN, LANES)
OCT = (8, ROWS, D)
unit = 2 * LEN * D * D
FORWARD_OUTS = [(TOK, BF)] * 4 + [(STAT, BF), (TOK, F32), (STAT, F32)]
HALVES = ((4, ROWS + 16, D), BF)
TOKB = (TOK, BF)
PROBS = ((2, LEN, LEN), BF)
TURN = ((D, LEN), BF)
TURN32 = ((D, LEN), F32)
FORWARD_SCRATCH = [(OCT, BF), TURN, ((LANES, LEN), BF)]


def self_forward(core, w, *args):
    return call(self_forward_kernel, FORWARD_OUTS, FORWARD_SCRATCH, 20 * unit, core, [w], args)


def cross_forward(core, w, *args):
    return call(cross_forward_kernel, FORWARD_OUTS, FORWARD_SCRATCH, 25 * unit, core, [w], args)


def ffn(core, w, *args):
    outs = [TOKB, ((4, 2 * ROWS, D), BF), ((4, 2 * ROWS, D), BF), (TOK, F32), ((32, D), F32)]
    scratch = [(OCT, BF), (OCT, BF), ((LEN, FF), BF), ((LEN, FF), BF), TOKB, TOKB]
    scratch += [((TALL, FF), F32), ((2, ROWS, LEN), BF)]
    return call(ffn_kernel, outs, scratch, 26 * unit, core, [w], args)


def cross_backward(core, w, *args):
    outs = [HALVES, HALVES, (TOK, F32), TOKB, TOKB]
    scratch = [TOKB, TOKB, (STAT, BF), TOKB, PROBS, PROBS, TOKB, (OCT, BF), ((32, D), F32), TURN, TURN32]
    return call(cross_backward_kernel, outs, scratch, 50 * unit, core, [w], args)


def self_backward_start(core, w, *args):
    outs = [TOKB, (STAT, BF), TOKB, TOKB, TOKB, ((2, ROWS, D), BF)]
    scratch = [TOKB, PROBS, PROBS, (OCT, BF), TURN, TURN32]
    return call(self_backward_start_kernel, outs, scratch, 25 * unit, core, [w], args)


def self_backward_end(core, *args):
    outs = [HALVES, HALVES, TOKB, TOKB, TOKB]
    scratch = [PROBS, PROBS, ((8, D), F32), TURN, TURN32]
    views = {i: (EVERY, LATE) for i in (0, 1, 2, 3)} | {i: (EVERY, EARLY) for i in (7, 8, 9)}
    return call(self_backward_end_kernel, outs, scratch, 12 * unit, core, [], args, views)


def input_grads(core, ws, wc, *args):
    scratch = [(OCT, BF), (OCT, BF)]
    return call(input_grads_kernel, [TOKB, TOKB], scratch, 6 * unit, core, [ws, wc], args)


SQUARES = 8 * D * D
VEC_ROWS = 17
VEC_LEN = VEC_ROWS * D


def groups_xy():
    return [[z * 8 + c * 2 + core for c in range(4)] for z in range(4) for core in range(2)]


def groups_z():
    return [[z * 8 + p for z in range(4)] for p in range(8)]


def swap(x, bit):
    return lax.ppermute(x, "dp", [(i, i ^ bit) for i in range(32)])


def turn_w1(chunk, here, out_first):
    if out_first:
        alt = chunk.reshape(64, 4, D).transpose(1, 0, 2).reshape(ROWS, D)
    else:
        alt = chunk.reshape(4, 64, D).transpose(1, 0, 2).reshape(ROWS, D)
    return jnp.where(here, alt, chunk)


def along_z(x, moves):
    return lax.ppermute(x, "dp", [(8 * a + p, 8 * b + p) for a, b in moves for p in range(8)])


def gather_blocks(params, index, others):
    low = params.astype(BF)
    share = low.shape[0]
    shift = share - ROWS * D
    z = index // 8
    prev = lax.ppermute(low[share - VEC_LEN :], "dp", [(i, (i + 1) % 32) for i in range(32)])
    flat = lax.dynamic_slice(jnp.concatenate([prev, low]), (VEC_LEN - shift * index,), (ROWS * D,))
    chunk = turn_w1(flat.reshape(ROWS, D), z == 2, True)
    vec = jnp.pad(prev.reshape(VEC_ROWS, D), ((0, 15), (0, 0)))
    mine = jnp.concatenate([chunk, vec])
    first = along_z(mine, ((0, 2), (1, 0), (2, 3), (3, 1)))
    first, others = lax.optimization_barrier((first, others))
    second = along_z(jnp.where(z == 2, first, mine), ((0, 1), (1, 2), (2, 3)))
    third = along_z(jnp.where(z == 1, first, mine)[:ROWS], ((3, 2), (2, 1), (1, 0)))
    second, third = lax.optimization_barrier((second, third))
    block0 = jnp.where(z == 0, mine, jnp.where(z == 2, first, second))
    fourth = along_z(jnp.where(z == 1, third, second[:ROWS]), ((1, 0), (2, 3)))
    pair0, near0 = to_sides(block0)
    near0, fourth = lax.optimization_barrier((near0, fourth))
    first, second = first[:ROWS], second[:ROWS]

    def pick(*blocks):
        return jnp.where(z < 2, jnp.where(z == 0, *blocks[:2]), jnp.where(z == 2, *blocks[2:]))

    block1 = pick(first, chunk, second, fourth)
    block2 = pick(fourth, third, chunk, first)
    block3 = pick(third, first, third, chunk)
    across0 = to_corners(near0)
    pair1, near1 = to_sides(block1)
    across0, near1 = lax.optimization_barrier((across0, near1))
    part0 = finish_block(pair0, near0, across0)
    across1 = to_corners(near1)
    pair2, near2 = to_sides(jnp.concatenate([block2, block3]))
    core, chip = index % 2, index % 8 // 2
    rows = [part0[0], part0[1], part0[2], part0[2], part0[3], part0[3], part0[4], part0[5]]
    starts = [ROWS, ROWS, ROWS, 2 * ROWS + 32, ROWS, 2 * ROWS + 32, ROWS, ROWS]
    rows = jnp.stack([lax.slice_in_dim(a, s, s + 32) for a, s in zip(rows, starts)])
    place = jnp.where(chip == 0, core, jnp.where(chip == 3, 6 + core, jnp.where(chip == 1 + core, 2 + core, 5 - core)))
    source = lax.dynamic_index_in_dim(rows, place, 0, keepdims=False)
    return part0, (pair1, near1, across1), (pair2, near2), source.astype(F32), others


def sides(first, second):
    return [(i, i ^ (first if i % 2 == 0 else second)) for i in range(32)]


def to_sides(block):
    pair = (block, swap(block, 1))
    return pair, lax.ppermute(jnp.concatenate(pair), "dp", sides(2, 4))


def to_corners(near):
    return lax.ppermute(near[: near.shape[0] // 2], "dp", sides(4, 2))


def finish_block(pair, near, across):
    return [*pair, near, swap(near, 1), across, swap(across, 1)]


def gather_plain(params, index, others):
    flat = lax.all_gather(params.astype(BF), "dp", axis=0, tiled=True)
    end = SQUARES + D * FF
    w1 = flat[SQUARES:end].reshape(8, 64, 4, D).transpose(0, 2, 1, 3).reshape(8, ROWS, D)
    w2 = flat[end : end + D * FF].reshape(8, ROWS, D)
    vec = flat[end + D * FF :].reshape(VEC_ROWS, D).astype(F32)
    mats = flat[:SQUARES].reshape(2, 4, 2, ROWS, D)

    core = index % 2

    def parts(pairs, rows):
        pairs = jnp.pad(pairs, ((0, 0), (0, 0), (0, rows - pairs.shape[2]), (0, 0)))
        own = lax.dynamic_index_in_dim(pairs, core, 1, keepdims=False)
        other = lax.dynamic_index_in_dim(pairs, 1 - core, 1, keepdims=False)
        one, two = jnp.concatenate([own, other], axis=1), jnp.concatenate([other, own], axis=1)
        near = lax.dynamic_index_in_dim(one, 1 + core, 0, keepdims=False)
        far = lax.dynamic_index_in_dim(two, 2 - core, 0, keepdims=False)
        return [own[0], other[0], near, far, own[3], other[3]]

    vec = jnp.pad(vec, ((0, 15), (0, 0)))
    wide = jnp.concatenate([w1.reshape(4, 2, ROWS, D), w2.reshape(4, 2, ROWS, D)], axis=2)
    return parts(mats[0], FIRST_ROWS), parts(mats[1], ROWS), parts(wide, 2 * ROWS), vec, others


def plane_sum(mine, other):
    pair = (mine.astype(F32) + swap(other, 1).astype(F32)).astype(BF)
    parts = lax.all_to_all(pair, "dp", 0, 0, tiled=True, axis_index_groups=groups_xy())
    return jnp.sum(parts.astype(F32), axis=0).astype(BF)


def add(a, b):
    return (a.astype(F32) + b.astype(F32)).astype(BF)


def first_round(part_c, part_f, z):
    extra = part_c[ROWS:]
    part_1 = jnp.concatenate([part_f[:ROWS], extra])
    part_2 = jnp.concatenate([part_f[ROWS:], extra])
    return part_c, part_1, part_2, along_z(jnp.where(z == 0, part_1, part_c), ((0, 1), (3, 2)))


def finish_blocks(mine, other, blocks, grads, index):
    z = index // 8
    got = swap(other, 1)
    pairs = [(mine[j].astype(F32) + got[j].astype(F32)).astype(BF) for j in range(4)]
    part_c, part_1, part_2, early = blocks
    part = pairs[0].astype(F32) + swap(pairs[1], 2).astype(F32) + swap(pairs[2], 4).astype(F32)
    part = part + swap(pairs[3], 6).astype(F32)
    part, grads = lax.optimization_barrier((part, grads))
    part = (part + jnp.pad(part_c[ROWS:].astype(F32), ((ROWS, 0), (0, 0)))).astype(BF)
    left = jnp.where(z == 2, add(part_c, early), part)
    right = jnp.where(z == 1, add(part_1, early), part_2)
    got_left = along_z(left, ((1, 0), (2, 1), (3, 2)))
    got_right = along_z(right, ((0, 1), (1, 2), (2, 3)))
    last = jnp.where(z < 2, jnp.where(z == 0, part_c, add(part_2, got_right)), jnp.where(z == 2, add(part, got_left), part_1))
    got = along_z(last, ((2, 0), (0, 1), (3, 2), (1, 3)))
    own = jnp.where(z < 2, jnp.where(z == 0, part, part_c), jnp.where(z == 2, part_1, part_2)).astype(F32)
    own = own + jnp.where(z < 2, got_left, got_right).astype(F32) + got.astype(F32)
    chunk = own[:ROWS]
    flat = turn_w1(chunk, z == 2, False).reshape(ROWS * D)
    after = lax.ppermute(flat[:VEC_LEN], "dp", [(i + 1, i) for i in range(31)])
    pieces = jnp.concatenate(
        [
            lax.dynamic_index_in_dim(own[ROWS : ROWS + 4], z, 0, keepdims=False).reshape(4, LANES),
            own[ROWS + 4 : ROWS + 5, :LANES],
            jnp.full((3, LANES), jnp.sum(chunk * chunk)),
        ]
    )
    pieces = jnp.broadcast_to(pieces[None], (32, 8, LANES))
    pieces = lax.all_to_all(pieces, "dp", 0, 0, tiled=True)
    vec = pieces[:, :4].reshape(4, 8, D).transpose(1, 0, 2).reshape(32, D)
    late = jnp.pad(pieces[:8, 4].reshape(2, D), ((6, 9), (0, 0)))
    vec = (vec[:VEC_ROWS] + late).reshape(VEC_LEN)
    square = jnp.sum(pieces[:, 5, 0]) + jnp.sum(vec * vec)
    after = jnp.where(index == 31, vec, after)
    share = lax.dynamic_slice(jnp.concatenate([flat, after]), (272 * index,), (ROWS * D + 272,))
    return share, vec, square, grads


def share_plain(pairs, index, share_len):
    def joined(mine, other):
        low = jnp.where(index % 2 == 0, mine, other).astype(F32)
        return jnp.stack([low, jnp.where(index % 2 == 0, other, mine).astype(F32)], axis=1)

    self_g, cross_g, ffn_g = (joined(*pair) for pair in pairs)
    dw1 = ffn_g[:, :, :ROWS].reshape(8, 4, 64, D).transpose(0, 2, 1, 3)
    vec = cross_g[:, :, ROWS : ROWS + 4].reshape(32, D)
    late = jnp.pad(self_g[:, :, ROWS + 4, :LANES].reshape(2, D), ((6, 9), (0, 0)))
    vec = vec[:VEC_ROWS] + late
    parts = (self_g[:, :, :ROWS], cross_g[:, :, :ROWS], dw1, ffn_g[:, :, ROWS:], vec)
    flat = lax.psum(jnp.concatenate([g.reshape(-1) for g in parts]), "dp")
    share = lax.dynamic_slice(flat, (index * share_len,), (share_len,))
    return share, flat[-VEC_LEN:], jnp.sum(flat * flat)


def shards(count, targets, memory, target_ids, memory_ids, cotangent, params, first_moment, second_moment):
    index = lax.axis_index("dp")
    blocked = count == 32
    place = jnp.where(blocked, index % 8 // 2, 0)
    core = jnp.stack([index % 2, place]).astype(jnp.int32)
    lane = jnp.arange(LANES)[None, :] - MASK_LANE
    live = (lane >= 0) & (lane < 8)
    same_t = lane == target_ids[:, None]
    same_m = lane == memory_ids[:, None]
    others = (
        jnp.where(live & ~same_t, masked_value, 0.0).astype(BF),
        jnp.where(same_t, 1.0, 0.0).astype(BF),
        jnp.where(same_m, 1.0, 0.0).astype(BF),
        memory.T,
        targets.T,
        core,
    )
    gather = gather_blocks if blocked else gather_plain
    ws, wc, wide, vec, others = gather(params, index, others)
    qa, ka_self, ka_cross, memory_turn, targets_turn, core = others
    qs, ks, vs, os, qal_s, n1, r1 = self_forward(core, ws, targets, vec, qa, ka_self)
    if blocked:
        wc, wide, n1 = lax.optimization_barrier((wc, wide, n1))
        wc = finish_block(*wc)
        across = to_corners(wide[1])
    qc, kc, vc, oc, qal_c, n2, r2 = cross_forward(core, wc, n1, vec, memory, qa, ka_cross)
    if blocked:
        across, n2 = lax.optimization_barrier((across, n2))
        wide = finish_block(*wide, across)
    out, mine_f, other_f, dr2, vg_f = ffn(core, wide, n2, vec, cotangent, r2)
    mine_c, other_c, dr1, dkc, dvc = cross_backward(
        core, wc, dr2, oc, qc, kc, vc, qal_c, ka_cross, memory_turn, n1, vec, vg_f, r1
    )
    if blocked:
        part_f = plane_sum(mine_f, other_f)
        part_f, mine_c, other_c, dr1 = lax.optimization_barrier((part_f, mine_c, other_c, dr1))
        part_c = plane_sum(mine_c, other_c)
    early = self_backward_start(core, ws, dr1, os, qs, ks, vs, qal_s, ka_self)
    if blocked:
        part_c, early = lax.optimization_barrier((part_c, early))
        blocks = first_round(part_c, part_f, index // 8)
    mine_s, other_s, dqs, dks, dvs = self_backward_end(
        core, qs, ks, vs, early[0], qal_s, early[1], ka_self, *early[2:5], targets_turn, early[5]
    )
    input_grad, memory_grad = input_grads(core, ws, wc, dr1, dqs, dks, dvs, dkc, dvc)
    if blocked:
        blocks, mine_s, other_s = lax.optimization_barrier((blocks, mine_s, other_s))
        grads = (input_grad, memory_grad)
        grad, vec_total, square, grads = finish_blocks(mine_s, other_s, blocks, grads, index)
        input_grad, memory_grad = grads
    else:
        pairs = ((mine_s, other_s), (mine_c, other_c), (mine_f, other_f))
        grad, vec_total, square = share_plain(pairs, index, params.shape[0])
    norm_value = jnp.sqrt(square)
    factor = jnp.minimum(1.0, clip_limit / (norm_value + 1e-06))
    clipped = grad * factor
    new_first = beta_one * first_moment + (1.0 - beta_one) * clipped
    new_second = beta_two * second_moment + (1.0 - beta_two) * clipped * clipped
    first_hat = new_first / (1.0 - beta_one**STEP)
    second_hat = new_second / (1.0 - beta_two**STEP)
    new_params = params - step_rate * (
        first_hat / (jnp.sqrt(second_hat) + adam_eps) + weight_decay * params
    )
    return (
        out,
        input_grad,
        memory_grad,
        norm_value,
        grad,
        vec_total,
        new_params,
        new_first,
        new_second,
        new_params.astype(BF),
    )


def solution(mesh):
    rows, flat = P("dp", None), P("dp")
    return jax.shard_map(
        functools.partial(shards, mesh.shape["dp"]),
        mesh=mesh,
        in_specs=(rows, rows, flat, flat, rows, flat, flat, flat),
        out_specs=(rows, rows, rows, P(), flat, P(), flat, flat, flat, flat),
        check_vma=False,
    )
```

```python
import functools
import jax
import jax.numpy as jnp
from jax import lax
from jax.experimental import pallas as pl
from jax.experimental.pallas import tpu as pltpu
from jax.sharding import PartitionSpec as P

D = 512
FF = 2048
HEADS = 8
LEN = 1024
STEP = 10
ROWS = 256
BLOCKS = LEN // ROWS
TALL = 512
TALLS = LEN // TALL
LANES = 128
PAIRS = D // LANES
MASK_LANE = 32
EARLY_PAIRS = 3
FIRST_ROWS = ROWS + 32

eps_norm = 1e-05
beta_one = 0.9
beta_two = 0.999
adam_eps = 1e-08
step_rate = 0.05
weight_decay = 0.01
clip_limit = 1.0
masked_value = -1e30
log2_e = 1.4426950408889634
query_scale = 0.125 * log2_e
key_scale = 1.0 / log2_e
safe_least, safe_most = 2.0**-40, 2.0**40

BF = jnp.bfloat16
F32 = jnp.float32
VMEM_BYTES = 60 * 1024 * 1024


def nn(a, b):
    return jnp.dot(a, b, preferred_element_type=F32)


def nt(a, b):
    return lax.dot_general(a, b, (((1,), (1,)), ((), ())), preferred_element_type=F32)


def tn(a, b):
    return lax.dot_general(a, b, (((0,), (0,)), ((), ())), preferred_element_type=F32)


def layer_norm(resid):
    center = resid - jnp.mean(resid, axis=1, keepdims=True)
    inv_std = lax.rsqrt(jnp.mean(center * center, axis=1, keepdims=True) + eps_norm)
    return center * inv_std, inv_std


def norm_back(grad, normed, inv_std, gain):
    scaled = grad * gain
    return inv_std * (
        scaled
        - jnp.mean(scaled, axis=1, keepdims=True)
        - normed * jnp.mean(scaled * normed, axis=1, keepdims=True)
    )


def half_row(parity):
    lane = lax.broadcasted_iota(jnp.int32, (1, LANES), 1)
    inside = (lane // 64) == parity
    return jnp.where(inside, 1.0, 0.0).astype(BF)


def lane_row(first, count):
    lane = lax.broadcasted_iota(jnp.int32, (1, LANES), 1)
    inside = (lane >= first) & (lane < first + count)
    return jnp.where(inside, 1.0, 0.0).astype(BF)


def causal_bias(transposed):
    row = lax.broadcasted_iota(jnp.int32, (ROWS, ROWS), 0)
    col = lax.broadcasted_iota(jnp.int32, (ROWS, ROWS), 1)
    ok = (row <= col) if transposed else (col <= row)
    return jnp.where(ok, 0.0, masked_value)


def attend_forward(moves, q_ref, k_ref, v_ref, qa_ref, ka_ref, o_ref, qal_ref, kt_ref, kat_ref, causal):
    size, depth = (ROWS, 2) if causal else (2 * ROWS, 1)
    low = lax.broadcasted_iota(jnp.int32, (size, LANES), 1) < 64
    bias = causal_bias(False) if causal else None
    kt_ref[...] = k_ref[...].T
    kat_ref[...] = ka_ref[...].T

    def score(block, head):
        rows = pl.ds(block * size, size)
        lanes = pl.ds(head // 2 * LANES, LANES)
        keys = (block + 1) * size if causal else LEN
        q_cat = jnp.concatenate([q_ref[rows, lanes] * half_row(head % 2), qa_ref[rows, :]], axis=1)
        k_cat = jnp.concatenate([kt_ref[lanes, :keys], kat_ref[:, :keys]], axis=0)
        scores = nn(q_cat, k_cat)
        if causal:
            diag = scores[:, keys - size :] + bias
            scores = jnp.concatenate([scores[:, : keys - size], diag], axis=1) if block else diag
        return scores

    def parts_of(lse, head, lse_parts):
        place = lax.broadcasted_iota(jnp.int32, lse.shape, 1)
        first = lse.astype(BF).astype(F32)
        rest = lse - first
        second = rest.astype(BF).astype(F32)
        for i, part in enumerate((first, second, rest - second)):
            lse_parts = jnp.where(place == head * 3 + i, part, lse_parts)
        return lse_parts

    def finish(head, scores, lse_parts, least, most):
        half = half_row(head % 2)
        probs = jnp.exp2(scores).astype(BF)
        values = v_ref[: scores.shape[1], pl.ds(head // 2 * LANES, LANES)]
        mixed = nn(probs, values * half + (1.0 - half).astype(BF))
        turned = pltpu.roll(mixed, 64, 1)
        total = jnp.where(low, turned, mixed) if head % 2 == 0 else jnp.where(low, mixed, turned)
        lse_parts = parts_of(-jnp.log2(total), head, lse_parts)
        return mixed / turned, lse_parts, jnp.minimum(least, total), jnp.maximum(most, total)

    least = jnp.full((size, LANES), 1.0, F32)
    most = least
    for block in range(LEN // size):
        rows = pl.ds(block * size, size)
        waiting, outs = [], []
        lse_parts = jnp.zeros((size, LANES), F32)
        for step in range(HEADS + depth):
            if step < HEADS:
                waiting.append(score(block, step))
            if step >= depth:
                head = step - depth
                out, lse_parts, least, most = finish(head, waiting.pop(0), lse_parts, least, most)
                outs.append(out)
                if head % 2:
                    lanes = pl.ds(head // 2 * LANES, LANES)
                    o_ref[rows, lanes] = jnp.where(low, outs[-2], outs[-1]).astype(BF)
        qal_ref[rows, :] = (qa_ref[rows, :].astype(F32) + lse_parts).astype(BF)
    safe = (jnp.min(least) > safe_least) & (jnp.max(most) < safe_most)

    @pl.when(jnp.logical_not(safe))
    def _():
        for block in range(BLOCKS):
            rows = pl.ds(block * ROWS, ROWS)
            keys = (block + 1) * ROWS if causal else LEN
            qa = qa_ref[rows, :]

            def one_pair(pair, lse_parts):
                lanes = pl.ds(pl.multiple_of(pair * LANES, LANES), LANES)
                k_cat = jnp.concatenate([kt_ref[lanes, :keys], kat_ref[:, :keys]], axis=0)
                outs = []
                for parity in range(2):
                    half = half_row(parity)
                    scores = nn(jnp.concatenate([q_ref[rows, lanes] * half, qa], axis=1), k_cat)
                    if causal:
                        diag = scores[:, keys - ROWS :] + bias
                        scores = (
                            jnp.concatenate([scores[:, : keys - ROWS], diag], axis=1) if block else diag
                        )
                    top = jnp.max(scores, axis=1, keepdims=True)
                    probs = jnp.exp2(scores - top).astype(BF)
                    mixed = nn(probs, v_ref[:keys, lanes] * half + (1.0 - half).astype(BF))
                    turned = pltpu.roll(mixed, 64, 1)
                    outs.append(mixed / turned)
                    lse = -(top + jnp.log2(turned if parity == 0 else mixed))
                    lse_parts = parts_of(lse, pair * 2 + parity, lse_parts)
                lower = lax.broadcasted_iota(jnp.int32, (ROWS, LANES), 1) < 64
                o_ref[rows, lanes] = jnp.where(lower, outs[0], outs[1]).astype(BF)
                return lse_parts

            lse_parts = lax.fori_loop(0, PAIRS, one_pair, jnp.zeros((ROWS, LANES), F32))
            qal_ref[rows, :] = (qa.astype(F32) + lse_parts).astype(BF)

    moves.done(o_ref)
    moves.done(qal_ref)


def attend_backward(
    q_ref, k_ref, v_ref, do_ref, qal_ref, del_ref, ka_ref, dq_ref, dk_ref, dv_ref, p_ref, s_ref, kt_ref, dqt_ref,
    causal, span=(0, PAIRS),
):
    bias = causal_bias(True) if causal else None
    cols = pl.ds(span[0] * LANES, (span[1] - span[0]) * LANES)
    kt_ref[cols, :] = k_ref[:, cols].T

    def score(head, block):
        lanes = pl.ds(head // 2 * LANES, LANES)
        half = half_row(head % 2)
        rows = pl.ds(block * ROWS, ROWS)
        keys = (block + 1) * ROWS if causal else LEN
        marks = ka_ref[:keys, :] + lane_row(head * 3, 3)
        k_cat = jnp.concatenate([k_ref[:keys, lanes] * half, marks], axis=1)
        ones = jnp.broadcast_to(lane_row(head * 2, 2), (keys, LANES))
        v_cat = jnp.concatenate([v_ref[:keys, lanes] * half, ones], axis=1)
        q_cat = jnp.concatenate([q_ref[rows, lanes], qal_ref[rows, :]], axis=1)
        do_cat = jnp.concatenate([do_ref[rows, lanes], del_ref[rows, :]], axis=1)
        return nt(k_cat, q_cat), nt(v_cat, do_cat)

    def finish(head, block, scores, grads):
        rows = pl.ds(block * ROWS, ROWS)
        keys = scores.shape[0]
        if causal:
            diag = scores[keys - ROWS :] + bias
            scores = jnp.concatenate([scores[: keys - ROWS], diag], axis=0) if block else diag
        probs = jnp.exp2(scores)
        p_ref[head % 2, :keys, rows] = probs.astype(BF)
        inner = (probs * grads).astype(BF)
        s_ref[head % 2, :keys, rows] = inner
        own = pl.ds(head * 64, 64)
        dqt_ref[own, rows] = nn(kt_ref[own, :keys], inner)

    def pair_end(pair):
        lanes = pl.ds(pair * LANES, LANES)
        for kb in range(BLOCKS):
            rows = pl.ds(kb * ROWS, ROWS)
            first = kb * ROWS if causal else 0
            tail = pl.ds(first, LEN - first)
            do_pair = do_ref[tail, lanes]
            q_pair = q_ref[tail, lanes]
            dv = nn(p_ref[0, rows, tail], do_pair * half_row(0))
            dv = dv + nn(p_ref[1, rows, tail], do_pair * half_row(1))
            dv_ref[rows, lanes] = dv.astype(BF)
            dk = nn(s_ref[0, rows, tail], q_pair * half_row(0))
            dk = dk + nn(s_ref[1, rows, tail], q_pair * half_row(1))
            dk_ref[rows, lanes] = (dk * key_scale).astype(BF)

    steps = [(h, b) for h in range(2 * span[0], 2 * span[1]) for b in range(BLOCKS)]
    waiting = score(*steps[0])
    for place, (head, block) in enumerate(steps):
        current = waiting
        if place + 1 < len(steps):
            waiting = score(*steps[place + 1])
        finish(head, block, *current)
        if head % 2 and block == BLOCKS - 1:
            pair_end(head // 2)
    for block in range(BLOCKS):
        rows = pl.ds(block * ROWS, ROWS)
        dq_ref[rows, cols] = (dqt_ref[cols, rows] * 0.125).T.astype(BF)


def mix_gradient(g_ref, w_out, o_ref, do_ref, del_ref):
    lane = lax.broadcasted_iota(jnp.int32, (TALL, LANES), 1)
    even = lane % 2 == 0
    col = lax.broadcasted_iota(jnp.int32, (D, LANES), 0) // 64
    pick = jnp.where(lax.broadcasted_iota(jnp.int32, (D, LANES), 1) // 2 == col, -1.0, 0.0).astype(BF)
    for qb in range(TALLS):
        rows = pl.ds(qb * TALL, TALL)
        do = nt(g_ref[rows, :], w_out).astype(BF)
        do_ref[rows, :] = do
        prod = do.astype(F32) * o_ref[rows, :].astype(F32)
        high = prod.astype(BF)
        inner = nn(high, pick) + nn((prod - high.astype(F32)).astype(BF), pick)
        first = inner.astype(BF).astype(F32)
        del_ref[rows, :] = jnp.where(even, first, inner - first).astype(BF)


def vec_row(vec_ref, index):
    return vec_ref[index : index + 1, :]


class Moves:
    def __init__(self, sems):
        self.sems, self.used = sems, 0
        self.asked, self.inward, self.outward = {}, {}, []

    def copy(self, source, target):
        move = pltpu.make_async_copy(source, target, self.sems.at[self.used])
        self.used += 1
        move.start()
        return move

    def bring(self, source, target, key):
        self.asked.setdefault(id(key), []).append((source, target))

    def start(self, keys):
        for key in keys:
            for source, target in self.asked.pop(key, []):
                self.inward.setdefault(key, []).append(self.copy(source, target))

    def first(self, *refs):
        self.start([id(ref) for ref in refs])
        self.need(*refs)
        self.start(list(self.asked))

    def need(self, *refs):
        for ref in refs:
            for move in self.inward.pop(id(ref), []):
                move.wait()

    def pair(self, scratch, out):
        self.outs = getattr(self, "outs", {})
        self.outs[id(scratch)] = out

    def done(self, ref, *where):
        out = self.outs[id(ref)]
        if where:
            ref, out = ref.at[where], out.at[where]
        self.outward.append(self.copy(ref, out))

    def finish(self):
        for moves in self.inward.values():
            for move in moves:
                move.wait()
        for move in self.outward:
            move.wait()


def fetch(moves, core_ref, parts, w_ref, rows=ROWS, first=0):
    core, chip = core_ref[0], core_ref[1]
    near, far = chip ^ (1 + core), chip ^ (2 - core)
    own, other = core, 1 - core
    places = (
        (0, 0, chip, own),
        (1, 0, chip, other),
        (2, 0, near, own),
        (2, rows, near, other),
        (3, 0, far, other),
        (3, rows, far, own),
        (4, 0, chip ^ 3, own),
        (5, 0, chip ^ 3, other),
    )
    for part, start, place, half in places:
        source = parts[part].at[pl.ds(start + first, ROWS)]
        moves.bring(source, w_ref.at[2 * place + half], w_ref)


def square(w_ref, matrix):
    return w_ref[2 * matrix : 2 * matrix + 2].reshape(D, D)


def put_square(mine_ref, other_ref, core, matrix, turned_ref, grad, place=0):
    halves = [turned_ref[pl.ds(pl.multiple_of(h * ROWS, ROWS), ROWS), :] for h in (core, 1 - core)]
    both = nn(jnp.concatenate(halves, axis=0), grad).astype(BF)
    mine_ref[matrix ^ place, :ROWS, :] = both[:ROWS]
    other_ref[matrix ^ place, :ROWS, :] = both[ROWS:]


def put_square_tn(mine_ref, other_ref, core, matrix, left_ref, grad, place=0):
    halves = [left_ref[:, pl.ds(pl.multiple_of(h * ROWS, ROWS), ROWS)] for h in (core, 1 - core)]
    both = tn(jnp.concatenate(halves, axis=1), grad).astype(BF)
    mine_ref[matrix ^ place, :ROWS, :] = both[:ROWS]
    other_ref[matrix ^ place, :ROWS, :] = both[ROWS:]


def self_forward_kernel(
    moves, core_ref, parts, x_ref, vec_ref, qa_ref, ka_ref,
    q_ref, k_ref, v_ref, o_ref, qal_ref, n_ref, r_ref,
    w_ref, kt_ref, kat_ref,
):
    fetch(moves, core_ref, parts, w_ref, FIRST_ROWS)
    moves.first(x_ref, vec_ref, w_ref)
    for qb in range(TALLS):
        rows = pl.ds(qb * TALL, TALL)
        x = x_ref[rows, :]
        q_ref[rows, :] = ((nn(x, square(w_ref, 0)) + vec_row(vec_ref, 6)) * query_scale).astype(BF)
        k_ref[rows, :] = nn(x, square(w_ref, 1)).astype(BF)
        v_ref[rows, :] = (nn(x, square(w_ref, 2)) + vec_row(vec_ref, 7)).astype(BF)
    moves.need(qa_ref, ka_ref)
    for ref in (q_ref, k_ref, v_ref):
        moves.done(ref)
    attend_forward(moves, q_ref, k_ref, v_ref, qa_ref, ka_ref, o_ref, qal_ref, kt_ref, kat_ref, True)
    for qb in range(TALLS):
        rows = pl.ds(qb * TALL, TALL)
        resid = x_ref[rows, :].astype(F32) + nn(o_ref[rows, :], square(w_ref, 3)) + vec_row(vec_ref, 8)
        normed, inv_std = layer_norm(resid)
        n_ref[rows, :] = normed
        r_ref[rows, :] = jnp.broadcast_to(inv_std, (TALL, LANES))
        moves.done(n_ref, rows)
    moves.done(r_ref)


def cross_forward_kernel(
    moves, core_ref, parts, n1_ref, vec_ref, m_ref, qa_ref, ka_ref,
    q_ref, k_ref, v_ref, o_ref, qal_ref, n_ref, r_ref,
    w_ref, kt_ref, kat_ref,
):
    fetch(moves, core_ref, parts, w_ref)
    moves.first(m_ref, vec_ref, w_ref)
    for qb in range(TALLS):
        rows = pl.ds(qb * TALL, TALL)
        m = m_ref[rows, :]
        k_ref[rows, :] = nn(m, square(w_ref, 1)).astype(BF)
        v_ref[rows, :] = (nn(m, square(w_ref, 2)) + vec_row(vec_ref, 10)).astype(BF)
    moves.need(n1_ref)
    for qb in range(TALLS):
        rows = pl.ds(qb * TALL, TALL)
        h = (n1_ref[rows, :] * vec_row(vec_ref, 0) + vec_row(vec_ref, 1)).astype(BF)
        q_ref[rows, :] = ((nn(h, square(w_ref, 0)) + vec_row(vec_ref, 9)) * query_scale).astype(BF)
    moves.need(qa_ref, ka_ref)
    for ref in (q_ref, k_ref, v_ref):
        moves.done(ref)
    attend_forward(moves, q_ref, k_ref, v_ref, qa_ref, ka_ref, o_ref, qal_ref, kt_ref, kat_ref, False)
    for qb in range(TALLS):
        rows = pl.ds(qb * TALL, TALL)
        h = n1_ref[rows, :] * vec_row(vec_ref, 0) + vec_row(vec_ref, 1)
        resid = h + nn(o_ref[rows, :], square(w_ref, 3)) + vec_row(vec_ref, 11)
        normed, inv_std = layer_norm(resid)
        n_ref[rows, :] = normed
        r_ref[rows, :] = jnp.broadcast_to(inv_std, (TALL, LANES))
        moves.done(n_ref, rows)
    moves.done(r_ref)


def col_sum(x):
    return jnp.sum(x.astype(F32), axis=0, keepdims=True)


def ffn_kernel(
    moves, core_ref, parts, n2_ref, vec_ref, cot_ref, r2_ref,
    out_ref, mine_ref, other_ref, dr_ref, vg_ref,
    w1_ref, w2_ref, u_ref, da_ref, h_ref, dz_ref, f_ref, ht_ref,
):
    fetch(moves, core_ref, parts, w1_ref, 2 * ROWS)
    fetch(moves, core_ref, parts, w2_ref, 2 * ROWS, ROWS)

    def w1_block(j):
        return w1_ref[:, 64 * j : 64 * j + 64].reshape(D, D)

    def w2_block(j):
        return square(w2_ref, j)

    vg_ref[...] = jnp.zeros_like(vg_ref)
    moves.first(n2_ref, vec_ref, w1_ref, w2_ref)
    for tile in range(TALLS):
        rows = pl.ds(tile * TALL, TALL)
        n2 = n2_ref[rows, :]
        h2 = n2 * vec_row(vec_ref, 2) + vec_row(vec_ref, 3)
        h2_low = h2.astype(BF)
        h_ref[rows, :] = h2_low
        resid = h2 + vec_row(vec_ref, 16)
        for j in range(4):
            a = nn(h2_low, w1_block(j)) + vec_row(vec_ref, 12 + j)
            s = 0.5 * jnp.tanh(0.5 * a) + 0.5
            u = (a * s).astype(BF)
            u_ref[rows, j * D : (j + 1) * D] = u
            f_ref[:, j * D : (j + 1) * D] = s * (1.0 + a * (1.0 - s))
            moves.need(w2_ref)
            resid = resid + nn(u, w2_block(j))
        n3, inv3 = layer_norm(resid)
        gain3 = vec_row(vec_ref, 4)
        out_ref[rows, :] = (n3 * gain3 + vec_row(vec_ref, 5)).astype(BF)
        moves.done(out_ref, rows)
        moves.need(cot_ref)
        cot = cot_ref[rows, :].astype(F32)
        dr3 = norm_back(cot, n3, inv3, gain3)
        dz = dr3.astype(BF)
        dz_ref[rows, :] = dz
        vg_ref[4:5, :] += col_sum(cot * n3)
        vg_ref[5:6, :] += col_sum(cot)
        vg_ref[16:17, :] += col_sum(dz)
        dh = dr3
        for j in range(4):
            da = (nt(dz, w2_block(j)) * f_ref[:, j * D : (j + 1) * D]).astype(BF)
            da_ref[rows, j * D : (j + 1) * D] = da
            vg_ref[12 + j : 13 + j, :] += col_sum(da)
            dh = dh + nt(da, w1_block(j))
        vg_ref[2:3, :] += col_sum(dh * n2)
        vg_ref[3:4, :] += col_sum(dh)
        moves.need(r2_ref)
        dr2 = norm_back(dh, n2, r2_ref[rows, 0:1], vec_row(vec_ref, 2))
        dr_ref[rows, :] = dr2
        moves.done(dr_ref, rows)
        vg_ref[11:12, :] += col_sum(dr2.astype(BF))
    moves.done(vg_ref)
    core = core_ref[0]
    ht_ref[...] = jnp.swapaxes(h_ref[...].T.reshape(4, 2, 64, LEN), 0, 1).reshape(2, ROWS, LEN)
    dz = dz_ref[...]
    turned = jnp.concatenate([ht_ref[1 - core], ht_ref[core]], axis=0)
    for j in range(4):
        starts = [pl.multiple_of(j * D + h * ROWS, ROWS) for h in (1 - core, core)]
        cols = jnp.concatenate([u_ref[:, pl.ds(start, ROWS)] for start in starts], axis=1)
        dw1 = nn(turned, da_ref[:, j * D : (j + 1) * D]).astype(BF)
        dw2 = tn(cols, dz).astype(BF)
        for place, ref in enumerate((other_ref, mine_ref)):
            half = slice(place * ROWS, place * ROWS + ROWS)
            ref[:, 64 * j : 64 * j + 64, :] = dw1[half].reshape(4, 64, D)
            ref[j, ROWS:, :] = dw2[half]
            moves.done(ref, j, pl.ds(ROWS, ROWS))
    for j in range(4):
        for ref in (other_ref, mine_ref):
            moves.done(ref, j, pl.ds(0, ROWS))


def cross_backward_kernel(
    moves, core_ref, parts, dr2_ref, o_ref, q_ref, k_ref, v_ref, qal_ref, ka_ref, mt_ref, n1_ref, vec_ref, vf_ref, r1_ref,
    mine_ref, other_ref, dr1_ref, dk_ref, dv_ref,
    g_ref, do_ref, del_ref, dq_ref, p_ref, s_ref, h_ref, w_ref, vg_ref, kt_ref, dqt_ref,
):
    core = core_ref[0]
    fetch(moves, core_ref, parts, w_ref)
    moves.first(dr2_ref, w_ref, o_ref)
    for qb in range(TALLS):
        rows = pl.ds(qb * TALL, TALL)
        g_ref[rows, :] = dr2_ref[rows, :].astype(BF)
    mix_gradient(g_ref, square(w_ref, 3), o_ref, do_ref, del_ref)
    put_square_tn(mine_ref, other_ref, core, 3, o_ref, g_ref[...])
    moves.need(q_ref, k_ref, v_ref, qal_ref, ka_ref)
    attend_backward(
        q_ref, k_ref, v_ref, do_ref, qal_ref, del_ref, ka_ref, dq_ref, dk_ref, dv_ref, p_ref, s_ref, kt_ref, dqt_ref, False
    )
    moves.done(dk_ref)
    moves.done(dv_ref)
    moves.need(n1_ref, vec_ref, vf_ref, r1_ref, mt_ref)
    vg_ref[...] = vf_ref[...]
    for qb in range(TALLS):
        rows = pl.ds(qb * TALL, TALL)
        dq = dq_ref[rows, :]
        vg_ref[9:10, :] += col_sum(dq)
        vg_ref[10:11, :] += col_sum(dv_ref[rows, :])
        dh = dr2_ref[rows, :] + nt(dq, square(w_ref, 0))
        n1 = n1_ref[rows, :]
        vg_ref[0:1, :] += col_sum(dh * n1)
        vg_ref[1:2, :] += col_sum(dh)
        dr1 = norm_back(dh, n1, r1_ref[rows, 0:1], vec_row(vec_ref, 0))
        dr1_ref[rows, :] = dr1
        moves.done(dr1_ref, rows)
        vg_ref[8:9, :] += col_sum(dr1.astype(BF))
        h_ref[rows, :] = (n1 * vec_row(vec_ref, 0) + vec_row(vec_ref, 1)).astype(BF)
    blank = jnp.zeros((12, D), F32)
    for ref, half in ((mine_ref, core), (other_ref, 1 - core)):
        for xy in range(4):
            low, high = vg_ref[8 * xy : 8 * xy + 4, :], vg_ref[8 * xy + 4 : 8 * xy + 8, :]
            rows = jnp.where(half == 0, low, high)
            ref[xy, ROWS:, :] = jnp.concatenate([rows, blank], axis=0).astype(BF)
        moves.done(ref, 3)
    put_square(mine_ref, other_ref, core, 1, mt_ref, dk_ref[...])
    put_square(mine_ref, other_ref, core, 2, mt_ref, dv_ref[...])
    for ref in (mine_ref, other_ref):
        moves.done(ref, 1)
        moves.done(ref, 2)
    put_square_tn(mine_ref, other_ref, core, 0, h_ref, dq_ref[...])
    for ref in (mine_ref, other_ref):
        moves.done(ref, 0)


EARLY = pl.ds(0, EARLY_PAIRS * LANES)
LATE = pl.ds(EARLY_PAIRS * LANES, (PAIRS - EARLY_PAIRS) * LANES)
EVERY = slice(None)


def self_backward_start_kernel(
    moves, core_ref, parts, dr1_ref, o_ref, q_ref, k_ref, v_ref, qal_ref, ka_ref,
    do_ref, del_ref, dq_ref, dk_ref, dv_ref, so_ref,
    g_ref, p_ref, s_ref, w_ref, kt_ref, dqt_ref,
):
    core = core_ref[0]
    fetch(moves, core_ref, parts, w_ref, FIRST_ROWS)
    moves.first(dr1_ref, w_ref, o_ref)
    for qb in range(TALLS):
        rows = pl.ds(qb * TALL, TALL)
        g_ref[rows, :] = dr1_ref[rows, :].astype(BF)
    mix_gradient(g_ref, square(w_ref, 3), o_ref, do_ref, del_ref)
    moves.done(do_ref, EVERY, LATE)
    moves.done(del_ref)
    halves = [o_ref[:, pl.ds(pl.multiple_of(h * ROWS, ROWS), ROWS)] for h in (core, 1 - core)]
    so_ref[...] = tn(jnp.concatenate(halves, axis=1), g_ref[...]).astype(BF).reshape(2, ROWS, D)
    moves.done(so_ref)
    moves.need(q_ref, k_ref, v_ref, qal_ref, ka_ref)
    attend_backward(
        q_ref, k_ref, v_ref, do_ref, qal_ref, del_ref, ka_ref, dq_ref, dk_ref, dv_ref, p_ref, s_ref, kt_ref, dqt_ref, True,
        (0, EARLY_PAIRS),
    )
    for ref in (dq_ref, dk_ref, dv_ref):
        moves.done(ref, EVERY, EARLY)


def self_backward_end_kernel(
    moves, core_ref, q_ref, k_ref, v_ref, do_ref, qal_ref, del_ref, ka_ref, dqe_ref, dke_ref, dve_ref, xt_ref, so_ref,
    mine_ref, other_ref, dq_ref, dk_ref, dv_ref,
    p_ref, s_ref, late_ref, kt_ref, dqt_ref,
):
    core, chip = core_ref[0], core_ref[1]
    moves.first(q_ref, k_ref, v_ref, do_ref, qal_ref, del_ref, ka_ref)
    attend_backward(
        q_ref, k_ref, v_ref, do_ref, qal_ref, del_ref, ka_ref, dq_ref, dk_ref, dv_ref, p_ref, s_ref, kt_ref, dqt_ref, True,
        (EARLY_PAIRS, PAIRS),
    )
    for ref, source in ((dq_ref, dqe_ref), (dk_ref, dke_ref), (dv_ref, dve_ref)):
        moves.need(source)
        ref[:, EARLY] = source[:, EARLY]
        moves.done(ref)
    moves.need(xt_ref, so_ref)
    mine_ref[3 ^ chip, :ROWS, :] = so_ref[0]
    other_ref[3 ^ chip, :ROWS, :] = so_ref[1]
    late_ref[0:1, :] = col_sum(dq_ref[...])
    late_ref[1:2, :] = col_sum(dv_ref[...])
    for ref, half in ((mine_ref, core), (other_ref, 1 - core)):
        for xy in range(4):
            place = pl.multiple_of((2 * (xy % 2) + half) * LANES, LANES)
            piece = late_ref[xy // 2 : xy // 2 + 1, pl.ds(place, LANES)]
            after = lax.broadcasted_iota(jnp.int32, (16, LANES), 0) >= 4
            ref[xy ^ chip, ROWS:, :] = jnp.zeros((16, D), BF)
            ref[xy ^ chip, ROWS:, :LANES] = jnp.where(after, piece, 0.0).astype(BF)
        moves.done(ref, 3 ^ chip)
    for matrix, source in ((0, dq_ref), (1, dk_ref), (2, dv_ref)):
        put_square(mine_ref, other_ref, core, matrix, xt_ref, source[...], chip)
        moves.done(mine_ref, matrix ^ chip)
        moves.done(other_ref, matrix ^ chip)


def input_grads_kernel(
    moves, core_ref, parts, parts2, dr1_ref, dqs_ref, dks_ref, dvs_ref, dkc_ref, dvc_ref,
    ig_ref, mg_ref,
    w_ref, wc_ref,
):
    fetch(moves, core_ref, parts, w_ref, FIRST_ROWS)
    fetch(moves, core_ref, parts2, wc_ref)
    moves.first(w_ref, dr1_ref, dqs_ref, dks_ref, dvs_ref)
    for qb in range(TALLS):
        rows = pl.ds(qb * TALL, TALL)
        total = dr1_ref[rows, :] + nt(dqs_ref[rows, :], square(w_ref, 0))
        total = total + nt(dks_ref[rows, :], square(w_ref, 1))
        ig_ref[rows, :] = (total + nt(dvs_ref[rows, :], square(w_ref, 2))).astype(BF)
        moves.done(ig_ref, rows)
    moves.need(wc_ref, dkc_ref, dvc_ref)
    for qb in range(TALLS):
        rows = pl.ds(qb * TALL, TALL)
        total = nt(dkc_ref[rows, :], square(wc_ref, 1))
        mg_ref[rows, :] = (total + nt(dvc_ref[rows, :], square(wc_ref, 2))).astype(BF)
        moves.done(mg_ref, rows)


def call(kernel, outs, scratch, flops, core, parts, args, views=None):
    views = views or {}
    sds = [jax.ShapeDtypeStruct(shape, dtype) for shape, dtype in outs]
    arrays = [block for group in parts for block in group]
    moved = sum(a.size * a.dtype.itemsize for a in arrays + list(args))
    spaces = [pltpu.SMEM] + [pl.ANY] * (len(arrays) + len(args))
    memory = [pltpu.VMEM(a.shape, a.dtype) for a in args]
    memory += [pltpu.VMEM(shape, dtype) for shape, dtype in list(outs) + scratch]
    memory += [pltpu.SemaphoreType.DMA((64,))]

    def body(core_ref, *refs):
        groups = [refs[6 * i : 6 * i + 6] for i in range(len(parts))]
        refs = refs[6 * len(parts) :]
        given, refs = refs[: len(args)], refs[len(args) :]
        results, refs = refs[: len(outs)], refs[len(outs) :]
        held, refs = refs[: len(args)], refs[len(args) :]
        moves = Moves(refs[-1])
        for i, (source, target) in enumerate(zip(given, held)):
            if i in views:
                moves.bring(source.at[views[i]], target.at[views[i]], target)
            else:
                moves.bring(source, target, target)
        for place, result in zip(refs, results):
            moves.pair(place, result)
        kernel(moves, core_ref, *groups, *held, *refs[:-1])
        moves.finish()

    return pl.pallas_call(
        body,
        out_shape=sds,
        in_specs=[pl.BlockSpec(memory_space=space) for space in spaces],
        out_specs=[pl.BlockSpec(memory_space=pl.ANY)] * len(outs),
        scratch_shapes=memory,
        compiler_params=pltpu.CompilerParams(vmem_limit_bytes=VMEM_BYTES),
        cost_estimate=pl.CostEstimate(flops=flops, bytes_accessed=moved, transcendentals=0),
    )(core, *arrays, *args)


TOK = (LEN, D)
STAT = (LEN, LANES)
OCT = (8, ROWS, D)
unit = 2 * LEN * D * D
FORWARD_OUTS = [(TOK, BF)] * 4 + [(STAT, BF), (TOK, F32), (STAT, F32)]
HALVES = ((4, ROWS + 16, D), BF)
TOKB = (TOK, BF)
PROBS = ((2, LEN, LEN), BF)
TURN = ((D, LEN), BF)
TURN32 = ((D, LEN), F32)
FORWARD_SCRATCH = [(OCT, BF), TURN, ((LANES, LEN), BF)]


def self_forward(core, w, *args):
    return call(self_forward_kernel, FORWARD_OUTS, FORWARD_SCRATCH, 20 * unit, core, [w], args)


def cross_forward(core, w, *args):
    return call(cross_forward_kernel, FORWARD_OUTS, FORWARD_SCRATCH, 25 * unit, core, [w], args)


def ffn(core, w, *args):
    outs = [TOKB, ((4, 2 * ROWS, D), BF), ((4, 2 * ROWS, D), BF), (TOK, F32), ((32, D), F32)]
    scratch = [(OCT, BF), (OCT, BF), ((LEN, FF), BF), ((LEN, FF), BF), TOKB, TOKB]
    scratch += [((TALL, FF), F32), ((2, ROWS, LEN), BF)]
    return call(ffn_kernel, outs, scratch, 26 * unit, core, [w], args)


def cross_backward(core, w, *args):
    outs = [HALVES, HALVES, (TOK, F32), TOKB, TOKB]
    scratch = [TOKB, TOKB, (STAT, BF), TOKB, PROBS, PROBS, TOKB, (OCT, BF), ((32, D), F32), TURN, TURN32]
    return call(cross_backward_kernel, outs, scratch, 50 * unit, core, [w], args)


def self_backward_start(core, w, *args):
    outs = [TOKB, (STAT, BF), TOKB, TOKB, TOKB, ((2, ROWS, D), BF)]
    scratch = [TOKB, PROBS, PROBS, (OCT, BF), TURN, TURN32]
    return call(self_backward_start_kernel, outs, scratch, 25 * unit, core, [w], args)


def self_backward_end(core, *args):
    outs = [HALVES, HALVES, TOKB, TOKB, TOKB]
    scratch = [PROBS, PROBS, ((8, D), F32), TURN, TURN32]
    views = {i: (EVERY, LATE) for i in (0, 1, 2, 3)} | {i: (EVERY, EARLY) for i in (7, 8, 9)}
    return call(self_backward_end_kernel, outs, scratch, 12 * unit, core, [], args, views)


def input_grads(core, ws, wc, *args):
    scratch = [(OCT, BF), (OCT, BF)]
    return call(input_grads_kernel, [TOKB, TOKB], scratch, 6 * unit, core, [ws, wc], args)


SQUARES = 8 * D * D
VEC_ROWS = 17
VEC_LEN = VEC_ROWS * D


def groups_xy():
    return [[z * 8 + c * 2 + core for c in range(4)] for z in range(4) for core in range(2)]


def groups_z():
    return [[z * 8 + p for z in range(4)] for p in range(8)]


def swap(x, bit):
    return lax.ppermute(x, "dp", [(i, i ^ bit) for i in range(32)])


def turn_w1(chunk, here, out_first):
    if out_first:
        alt = chunk.reshape(64, 4, D).transpose(1, 0, 2).reshape(ROWS, D)
    else:
        alt = chunk.reshape(4, 64, D).transpose(1, 0, 2).reshape(ROWS, D)
    return jnp.where(here, alt, chunk)


def along_z(x, moves):
    return lax.ppermute(x, "dp", [(8 * a + p, 8 * b + p) for a, b in moves for p in range(8)])


def gather_blocks(params, index, others):
    low = params.astype(BF)
    share = low.shape[0]
    shift = share - ROWS * D
    z = index // 8
    prev = lax.ppermute(low[share - VEC_LEN :], "dp", [(i, (i + 1) % 32) for i in range(32)])
    flat = lax.dynamic_slice(jnp.concatenate([prev, low]), (VEC_LEN - shift * index,), (ROWS * D,))
    chunk = turn_w1(flat.reshape(ROWS, D), z == 2, True)
    vec = jnp.pad(prev.reshape(VEC_ROWS, D), ((0, 15), (0, 0)))
    mine = jnp.concatenate([chunk, vec])
    first = along_z(mine, ((0, 2), (1, 0), (2, 3), (3, 1)))
    first, others = lax.optimization_barrier((first, others))
    second = along_z(jnp.where(z == 2, first, mine), ((0, 1), (1, 2), (2, 3)))
    third = along_z(jnp.where(z == 1, first, mine)[:ROWS], ((3, 2), (2, 1), (1, 0)))
    second, third = lax.optimization_barrier((second, third))
    block0 = jnp.where(z == 0, mine, jnp.where(z == 2, first, second))
    fourth = along_z(jnp.where(z == 1, third, second[:ROWS]), ((1, 0), (2, 3)))
    pair0, near0 = to_sides(block0)
    near0, fourth = lax.optimization_barrier((near0, fourth))
    first, second = first[:ROWS], second[:ROWS]

    def pick(*blocks):
        return jnp.where(z < 2, jnp.where(z == 0, *blocks[:2]), jnp.where(z == 2, *blocks[2:]))

    block1 = pick(first, chunk, second, fourth)
    block2 = pick(fourth, third, chunk, first)
    block3 = pick(third, first, third, chunk)
    across0 = to_corners(near0)
    pair1, near1 = to_sides(block1)
    part0 = finish_block(pair0, near0, across0)
    across1 = to_corners(near1)
    pair2, near2 = to_sides(jnp.concatenate([block2, block3]))
    core, chip = index % 2, index % 8 // 2
    rows = [part0[0], part0[1], part0[2], part0[2], part0[3], part0[3], part0[4], part0[5]]
    starts = [ROWS, ROWS, ROWS, 2 * ROWS + 32, ROWS, 2 * ROWS + 32, ROWS, ROWS]
    rows = jnp.stack([lax.slice_in_dim(a, s, s + 32) for a, s in zip(rows, starts)])
    place = jnp.where(chip == 0, core, jnp.where(chip == 3, 6 + core, jnp.where(chip == 1 + core, 2 + core, 5 - core)))
    source = lax.dynamic_index_in_dim(rows, place, 0, keepdims=False)
    return part0, (pair1, near1, across1), (pair2, near2), source.astype(F32), others


def sides(first, second):
    return [(i, i ^ (first if i % 2 == 0 else second)) for i in range(32)]


def to_sides(block):
    pair = (block, swap(block, 1))
    return pair, lax.ppermute(jnp.concatenate(pair), "dp", sides(2, 4))


def to_corners(near):
    return lax.ppermute(near[: near.shape[0] // 2], "dp", sides(4, 2))


def finish_block(pair, near, across):
    return [*pair, near, swap(near, 1), across, swap(across, 1)]


def gather_plain(params, index, others):
    flat = lax.all_gather(params.astype(BF), "dp", axis=0, tiled=True)
    end = SQUARES + D * FF
    w1 = flat[SQUARES:end].reshape(8, 64, 4, D).transpose(0, 2, 1, 3).reshape(8, ROWS, D)
    w2 = flat[end : end + D * FF].reshape(8, ROWS, D)
    vec = flat[end + D * FF :].reshape(VEC_ROWS, D).astype(F32)
    mats = flat[:SQUARES].reshape(2, 4, 2, ROWS, D)

    core = index % 2

    def parts(pairs, rows):
        pairs = jnp.pad(pairs, ((0, 0), (0, 0), (0, rows - pairs.shape[2]), (0, 0)))
        own = lax.dynamic_index_in_dim(pairs, core, 1, keepdims=False)
        other = lax.dynamic_index_in_dim(pairs, 1 - core, 1, keepdims=False)
        one, two = jnp.concatenate([own, other], axis=1), jnp.concatenate([other, own], axis=1)
        near = lax.dynamic_index_in_dim(one, 1 + core, 0, keepdims=False)
        far = lax.dynamic_index_in_dim(two, 2 - core, 0, keepdims=False)
        return [own[0], other[0], near, far, own[3], other[3]]

    vec = jnp.pad(vec, ((0, 15), (0, 0)))
    wide = jnp.concatenate([w1.reshape(4, 2, ROWS, D), w2.reshape(4, 2, ROWS, D)], axis=2)
    return parts(mats[0], FIRST_ROWS), parts(mats[1], ROWS), parts(wide, 2 * ROWS), vec, others


def plane_sum(mine, other):
    pair = (mine.astype(F32) + swap(other, 1).astype(F32)).astype(BF)
    parts = lax.all_to_all(pair, "dp", 0, 0, tiled=True, axis_index_groups=groups_xy())
    return jnp.sum(parts.astype(F32), axis=0).astype(BF)


def add(a, b):
    return (a.astype(F32) + b.astype(F32)).astype(BF)


def first_round(part_c, part_f, z):
    extra = part_c[ROWS:]
    part_1 = jnp.concatenate([part_f[:ROWS], extra])
    part_2 = jnp.concatenate([part_f[ROWS:], extra])
    return part_c, part_1, part_2, along_z(jnp.where(z == 0, part_1, part_c), ((0, 1), (3, 2)))


def finish_blocks(mine, other, blocks, grads, index):
    z = index // 8
    got = swap(other, 1)
    pairs = [(mine[j].astype(F32) + got[j].astype(F32)).astype(BF) for j in range(4)]
    part_c, part_1, part_2, early = blocks
    part = pairs[0].astype(F32) + swap(pairs[1], 2).astype(F32) + swap(pairs[2], 4).astype(F32)
    part = part + swap(pairs[3], 6).astype(F32)
    part, grads = lax.optimization_barrier((part, grads))
    part = (part + jnp.pad(part_c[ROWS:].astype(F32), ((ROWS, 0), (0, 0)))).astype(BF)
    left = jnp.where(z == 2, add(part_c, early), part)
    right = jnp.where(z == 1, add(part_1, early), part_2)
    got_left = along_z(left, ((1, 0), (2, 1), (3, 2)))
    got_right = along_z(right, ((0, 1), (1, 2), (2, 3)))
    last = jnp.where(z < 2, jnp.where(z == 0, part_c, add(part_2, got_right)), jnp.where(z == 2, add(part, got_left), part_1))
    got = along_z(last, ((2, 0), (0, 1), (3, 2), (1, 3)))
    own = jnp.where(z < 2, jnp.where(z == 0, part, part_c), jnp.where(z == 2, part_1, part_2)).astype(F32)
    own = own + jnp.where(z < 2, got_left, got_right).astype(F32) + got.astype(F32)
    chunk = own[:ROWS]
    flat = turn_w1(chunk, z == 2, False).reshape(ROWS * D)
    after = lax.ppermute(flat[:VEC_LEN], "dp", [(i + 1, i) for i in range(31)])
    pieces = jnp.concatenate(
        [
            lax.dynamic_index_in_dim(own[ROWS : ROWS + 4], z, 0, keepdims=False).reshape(4, LANES),
            own[ROWS + 4 : ROWS + 5, :LANES],
            jnp.full((3, LANES), jnp.sum(chunk * chunk)),
        ]
    )
    pieces = jnp.broadcast_to(pieces[None], (32, 8, LANES))
    pieces = lax.all_to_all(pieces, "dp", 0, 0, tiled=True)
    vec = pieces[:, :4].reshape(4, 8, D).transpose(1, 0, 2).reshape(32, D)
    late = jnp.pad(pieces[:8, 4].reshape(2, D), ((6, 9), (0, 0)))
    vec = (vec[:VEC_ROWS] + late).reshape(VEC_LEN)
    square = jnp.sum(pieces[:, 5, 0]) + jnp.sum(vec * vec)
    after = jnp.where(index == 31, vec, after)
    share = lax.dynamic_slice(jnp.concatenate([flat, after]), (272 * index,), (ROWS * D + 272,))
    return share, vec, square, grads


def share_plain(pairs, index, share_len):
    def joined(mine, other):
        low = jnp.where(index % 2 == 0, mine, other).astype(F32)
        return jnp.stack([low, jnp.where(index % 2 == 0, other, mine).astype(F32)], axis=1)

    self_g, cross_g, ffn_g = (joined(*pair) for pair in pairs)
    dw1 = ffn_g[:, :, :ROWS].reshape(8, 4, 64, D).transpose(0, 2, 1, 3)
    vec = cross_g[:, :, ROWS : ROWS + 4].reshape(32, D)
    late = jnp.pad(self_g[:, :, ROWS + 4, :LANES].reshape(2, D), ((6, 9), (0, 0)))
    vec = vec[:VEC_ROWS] + late
    parts = (self_g[:, :, :ROWS], cross_g[:, :, :ROWS], dw1, ffn_g[:, :, ROWS:], vec)
    flat = lax.psum(jnp.concatenate([g.reshape(-1) for g in parts]), "dp")
    share = lax.dynamic_slice(flat, (index * share_len,), (share_len,))
    return share, flat[-VEC_LEN:], jnp.sum(flat * flat)


def shards(count, targets, memory, target_ids, memory_ids, cotangent, params, first_moment, second_moment):
    index = lax.axis_index("dp")
    blocked = count == 32
    place = jnp.where(blocked, index % 8 // 2, 0)
    core = jnp.stack([index % 2, place]).astype(jnp.int32)
    lane = jnp.arange(LANES)[None, :] - MASK_LANE
    live = (lane >= 0) & (lane < 8)
    same_t = lane == target_ids[:, None]
    same_m = lane == memory_ids[:, None]
    others = (
        jnp.where(live & ~same_t, masked_value, 0.0).astype(BF),
        jnp.where(same_t, 1.0, 0.0).astype(BF),
        jnp.where(same_m, 1.0, 0.0).astype(BF),
        memory.T,
        targets.T,
        core,
    )
    gather = gather_blocks if blocked else gather_plain
    ws, wc, wide, vec, others = gather(params, index, others)
    qa, ka_self, ka_cross, memory_turn, targets_turn, core = others
    qs, ks, vs, os, qal_s, n1, r1 = self_forward(core, ws, targets, vec, qa, ka_self)
    if blocked:
        wc, wide, n1 = lax.optimization_barrier((wc, wide, n1))
        wc = finish_block(*wc)
        across = to_corners(wide[1])
    qc, kc, vc, oc, qal_c, n2, r2 = cross_forward(core, wc, n1, vec, memory, qa, ka_cross)
    if blocked:
        across, n2 = lax.optimization_barrier((across, n2))
        wide = finish_block(*wide, across)
    out, mine_f, other_f, dr2, vg_f = ffn(core, wide, n2, vec, cotangent, r2)
    mine_c, other_c, dr1, dkc, dvc = cross_backward(
        core, wc, dr2, oc, qc, kc, vc, qal_c, ka_cross, memory_turn, n1, vec, vg_f, r1
    )
    if blocked:
        part_f = plane_sum(mine_f, other_f)
        part_f, mine_c, other_c, dr1 = lax.optimization_barrier((part_f, mine_c, other_c, dr1))
        part_c = plane_sum(mine_c, other_c)
    early = self_backward_start(core, ws, dr1, os, qs, ks, vs, qal_s, ka_self)
    if blocked:
        part_c, early = lax.optimization_barrier((part_c, early))
        blocks = first_round(part_c, part_f, index // 8)
    mine_s, other_s, dqs, dks, dvs = self_backward_end(
        core, qs, ks, vs, early[0], qal_s, early[1], ka_self, *early[2:5], targets_turn, early[5]
    )
    input_grad, memory_grad = input_grads(core, ws, wc, dr1, dqs, dks, dvs, dkc, dvc)
    if blocked:
        blocks, mine_s, other_s = lax.optimization_barrier((blocks, mine_s, other_s))
        grads = (input_grad, memory_grad)
        grad, vec_total, square, grads = finish_blocks(mine_s, other_s, blocks, grads, index)
        input_grad, memory_grad = grads
    else:
        pairs = ((mine_s, other_s), (mine_c, other_c), (mine_f, other_f))
        grad, vec_total, square = share_plain(pairs, index, params.shape[0])
    norm_value = jnp.sqrt(square)
    factor = jnp.minimum(1.0, clip_limit / (norm_value + 1e-06))
    clipped = grad * factor
    new_first = beta_one * first_moment + (1.0 - beta_one) * clipped
    new_second = beta_two * second_moment + (1.0 - beta_two) * clipped * clipped
    first_hat = new_first / (1.0 - beta_one**STEP)
    second_hat = new_second / (1.0 - beta_two**STEP)
    new_params = params - step_rate * (
        first_hat / (jnp.sqrt(second_hat) + adam_eps) + weight_decay * params
    )
    return (
        out,
        input_grad,
        memory_grad,
        norm_value,
        grad,
        vec_total,
        new_params,
        new_first,
        new_second,
        new_params.astype(BF),
    )


def solution(mesh):
    rows, flat = P("dp", None), P("dp")
    return jax.shard_map(
        functools.partial(shards, mesh.shape["dp"]),
        mesh=mesh,
        in_specs=(rows, rows, flat, flat, rows, flat, flat, flat),
        out_specs=(rows, rows, rows, P(), flat, P(), flat, flat, flat, flat),
        check_vma=False,
    )
```

```python
import functools
import jax
import jax.numpy as jnp
from jax import lax
from jax.experimental import pallas as pl
from jax.experimental.pallas import tpu as pltpu
from jax.sharding import PartitionSpec as P

D = 512
FF = 2048
HEADS = 8
LEN = 1024
STEP = 10
ROWS = 256
BLOCKS = LEN // ROWS
TALL = 512
TALLS = LEN // TALL
LANES = 128
PAIRS = D // LANES
MASK_LANE = 32
FIRST_ROWS = ROWS + 32

eps_norm = 1e-05
beta_one = 0.9
beta_two = 0.999
adam_eps = 1e-08
step_rate = 0.05
weight_decay = 0.01
clip_limit = 1.0
masked_value = -1e30
log2_e = 1.4426950408889634
query_scale = 0.125 * log2_e
key_scale = 1.0 / log2_e
safe_least, safe_most = 2.0**-40, 2.0**40

BF = jnp.bfloat16
F32 = jnp.float32
VMEM_BYTES = 60 * 1024 * 1024


def nn(a, b):
    return jnp.dot(a, b, preferred_element_type=F32)


def nt(a, b):
    return lax.dot_general(a, b, (((1,), (1,)), ((), ())), preferred_element_type=F32)


def tn(a, b):
    return lax.dot_general(a, b, (((0,), (0,)), ((), ())), preferred_element_type=F32)


def layer_norm(resid):
    center = resid - jnp.mean(resid, axis=1, keepdims=True)
    inv_std = lax.rsqrt(jnp.mean(center * center, axis=1, keepdims=True) + eps_norm)
    return center * inv_std, inv_std


def norm_back(grad, normed, inv_std, gain):
    scaled = grad * gain
    return inv_std * (
        scaled
        - jnp.mean(scaled, axis=1, keepdims=True)
        - normed * jnp.mean(scaled * normed, axis=1, keepdims=True)
    )


def half_row(parity):
    lane = lax.broadcasted_iota(jnp.int32, (1, LANES), 1)
    inside = (lane // 64) == parity
    return jnp.where(inside, 1.0, 0.0).astype(BF)


def lane_row(first, count):
    lane = lax.broadcasted_iota(jnp.int32, (1, LANES), 1)
    inside = (lane >= first) & (lane < first + count)
    return jnp.where(inside, 1.0, 0.0).astype(BF)


def causal_bias(transposed):
    row = lax.broadcasted_iota(jnp.int32, (ROWS, ROWS), 0)
    col = lax.broadcasted_iota(jnp.int32, (ROWS, ROWS), 1)
    ok = (row <= col) if transposed else (col <= row)
    return jnp.where(ok, 0.0, masked_value)


def attend_forward(moves, q_ref, k_ref, v_ref, qa_ref, ka_ref, o_ref, qal_ref, kt_ref, kat_ref, causal):
    size, depth = (ROWS, 2) if causal else (2 * ROWS, 1)
    low = lax.broadcasted_iota(jnp.int32, (size, LANES), 1) < 64
    bias = causal_bias(False) if causal else None
    kt_ref[...] = k_ref[...].T
    kat_ref[...] = ka_ref[...].T

    def score(block, head):
        rows = pl.ds(block * size, size)
        lanes = pl.ds(head // 2 * LANES, LANES)
        keys = (block + 1) * size if causal else LEN
        q_cat = jnp.concatenate([q_ref[rows, lanes] * half_row(head % 2), qa_ref[rows, :]], axis=1)
        k_cat = jnp.concatenate([kt_ref[lanes, :keys], kat_ref[:, :keys]], axis=0)
        scores = nn(q_cat, k_cat)
        if causal:
            diag = scores[:, keys - size :] + bias
            scores = jnp.concatenate([scores[:, : keys - size], diag], axis=1) if block else diag
        return scores

    def parts_of(lse, head, lse_parts):
        place = lax.broadcasted_iota(jnp.int32, lse.shape, 1)
        first = lse.astype(BF).astype(F32)
        rest = lse - first
        second = rest.astype(BF).astype(F32)
        for i, part in enumerate((first, second, rest - second)):
            lse_parts = jnp.where(place == head * 3 + i, part, lse_parts)
        return lse_parts

    def finish(head, scores, lse_parts, least, most):
        half = half_row(head % 2)
        probs = jnp.exp2(scores).astype(BF)
        values = v_ref[: scores.shape[1], pl.ds(head // 2 * LANES, LANES)]
        mixed = nn(probs, values * half + (1.0 - half).astype(BF))
        turned = pltpu.roll(mixed, 64, 1)
        total = jnp.where(low, turned, mixed) if head % 2 == 0 else jnp.where(low, mixed, turned)
        lse_parts = parts_of(-jnp.log2(total), head, lse_parts)
        return mixed / turned, lse_parts, jnp.minimum(least, total), jnp.maximum(most, total)

    least = jnp.full((size, LANES), 1.0, F32)
    most = least
    for block in range(LEN // size):
        rows = pl.ds(block * size, size)
        waiting, outs = [], []
        lse_parts = jnp.zeros((size, LANES), F32)
        for step in range(HEADS + depth):
            if step < HEADS:
                waiting.append(score(block, step))
            if step >= depth:
                head = step - depth
                out, lse_parts, least, most = finish(head, waiting.pop(0), lse_parts, least, most)
                outs.append(out)
                if head % 2:
                    lanes = pl.ds(head // 2 * LANES, LANES)
                    o_ref[rows, lanes] = jnp.where(low, outs[-2], outs[-1]).astype(BF)
        qal_ref[rows, :] = (qa_ref[rows, :].astype(F32) + lse_parts).astype(BF)
    safe = (jnp.min(least) > safe_least) & (jnp.max(most) < safe_most)

    @pl.when(jnp.logical_not(safe))
    def _():
        for block in range(BLOCKS):
            rows = pl.ds(block * ROWS, ROWS)
            keys = (block + 1) * ROWS if causal else LEN
            qa = qa_ref[rows, :]

            def one_pair(pair, lse_parts):
                lanes = pl.ds(pl.multiple_of(pair * LANES, LANES), LANES)
                k_cat = jnp.concatenate([kt_ref[lanes, :keys], kat_ref[:, :keys]], axis=0)
                outs = []
                for parity in range(2):
                    half = half_row(parity)
                    scores = nn(jnp.concatenate([q_ref[rows, lanes] * half, qa], axis=1), k_cat)
                    if causal:
                        diag = scores[:, keys - ROWS :] + bias
                        scores = (
                            jnp.concatenate([scores[:, : keys - ROWS], diag], axis=1) if block else diag
                        )
                    top = jnp.max(scores, axis=1, keepdims=True)
                    probs = jnp.exp2(scores - top).astype(BF)
                    mixed = nn(probs, v_ref[:keys, lanes] * half + (1.0 - half).astype(BF))
                    turned = pltpu.roll(mixed, 64, 1)
                    outs.append(mixed / turned)
                    lse = -(top + jnp.log2(turned if parity == 0 else mixed))
                    lse_parts = parts_of(lse, pair * 2 + parity, lse_parts)
                lower = lax.broadcasted_iota(jnp.int32, (ROWS, LANES), 1) < 64
                o_ref[rows, lanes] = jnp.where(lower, outs[0], outs[1]).astype(BF)
                return lse_parts

            lse_parts = lax.fori_loop(0, PAIRS, one_pair, jnp.zeros((ROWS, LANES), F32))
            qal_ref[rows, :] = (qa.astype(F32) + lse_parts).astype(BF)

    moves.done(o_ref)
    moves.done(qal_ref)


def attend_backward(
    q_ref, k_ref, v_ref, do_ref, qal_ref, del_ref, ka_ref, dq_ref, dk_ref, dv_ref, p_ref, s_ref, kt_ref, dqt_ref,
    causal,
):
    bias = causal_bias(True) if causal else None
    kt_ref[...] = k_ref[...].T

    def score(head, block):
        lanes = pl.ds(head // 2 * LANES, LANES)
        half = half_row(head % 2)
        rows = pl.ds(block * ROWS, ROWS)
        keys = (block + 1) * ROWS if causal else LEN
        marks = ka_ref[:keys, :] + lane_row(head * 3, 3)
        k_cat = jnp.concatenate([k_ref[:keys, lanes] * half, marks], axis=1)
        ones = jnp.broadcast_to(lane_row(head * 2, 2), (keys, LANES))
        v_cat = jnp.concatenate([v_ref[:keys, lanes] * half, ones], axis=1)
        q_cat = jnp.concatenate([q_ref[rows, lanes], qal_ref[rows, :]], axis=1)
        do_cat = jnp.concatenate([do_ref[rows, lanes], del_ref[rows, :]], axis=1)
        return nt(k_cat, q_cat), nt(v_cat, do_cat)

    def finish(head, block, scores, grads):
        rows = pl.ds(block * ROWS, ROWS)
        keys = scores.shape[0]
        if causal:
            diag = scores[keys - ROWS :] + bias
            scores = jnp.concatenate([scores[: keys - ROWS], diag], axis=0) if block else diag
        probs = jnp.exp2(scores)
        p_ref[head % 2, :keys, rows] = probs.astype(BF)
        inner = (probs * grads).astype(BF)
        s_ref[head % 2, :keys, rows] = inner
        own = pl.ds(head * 64, 64)
        dqt_ref[own, rows] = nn(kt_ref[own, :keys], inner)

    def pair_end(pair):
        lanes = pl.ds(pair * LANES, LANES)
        for kb in range(BLOCKS):
            rows = pl.ds(kb * ROWS, ROWS)
            first = kb * ROWS if causal else 0
            tail = pl.ds(first, LEN - first)
            do_pair = do_ref[tail, lanes]
            q_pair = q_ref[tail, lanes]
            dv = nn(p_ref[0, rows, tail], do_pair * half_row(0))
            dv = dv + nn(p_ref[1, rows, tail], do_pair * half_row(1))
            dv_ref[rows, lanes] = dv.astype(BF)
            dk = nn(s_ref[0, rows, tail], q_pair * half_row(0))
            dk = dk + nn(s_ref[1, rows, tail], q_pair * half_row(1))
            dk_ref[rows, lanes] = (dk * key_scale).astype(BF)

    steps = [(h, b) for h in range(HEADS) for b in range(BLOCKS)]
    waiting = score(*steps[0])
    for place, (head, block) in enumerate(steps):
        current = waiting
        if place + 1 < len(steps):
            waiting = score(*steps[place + 1])
        finish(head, block, *current)
        if head % 2 and block == BLOCKS - 1:
            pair_end(head // 2)
    for block in range(BLOCKS):
        rows = pl.ds(block * ROWS, ROWS)
        dq_ref[rows, :] = (dqt_ref[:, rows] * 0.125).T.astype(BF)


def mix_gradient(g_ref, w_out, o_ref, do_ref, del_ref):
    lane = lax.broadcasted_iota(jnp.int32, (TALL, LANES), 1)
    even = lane % 2 == 0
    col = lax.broadcasted_iota(jnp.int32, (D, LANES), 0) // 64
    pick = jnp.where(lax.broadcasted_iota(jnp.int32, (D, LANES), 1) // 2 == col, -1.0, 0.0).astype(BF)
    for qb in range(TALLS):
        rows = pl.ds(qb * TALL, TALL)
        do = nt(g_ref[rows, :], w_out).astype(BF)
        do_ref[rows, :] = do
        prod = do.astype(F32) * o_ref[rows, :].astype(F32)
        high = prod.astype(BF)
        inner = nn(high, pick) + nn((prod - high.astype(F32)).astype(BF), pick)
        first = inner.astype(BF).astype(F32)
        del_ref[rows, :] = jnp.where(even, first, inner - first).astype(BF)


def vec_row(vec_ref, index):
    return vec_ref[index : index + 1, :]


class Moves:
    def __init__(self, sems):
        self.sems, self.used = sems, 0
        self.asked, self.inward, self.outward = {}, {}, []

    def copy(self, source, target):
        move = pltpu.make_async_copy(source, target, self.sems.at[self.used])
        self.used += 1
        move.start()
        return move

    def bring(self, source, target, key):
        self.asked.setdefault(id(key), []).append((source, target))

    def start(self, keys):
        for key in keys:
            for source, target in self.asked.pop(key, []):
                self.inward.setdefault(key, []).append(self.copy(source, target))

    def first(self, *refs):
        self.start([id(ref) for ref in refs])
        self.need(*refs)
        self.start(list(self.asked))

    def need(self, *refs):
        for ref in refs:
            for move in self.inward.pop(id(ref), []):
                move.wait()

    def pair(self, scratch, out):
        self.outs = getattr(self, "outs", {})
        self.outs[id(scratch)] = out

    def done(self, ref, *where):
        out = self.outs[id(ref)]
        if where:
            ref, out = ref.at[where], out.at[where]
        self.outward.append(self.copy(ref, out))

    def finish(self):
        for moves in self.inward.values():
            for move in moves:
                move.wait()
        for move in self.outward:
            move.wait()


def fetch(moves, core_ref, parts, w_ref, rows=ROWS, first=0):
    core, chip = core_ref[0], core_ref[1]
    near, far = chip ^ (1 + core), chip ^ (2 - core)
    own, other = core, 1 - core
    places = (
        (0, 0, chip, own),
        (1, 0, chip, other),
        (2, 0, near, own),
        (2, rows, near, other),
        (3, 0, far, other),
        (3, rows, far, own),
        (4, 0, chip ^ 3, own),
        (5, 0, chip ^ 3, other),
    )
    for part, start, place, half in places:
        source = parts[part].at[pl.ds(start + first, ROWS)]
        moves.bring(source, w_ref.at[2 * place + half], w_ref)


def square(w_ref, matrix):
    return w_ref[2 * matrix : 2 * matrix + 2].reshape(D, D)


def put_square(mine_ref, other_ref, core, matrix, turned_ref, grad, place=0):
    halves = [turned_ref[pl.ds(pl.multiple_of(h * ROWS, ROWS), ROWS), :] for h in (core, 1 - core)]
    both = nn(jnp.concatenate(halves, axis=0), grad).astype(BF)
    mine_ref[matrix ^ place, :ROWS, :] = both[:ROWS]
    other_ref[matrix ^ place, :ROWS, :] = both[ROWS:]


def put_square_tn(mine_ref, other_ref, core, matrix, left_ref, grad, place=0):
    halves = [left_ref[:, pl.ds(pl.multiple_of(h * ROWS, ROWS), ROWS)] for h in (core, 1 - core)]
    both = tn(jnp.concatenate(halves, axis=1), grad).astype(BF)
    mine_ref[matrix ^ place, :ROWS, :] = both[:ROWS]
    other_ref[matrix ^ place, :ROWS, :] = both[ROWS:]


def self_forward_kernel(
    moves, core_ref, parts, x_ref, vec_ref, qa_ref, ka_ref,
    q_ref, k_ref, v_ref, o_ref, qal_ref, n_ref, r_ref,
    w_ref, kt_ref, kat_ref,
):
    fetch(moves, core_ref, parts, w_ref, FIRST_ROWS)
    moves.first(x_ref, vec_ref, w_ref)
    for qb in range(TALLS):
        rows = pl.ds(qb * TALL, TALL)
        x = x_ref[rows, :]
        q_ref[rows, :] = ((nn(x, square(w_ref, 0)) + vec_row(vec_ref, 6)) * query_scale).astype(BF)
        k_ref[rows, :] = nn(x, square(w_ref, 1)).astype(BF)
        v_ref[rows, :] = (nn(x, square(w_ref, 2)) + vec_row(vec_ref, 7)).astype(BF)
    moves.need(qa_ref, ka_ref)
    for ref in (q_ref, k_ref, v_ref):
        moves.done(ref)
    attend_forward(moves, q_ref, k_ref, v_ref, qa_ref, ka_ref, o_ref, qal_ref, kt_ref, kat_ref, True)
    for qb in range(TALLS):
        rows = pl.ds(qb * TALL, TALL)
        resid = x_ref[rows, :].astype(F32) + nn(o_ref[rows, :], square(w_ref, 3)) + vec_row(vec_ref, 8)
        normed, inv_std = layer_norm(resid)
        n_ref[rows, :] = normed
        r_ref[rows, :] = jnp.broadcast_to(inv_std, (TALL, LANES))
        moves.done(n_ref, rows)
    moves.done(r_ref)


def cross_forward_kernel(
    moves, core_ref, parts, n1_ref, vec_ref, m_ref, qa_ref, ka_ref,
    q_ref, k_ref, v_ref, o_ref, qal_ref, n_ref, r_ref,
    w_ref, kt_ref, kat_ref,
):
    fetch(moves, core_ref, parts, w_ref)
    moves.first(m_ref, vec_ref, w_ref)
    for qb in range(TALLS):
        rows = pl.ds(qb * TALL, TALL)
        m = m_ref[rows, :]
        k_ref[rows, :] = nn(m, square(w_ref, 1)).astype(BF)
        v_ref[rows, :] = (nn(m, square(w_ref, 2)) + vec_row(vec_ref, 10)).astype(BF)
    moves.need(n1_ref)
    for qb in range(TALLS):
        rows = pl.ds(qb * TALL, TALL)
        h = (n1_ref[rows, :] * vec_row(vec_ref, 0) + vec_row(vec_ref, 1)).astype(BF)
        q_ref[rows, :] = ((nn(h, square(w_ref, 0)) + vec_row(vec_ref, 9)) * query_scale).astype(BF)
    moves.need(qa_ref, ka_ref)
    for ref in (q_ref, k_ref, v_ref):
        moves.done(ref)
    attend_forward(moves, q_ref, k_ref, v_ref, qa_ref, ka_ref, o_ref, qal_ref, kt_ref, kat_ref, False)
    for qb in range(TALLS):
        rows = pl.ds(qb * TALL, TALL)
        h = n1_ref[rows, :] * vec_row(vec_ref, 0) + vec_row(vec_ref, 1)
        resid = h + nn(o_ref[rows, :], square(w_ref, 3)) + vec_row(vec_ref, 11)
        normed, inv_std = layer_norm(resid)
        n_ref[rows, :] = normed
        r_ref[rows, :] = jnp.broadcast_to(inv_std, (TALL, LANES))
        moves.done(n_ref, rows)
    moves.done(r_ref)


def col_sum(x):
    return jnp.sum(x.astype(F32), axis=0, keepdims=True)


def ffn_kernel(
    moves, core_ref, parts, n2_ref, vec_ref, cot_ref, r2_ref,
    out_ref, mine_ref, other_ref, dr_ref, vg_ref,
    w1_ref, w2_ref, u_ref, da_ref, h_ref, dz_ref, f_ref, ht_ref,
):
    fetch(moves, core_ref, parts, w1_ref, 2 * ROWS)
    fetch(moves, core_ref, parts, w2_ref, 2 * ROWS, ROWS)

    def w1_block(j):
        return w1_ref[:, 64 * j : 64 * j + 64].reshape(D, D)

    def w2_block(j):
        return square(w2_ref, j)

    vg_ref[...] = jnp.zeros_like(vg_ref)
    moves.first(n2_ref, vec_ref, w1_ref, w2_ref)
    for tile in range(TALLS):
        rows = pl.ds(tile * TALL, TALL)
        n2 = n2_ref[rows, :]
        h2 = n2 * vec_row(vec_ref, 2) + vec_row(vec_ref, 3)
        h2_low = h2.astype(BF)
        h_ref[rows, :] = h2_low
        resid = h2 + vec_row(vec_ref, 16)
        for j in range(4):
            a = nn(h2_low, w1_block(j)) + vec_row(vec_ref, 12 + j)
            s = 0.5 * jnp.tanh(0.5 * a) + 0.5
            u = (a * s).astype(BF)
            u_ref[rows, j * D : (j + 1) * D] = u
            f_ref[:, j * D : (j + 1) * D] = s * (1.0 + a * (1.0 - s))
            moves.need(w2_ref)
            resid = resid + nn(u, w2_block(j))
        n3, inv3 = layer_norm(resid)
        gain3 = vec_row(vec_ref, 4)
        out_ref[rows, :] = (n3 * gain3 + vec_row(vec_ref, 5)).astype(BF)
        moves.done(out_ref, rows)
        moves.need(cot_ref)
        cot = cot_ref[rows, :].astype(F32)
        dr3 = norm_back(cot, n3, inv3, gain3)
        dz = dr3.astype(BF)
        dz_ref[rows, :] = dz
        vg_ref[4:5, :] += col_sum(cot * n3)
        vg_ref[5:6, :] += col_sum(cot)
        vg_ref[16:17, :] += col_sum(dz)
        dh = dr3
        for j in range(4):
            da = (nt(dz, w2_block(j)) * f_ref[:, j * D : (j + 1) * D]).astype(BF)
            da_ref[rows, j * D : (j + 1) * D] = da
            vg_ref[12 + j : 13 + j, :] += col_sum(da)
            dh = dh + nt(da, w1_block(j))
        vg_ref[2:3, :] += col_sum(dh * n2)
        vg_ref[3:4, :] += col_sum(dh)
        moves.need(r2_ref)
        dr2 = norm_back(dh, n2, r2_ref[rows, 0:1], vec_row(vec_ref, 2))
        dr_ref[rows, :] = dr2
        moves.done(dr_ref, rows)
        vg_ref[11:12, :] += col_sum(dr2.astype(BF))
    moves.done(vg_ref)
    core = core_ref[0]
    ht_ref[...] = jnp.swapaxes(h_ref[...].T.reshape(4, 2, 64, LEN), 0, 1).reshape(2, ROWS, LEN)
    dz = dz_ref[...]
    turned = jnp.concatenate([ht_ref[1 - core], ht_ref[core]], axis=0)
    for j in range(4):
        starts = [pl.multiple_of(j * D + h * ROWS, ROWS) for h in (1 - core, core)]
        cols = jnp.concatenate([u_ref[:, pl.ds(start, ROWS)] for start in starts], axis=1)
        dw1 = nn(turned, da_ref[:, j * D : (j + 1) * D]).astype(BF)
        dw2 = tn(cols, dz).astype(BF)
        for place, ref in enumerate((other_ref, mine_ref)):
            half = slice(place * ROWS, place * ROWS + ROWS)
            ref[:, 64 * j : 64 * j + 64, :] = dw1[half].reshape(4, 64, D)
            ref[j, ROWS:, :] = dw2[half]
            moves.done(ref, j, pl.ds(ROWS, ROWS))
    for j in range(4):
        for ref in (other_ref, mine_ref):
            moves.done(ref, j, pl.ds(0, ROWS))


def cross_backward_kernel(
    moves, core_ref, parts, dr2_ref, o_ref, q_ref, k_ref, v_ref, qal_ref, ka_ref, mt_ref, n1_ref, vec_ref, vf_ref, r1_ref,
    mine_ref, other_ref, dr1_ref, dk_ref, dv_ref,
    g_ref, do_ref, del_ref, dq_ref, p_ref, s_ref, h_ref, w_ref, vg_ref, kt_ref, dqt_ref,
):
    core = core_ref[0]
    fetch(moves, core_ref, parts, w_ref)
    moves.first(dr2_ref, w_ref, o_ref)
    for qb in range(TALLS):
        rows = pl.ds(qb * TALL, TALL)
        g_ref[rows, :] = dr2_ref[rows, :].astype(BF)
    mix_gradient(g_ref, square(w_ref, 3), o_ref, do_ref, del_ref)
    put_square_tn(mine_ref, other_ref, core, 3, o_ref, g_ref[...])
    moves.need(q_ref, k_ref, v_ref, qal_ref, ka_ref)
    attend_backward(
        q_ref, k_ref, v_ref, do_ref, qal_ref, del_ref, ka_ref, dq_ref, dk_ref, dv_ref, p_ref, s_ref, kt_ref, dqt_ref, False
    )
    moves.done(dk_ref)
    moves.done(dv_ref)
    moves.need(n1_ref, vec_ref, vf_ref, r1_ref, mt_ref)
    vg_ref[...] = vf_ref[...]
    for qb in range(TALLS):
        rows = pl.ds(qb * TALL, TALL)
        dq = dq_ref[rows, :]
        vg_ref[9:10, :] += col_sum(dq)
        vg_ref[10:11, :] += col_sum(dv_ref[rows, :])
        dh = dr2_ref[rows, :] + nt(dq, square(w_ref, 0))
        n1 = n1_ref[rows, :]
        vg_ref[0:1, :] += col_sum(dh * n1)
        vg_ref[1:2, :] += col_sum(dh)
        dr1 = norm_back(dh, n1, r1_ref[rows, 0:1], vec_row(vec_ref, 0))
        dr1_ref[rows, :] = dr1
        moves.done(dr1_ref, rows)
        vg_ref[8:9, :] += col_sum(dr1.astype(BF))
        h_ref[rows, :] = (n1 * vec_row(vec_ref, 0) + vec_row(vec_ref, 1)).astype(BF)
    blank = jnp.zeros((12, D), F32)
    for ref, half in ((mine_ref, core), (other_ref, 1 - core)):
        for xy in range(4):
            low, high = vg_ref[8 * xy : 8 * xy + 4, :], vg_ref[8 * xy + 4 : 8 * xy + 8, :]
            rows = jnp.where(half == 0, low, high)
            ref[xy, ROWS:, :] = jnp.concatenate([rows, blank], axis=0).astype(BF)
        moves.done(ref, 3)
    put_square(mine_ref, other_ref, core, 1, mt_ref, dk_ref[...])
    put_square(mine_ref, other_ref, core, 2, mt_ref, dv_ref[...])
    for ref in (mine_ref, other_ref):
        moves.done(ref, 1)
        moves.done(ref, 2)
    put_square_tn(mine_ref, other_ref, core, 0, h_ref, dq_ref[...])
    for ref in (mine_ref, other_ref):
        moves.done(ref, 0)


def self_backward_kernel(
    moves, core_ref, parts, dr1_ref, o_ref, q_ref, k_ref, v_ref, qal_ref, ka_ref, xt_ref,
    mine_ref, other_ref, dq_ref, dk_ref, dv_ref,
    g_ref, do_ref, del_ref, p_ref, s_ref, w_ref, late_ref, kt_ref, dqt_ref,
):
    core, chip = core_ref[0], core_ref[1]
    fetch(moves, core_ref, parts, w_ref, FIRST_ROWS)
    moves.first(dr1_ref, w_ref, o_ref)
    for qb in range(TALLS):
        rows = pl.ds(qb * TALL, TALL)
        g_ref[rows, :] = dr1_ref[rows, :].astype(BF)
    mix_gradient(g_ref, square(w_ref, 3), o_ref, do_ref, del_ref)
    put_square_tn(mine_ref, other_ref, core, 3, o_ref, g_ref[...], chip)
    moves.need(q_ref, k_ref, v_ref, qal_ref, ka_ref)
    attend_backward(
        q_ref, k_ref, v_ref, do_ref, qal_ref, del_ref, ka_ref, dq_ref, dk_ref, dv_ref, p_ref, s_ref, kt_ref, dqt_ref, True
    )
    for ref in (dq_ref, dk_ref, dv_ref):
        moves.done(ref)
    moves.need(xt_ref)
    late_ref[0:1, :] = col_sum(dq_ref[...])
    late_ref[1:2, :] = col_sum(dv_ref[...])
    for ref, half in ((mine_ref, core), (other_ref, 1 - core)):
        for xy in range(4):
            place = pl.multiple_of((2 * (xy % 2) + half) * LANES, LANES)
            piece = late_ref[xy // 2 : xy // 2 + 1, pl.ds(place, LANES)]
            after = lax.broadcasted_iota(jnp.int32, (16, LANES), 0) >= 4
            ref[xy ^ chip, ROWS:, :] = jnp.zeros((16, D), BF)
            ref[xy ^ chip, ROWS:, :LANES] = jnp.where(after, piece, 0.0).astype(BF)
        moves.done(ref, 3 ^ chip)
    for matrix, source in ((0, dq_ref), (1, dk_ref), (2, dv_ref)):
        put_square(mine_ref, other_ref, core, matrix, xt_ref, source[...], chip)
        moves.done(mine_ref, matrix ^ chip)
        moves.done(other_ref, matrix ^ chip)


def input_grads_kernel(
    moves, core_ref, parts, parts2, dr1_ref, dqs_ref, dks_ref, dvs_ref, dkc_ref, dvc_ref,
    ig_ref, mg_ref,
    w_ref, wc_ref,
):
    fetch(moves, core_ref, parts, w_ref, FIRST_ROWS)
    fetch(moves, core_ref, parts2, wc_ref)
    moves.first(w_ref, dr1_ref, dqs_ref, dks_ref, dvs_ref)
    for qb in range(TALLS):
        rows = pl.ds(qb * TALL, TALL)
        total = dr1_ref[rows, :] + nt(dqs_ref[rows, :], square(w_ref, 0))
        total = total + nt(dks_ref[rows, :], square(w_ref, 1))
        ig_ref[rows, :] = (total + nt(dvs_ref[rows, :], square(w_ref, 2))).astype(BF)
        moves.done(ig_ref, rows)
    moves.need(wc_ref, dkc_ref, dvc_ref)
    for qb in range(TALLS):
        rows = pl.ds(qb * TALL, TALL)
        total = nt(dkc_ref[rows, :], square(wc_ref, 1))
        mg_ref[rows, :] = (total + nt(dvc_ref[rows, :], square(wc_ref, 2))).astype(BF)
        moves.done(mg_ref, rows)


def call(kernel, outs, scratch, flops, core, parts, args):
    sds = [jax.ShapeDtypeStruct(shape, dtype) for shape, dtype in outs]
    arrays = [block for group in parts for block in group]
    moved = sum(a.size * a.dtype.itemsize for a in arrays + list(args))
    spaces = [pltpu.SMEM] + [pl.ANY] * (len(arrays) + len(args))
    memory = [pltpu.VMEM(a.shape, a.dtype) for a in args]
    memory += [pltpu.VMEM(shape, dtype) for shape, dtype in list(outs) + scratch]
    memory += [pltpu.SemaphoreType.DMA((64,))]

    def body(core_ref, *refs):
        groups = [refs[6 * i : 6 * i + 6] for i in range(len(parts))]
        refs = refs[6 * len(parts) :]
        given, refs = refs[: len(args)], refs[len(args) :]
        results, refs = refs[: len(outs)], refs[len(outs) :]
        held, refs = refs[: len(args)], refs[len(args) :]
        moves = Moves(refs[-1])
        for source, target in zip(given, held):
            moves.bring(source, target, target)
        for place, result in zip(refs, results):
            moves.pair(place, result)
        kernel(moves, core_ref, *groups, *held, *refs[:-1])
        moves.finish()

    return pl.pallas_call(
        body,
        out_shape=sds,
        in_specs=[pl.BlockSpec(memory_space=space) for space in spaces],
        out_specs=[pl.BlockSpec(memory_space=pl.ANY)] * len(outs),
        scratch_shapes=memory,
        compiler_params=pltpu.CompilerParams(vmem_limit_bytes=VMEM_BYTES),
        cost_estimate=pl.CostEstimate(flops=flops, bytes_accessed=moved, transcendentals=0),
    )(core, *arrays, *args)


TOK = (LEN, D)
STAT = (LEN, LANES)
OCT = (8, ROWS, D)
unit = 2 * LEN * D * D
FORWARD_OUTS = [(TOK, BF)] * 4 + [(STAT, BF), (TOK, F32), (STAT, F32)]
HALVES = ((4, ROWS + 16, D), BF)
TOKB = (TOK, BF)
PROBS = ((2, LEN, LEN), BF)
TURN = ((D, LEN), BF)
TURN32 = ((D, LEN), F32)
FORWARD_SCRATCH = [(OCT, BF), TURN, ((LANES, LEN), BF)]


def self_forward(core, w, *args):
    return call(self_forward_kernel, FORWARD_OUTS, FORWARD_SCRATCH, 20 * unit, core, [w], args)


def cross_forward(core, w, *args):
    return call(cross_forward_kernel, FORWARD_OUTS, FORWARD_SCRATCH, 25 * unit, core, [w], args)


def ffn(core, w, *args):
    outs = [TOKB, ((4, 2 * ROWS, D), BF), ((4, 2 * ROWS, D), BF), (TOK, F32), ((32, D), F32)]
    scratch = [(OCT, BF), (OCT, BF), ((LEN, FF), BF), ((LEN, FF), BF), TOKB, TOKB]
    scratch += [((TALL, FF), F32), ((2, ROWS, LEN), BF)]
    return call(ffn_kernel, outs, scratch, 26 * unit, core, [w], args)


def cross_backward(core, w, *args):
    outs = [HALVES, HALVES, (TOK, F32), TOKB, TOKB]
    scratch = [TOKB, TOKB, (STAT, BF), TOKB, PROBS, PROBS, TOKB, (OCT, BF), ((32, D), F32), TURN, TURN32]
    return call(cross_backward_kernel, outs, scratch, 50 * unit, core, [w], args)


def self_backward(core, w, *args):
    outs = [HALVES, HALVES, TOKB, TOKB, TOKB]
    scratch = [TOKB, TOKB, (STAT, BF), PROBS, PROBS, (OCT, BF), ((8, D), F32), TURN, TURN32]
    return call(self_backward_kernel, outs, scratch, 37 * unit, core, [w], args)


def input_grads(core, ws, wc, *args):
    scratch = [(OCT, BF), (OCT, BF)]
    return call(input_grads_kernel, [TOKB, TOKB], scratch, 6 * unit, core, [ws, wc], args)


SQUARES = 8 * D * D
VEC_ROWS = 17
VEC_LEN = VEC_ROWS * D


def groups_xy():
    return [[z * 8 + c * 2 + core for c in range(4)] for z in range(4) for core in range(2)]


def groups_z():
    return [[z * 8 + p for z in range(4)] for p in range(8)]


def swap(x, bit):
    return lax.ppermute(x, "dp", [(i, i ^ bit) for i in range(32)])


def turn_w1(chunk, here, out_first):
    if out_first:
        alt = chunk.reshape(64, 4, D).transpose(1, 0, 2).reshape(ROWS, D)
    else:
        alt = chunk.reshape(4, 64, D).transpose(1, 0, 2).reshape(ROWS, D)
    return jnp.where(here, alt, chunk)


def along_z(x, moves):
    return lax.ppermute(x, "dp", [(8 * a + p, 8 * b + p) for a, b in moves for p in range(8)])


def gather_blocks(params, index, others):
    low = params.astype(BF)
    share = low.shape[0]
    shift = share - ROWS * D
    z = index // 8
    prev = lax.ppermute(low[share - VEC_LEN :], "dp", [(i, (i + 1) % 32) for i in range(32)])
    flat = lax.dynamic_slice(jnp.concatenate([prev, low]), (VEC_LEN - shift * index,), (ROWS * D,))
    chunk = turn_w1(flat.reshape(ROWS, D), z == 2, True)
    vec = jnp.pad(prev.reshape(VEC_ROWS, D), ((0, 15), (0, 0)))
    mine = jnp.concatenate([chunk, vec])
    first = along_z(mine, ((0, 2), (1, 0), (2, 3), (3, 1)))
    first, others = lax.optimization_barrier((first, others))
    second = along_z(jnp.where(z == 2, first, mine), ((0, 1), (1, 2), (2, 3)))
    third = along_z(jnp.where(z == 1, first, mine)[:ROWS], ((3, 2), (2, 1), (1, 0)))
    second, third = lax.optimization_barrier((second, third))
    block0 = jnp.where(z == 0, mine, jnp.where(z == 2, first, second))
    fourth = along_z(jnp.where(z == 1, third, second[:ROWS]), ((1, 0), (2, 3)))
    pair0, near0 = to_sides(block0)
    near0, fourth = lax.optimization_barrier((near0, fourth))
    first, second = first[:ROWS], second[:ROWS]

    def pick(*blocks):
        return jnp.where(z < 2, jnp.where(z == 0, *blocks[:2]), jnp.where(z == 2, *blocks[2:]))

    block1 = pick(first, chunk, second, fourth)
    block2 = pick(fourth, third, chunk, first)
    block3 = pick(third, first, third, chunk)
    across0 = to_corners(near0)
    pair1, near1 = to_sides(block1)
    part0 = finish_block(pair0, near0, across0)
    across1 = to_corners(near1)
    pair2, near2 = to_sides(jnp.concatenate([block2, block3]))
    core, chip = index % 2, index % 8 // 2
    rows = [part0[0], part0[1], part0[2], part0[2], part0[3], part0[3], part0[4], part0[5]]
    starts = [ROWS, ROWS, ROWS, 2 * ROWS + 32, ROWS, 2 * ROWS + 32, ROWS, ROWS]
    rows = jnp.stack([lax.slice_in_dim(a, s, s + 32) for a, s in zip(rows, starts)])
    place = jnp.where(chip == 0, core, jnp.where(chip == 3, 6 + core, jnp.where(chip == 1 + core, 2 + core, 5 - core)))
    source = lax.dynamic_index_in_dim(rows, place, 0, keepdims=False)
    return part0, (pair1, near1, across1), (pair2, near2), source.astype(F32), others


def sides(first, second):
    return [(i, i ^ (first if i % 2 == 0 else second)) for i in range(32)]


def to_sides(block):
    pair = (block, swap(block, 1))
    return pair, lax.ppermute(jnp.concatenate(pair), "dp", sides(2, 4))


def to_corners(near):
    return lax.ppermute(near[: near.shape[0] // 2], "dp", sides(4, 2))


def finish_block(pair, near, across):
    return [*pair, near, swap(near, 1), across, swap(across, 1)]


def gather_plain(params, index, others):
    flat = lax.all_gather(params.astype(BF), "dp", axis=0, tiled=True)
    end = SQUARES + D * FF
    w1 = flat[SQUARES:end].reshape(8, 64, 4, D).transpose(0, 2, 1, 3).reshape(8, ROWS, D)
    w2 = flat[end : end + D * FF].reshape(8, ROWS, D)
    vec = flat[end + D * FF :].reshape(VEC_ROWS, D).astype(F32)
    mats = flat[:SQUARES].reshape(2, 4, 2, ROWS, D)

    core = index % 2

    def parts(pairs, rows):
        pairs = jnp.pad(pairs, ((0, 0), (0, 0), (0, rows - pairs.shape[2]), (0, 0)))
        own = lax.dynamic_index_in_dim(pairs, core, 1, keepdims=False)
        other = lax.dynamic_index_in_dim(pairs, 1 - core, 1, keepdims=False)
        one, two = jnp.concatenate([own, other], axis=1), jnp.concatenate([other, own], axis=1)
        near = lax.dynamic_index_in_dim(one, 1 + core, 0, keepdims=False)
        far = lax.dynamic_index_in_dim(two, 2 - core, 0, keepdims=False)
        return [own[0], other[0], near, far, own[3], other[3]]

    vec = jnp.pad(vec, ((0, 15), (0, 0)))
    wide = jnp.concatenate([w1.reshape(4, 2, ROWS, D), w2.reshape(4, 2, ROWS, D)], axis=2)
    return parts(mats[0], FIRST_ROWS), parts(mats[1], ROWS), parts(wide, 2 * ROWS), vec, others


def plane_parts(mine, other):
    pair = (mine.astype(F32) + swap(other, 1).astype(F32)).astype(BF)
    return lax.all_to_all(pair, "dp", 0, 0, tiled=True, axis_index_groups=groups_xy())


def summed(parts):
    return jnp.sum(parts.astype(F32), axis=0).astype(BF)


def add(a, b):
    return (a.astype(F32) + b.astype(F32)).astype(BF)


def first_round(parts_c, part_f, z):
    part_c = summed(parts_c)
    extra = part_c[ROWS:]
    part_1 = jnp.concatenate([part_f[:ROWS], extra])
    part_2 = jnp.concatenate([part_f[ROWS:], extra])
    return (part_c, part_1, part_2), jnp.where(z == 0, part_1, part_c)


def finish_blocks(mine, other, blocks, grads, index):
    z = index // 8
    got = swap(other, 1)
    pairs = [(mine[j].astype(F32) + got[j].astype(F32)).astype(BF) for j in range(4)]
    part_c, part_1, part_2, early = blocks
    part = pairs[0].astype(F32) + swap(pairs[1], 2).astype(F32) + swap(pairs[2], 4).astype(F32)
    part = part + swap(pairs[3], 6).astype(F32)
    part, grads = lax.optimization_barrier((part, grads))
    part = (part + jnp.pad(part_c[ROWS:].astype(F32), ((ROWS, 0), (0, 0)))).astype(BF)
    left = jnp.where(z == 2, add(part_c, early), part)
    right = jnp.where(z == 1, add(part_1, early), part_2)
    got_left = along_z(left, ((1, 0), (2, 1), (3, 2)))
    got_right = along_z(right, ((0, 1), (1, 2), (2, 3)))
    last = jnp.where(z < 2, jnp.where(z == 0, part_c, add(part_2, got_right)), jnp.where(z == 2, add(part, got_left), part_1))
    got = along_z(last, ((2, 0), (0, 1), (3, 2), (1, 3)))
    own = jnp.where(z < 2, jnp.where(z == 0, part, part_c), jnp.where(z == 2, part_1, part_2)).astype(F32)
    own = own + jnp.where(z < 2, got_left, got_right).astype(F32) + got.astype(F32)
    chunk = own[:ROWS]
    flat = turn_w1(chunk, z == 2, False).reshape(ROWS * D)
    after = lax.ppermute(flat[:VEC_LEN], "dp", [(i + 1, i) for i in range(31)])
    pieces = jnp.concatenate(
        [
            lax.dynamic_index_in_dim(own[ROWS : ROWS + 4], z, 0, keepdims=False).reshape(4, LANES),
            own[ROWS + 4 : ROWS + 5, :LANES],
            jnp.full((3, LANES), jnp.sum(chunk * chunk)),
        ]
    )
    pieces = jnp.broadcast_to(pieces[None], (32, 8, LANES))
    pieces = lax.all_to_all(pieces, "dp", 0, 0, tiled=True)
    vec = pieces[:, :4].reshape(4, 8, D).transpose(1, 0, 2).reshape(32, D)
    late = jnp.pad(pieces[:8, 4].reshape(2, D), ((6, 9), (0, 0)))
    vec = (vec[:VEC_ROWS] + late).reshape(VEC_LEN)
    square = jnp.sum(pieces[:, 5, 0]) + jnp.sum(vec * vec)
    after = jnp.where(index == 31, vec, after)
    share = lax.dynamic_slice(jnp.concatenate([flat, after]), (272 * index,), (ROWS * D + 272,))
    return share, vec, square, grads


def share_plain(pairs, index, share_len):
    def joined(mine, other):
        low = jnp.where(index % 2 == 0, mine, other).astype(F32)
        return jnp.stack([low, jnp.where(index % 2 == 0, other, mine).astype(F32)], axis=1)

    self_g, cross_g, ffn_g = (joined(*pair) for pair in pairs)
    dw1 = ffn_g[:, :, :ROWS].reshape(8, 4, 64, D).transpose(0, 2, 1, 3)
    vec = cross_g[:, :, ROWS : ROWS + 4].reshape(32, D)
    late = jnp.pad(self_g[:, :, ROWS + 4, :LANES].reshape(2, D), ((6, 9), (0, 0)))
    vec = vec[:VEC_ROWS] + late
    parts = (self_g[:, :, :ROWS], cross_g[:, :, :ROWS], dw1, ffn_g[:, :, ROWS:], vec)
    flat = lax.psum(jnp.concatenate([g.reshape(-1) for g in parts]), "dp")
    share = lax.dynamic_slice(flat, (index * share_len,), (share_len,))
    return share, flat[-VEC_LEN:], jnp.sum(flat * flat)


def shards(count, targets, memory, target_ids, memory_ids, cotangent, params, first_moment, second_moment):
    index = lax.axis_index("dp")
    blocked = count == 32
    place = jnp.where(blocked, index % 8 // 2, 0)
    core = jnp.stack([index % 2, place]).astype(jnp.int32)
    lane = jnp.arange(LANES)[None, :] - MASK_LANE
    live = (lane >= 0) & (lane < 8)
    same_t = lane == target_ids[:, None]
    same_m = lane == memory_ids[:, None]
    others = (
        jnp.where(live & ~same_t, masked_value, 0.0).astype(BF),
        jnp.where(same_t, 1.0, 0.0).astype(BF),
        jnp.where(same_m, 1.0, 0.0).astype(BF),
        memory.T,
        targets.T,
        core,
    )
    gather = gather_blocks if blocked else gather_plain
    ws, wc, wide, vec, others = gather(params, index, others)
    qa, ka_self, ka_cross, memory_turn, targets_turn, core = others
    qs, ks, vs, os, qal_s, n1, r1 = self_forward(core, ws, targets, vec, qa, ka_self)
    if blocked:
        wc, wide, n1 = lax.optimization_barrier((wc, wide, n1))
        wc = finish_block(*wc)
        across = to_corners(wide[1])
    qc, kc, vc, oc, qal_c, n2, r2 = cross_forward(core, wc, n1, vec, memory, qa, ka_cross)
    if blocked:
        across, n2 = lax.optimization_barrier((across, n2))
        wide = finish_block(*wide, across)
    out, mine_f, other_f, dr2, vg_f = ffn(core, wide, n2, vec, cotangent, r2)
    mine_c, other_c, dr1, dkc, dvc = cross_backward(
        core, wc, dr2, oc, qc, kc, vc, qal_c, ka_cross, memory_turn, n1, vec, vg_f, r1
    )
    if blocked:
        part_f = plane_parts(mine_f, other_f)
        part_f, mine_c, other_c, dr1 = lax.optimization_barrier((part_f, mine_c, other_c, dr1))
        part_c = plane_parts(mine_c, other_c)
        part_f, dr1 = lax.optimization_barrier((summed(part_f), dr1))
    mine_s, other_s, dqs, dks, dvs = self_backward(
        core, ws, dr1, os, qs, ks, vs, qal_s, ka_self, targets_turn
    )
    if blocked:
        part_c, part_f, mine_s = lax.optimization_barrier((part_c, part_f, mine_s))
        blocks, first_sent = first_round(part_c, part_f, index // 8)
        first_sent, dr1 = lax.optimization_barrier((first_sent, dr1))
        blocks += (along_z(first_sent, ((0, 1), (3, 2))),)
    input_grad, memory_grad = input_grads(core, ws, wc, dr1, dqs, dks, dvs, dkc, dvc)
    if blocked:
        grads = (input_grad, memory_grad)
        grad, vec_total, square, grads = finish_blocks(mine_s, other_s, blocks, grads, index)
        input_grad, memory_grad = grads
    else:
        pairs = ((mine_s, other_s), (mine_c, other_c), (mine_f, other_f))
        grad, vec_total, square = share_plain(pairs, index, params.shape[0])
    norm_value = jnp.sqrt(square)
    factor = jnp.minimum(1.0, clip_limit / (norm_value + 1e-06))
    clipped = grad * factor
    new_first = beta_one * first_moment + (1.0 - beta_one) * clipped
    new_second = beta_two * second_moment + (1.0 - beta_two) * clipped * clipped
    first_hat = new_first / (1.0 - beta_one**STEP)
    second_hat = new_second / (1.0 - beta_two**STEP)
    new_params = params - step_rate * (
        first_hat / (jnp.sqrt(second_hat) + adam_eps) + weight_decay * params
    )
    return (
        out,
        input_grad,
        memory_grad,
        norm_value,
        grad,
        vec_total,
        new_params,
        new_first,
        new_second,
        new_params.astype(BF),
    )


def solution(mesh):
    rows, flat = P("dp", None), P("dp")
    return jax.shard_map(
        functools.partial(shards, mesh.shape["dp"]),
        mesh=mesh,
        in_specs=(rows, rows, flat, flat, rows, flat, flat, flat),
        out_specs=(rows, rows, rows, P(), flat, P(), flat, flat, flat, flat),
        check_vma=False,
    )
```

```python
import functools
import jax
import jax.numpy as jnp
from jax import lax
from jax.experimental import pallas as pl
from jax.experimental.pallas import tpu as pltpu
from jax.sharding import PartitionSpec as P

D = 512
FF = 2048
HEADS = 8
LEN = 1024
STEP = 10
ROWS = 256
BLOCKS = LEN // ROWS
TALL = 512
TALLS = LEN // TALL
LANES = 128
PAIRS = D // LANES
MASK_LANE = 32
FIRST_ROWS = ROWS + 32

eps_norm = 1e-05
beta_one = 0.9
beta_two = 0.999
adam_eps = 1e-08
step_rate = 0.05
weight_decay = 0.01
clip_limit = 1.0
masked_value = -1e30
log2_e = 1.4426950408889634
query_scale = 0.125 * log2_e
key_scale = 1.0 / log2_e
safe_least, safe_most = 2.0**-40, 2.0**40

BF = jnp.bfloat16
F32 = jnp.float32
VMEM_BYTES = 60 * 1024 * 1024


def nn(a, b):
    return jnp.dot(a, b, preferred_element_type=F32)


def nt(a, b):
    return lax.dot_general(a, b, (((1,), (1,)), ((), ())), preferred_element_type=F32)


def tn(a, b):
    return lax.dot_general(a, b, (((0,), (0,)), ((), ())), preferred_element_type=F32)


def layer_norm(resid):
    center = resid - jnp.mean(resid, axis=1, keepdims=True)
    inv_std = lax.rsqrt(jnp.mean(center * center, axis=1, keepdims=True) + eps_norm)
    return center * inv_std, inv_std


def norm_back(grad, normed, inv_std, gain):
    scaled = grad * gain
    return inv_std * (
        scaled
        - jnp.mean(scaled, axis=1, keepdims=True)
        - normed * jnp.mean(scaled * normed, axis=1, keepdims=True)
    )


def half_row(parity):
    lane = lax.broadcasted_iota(jnp.int32, (1, LANES), 1)
    inside = (lane // 64) == parity
    return jnp.where(inside, 1.0, 0.0).astype(BF)


def lane_row(first, count):
    lane = lax.broadcasted_iota(jnp.int32, (1, LANES), 1)
    inside = (lane >= first) & (lane < first + count)
    return jnp.where(inside, 1.0, 0.0).astype(BF)


def causal_bias(transposed):
    row = lax.broadcasted_iota(jnp.int32, (ROWS, ROWS), 0)
    col = lax.broadcasted_iota(jnp.int32, (ROWS, ROWS), 1)
    ok = (row <= col) if transposed else (col <= row)
    return jnp.where(ok, 0.0, masked_value)


def attend_forward(moves, q_ref, k_ref, v_ref, qa_ref, ka_ref, o_ref, qal_ref, kt_ref, kat_ref, causal):
    size, depth = (ROWS, 2) if causal else (2 * ROWS, 1)
    low = lax.broadcasted_iota(jnp.int32, (size, LANES), 1) < 64
    bias = causal_bias(False) if causal else None
    kt_ref[...] = k_ref[...].T
    kat_ref[...] = ka_ref[...].T

    def score(block, head):
        rows = pl.ds(block * size, size)
        lanes = pl.ds(head // 2 * LANES, LANES)
        keys = (block + 1) * size if causal else LEN
        q_cat = jnp.concatenate([q_ref[rows, lanes] * half_row(head % 2), qa_ref[rows, :]], axis=1)
        k_cat = jnp.concatenate([kt_ref[lanes, :keys], kat_ref[:, :keys]], axis=0)
        scores = nn(q_cat, k_cat)
        if causal:
            diag = scores[:, keys - size :] + bias
            scores = jnp.concatenate([scores[:, : keys - size], diag], axis=1) if block else diag
        return scores

    def parts_of(lse, head, lse_parts):
        place = lax.broadcasted_iota(jnp.int32, lse.shape, 1)
        first = lse.astype(BF).astype(F32)
        rest = lse - first
        second = rest.astype(BF).astype(F32)
        for i, part in enumerate((first, second, rest - second)):
            lse_parts = jnp.where(place == head * 3 + i, part, lse_parts)
        return lse_parts

    def finish(head, scores, lse_parts, least, most):
        half = half_row(head % 2)
        probs = jnp.exp2(scores).astype(BF)
        values = v_ref[: scores.shape[1], pl.ds(head // 2 * LANES, LANES)]
        mixed = nn(probs, values * half + (1.0 - half).astype(BF))
        turned = pltpu.roll(mixed, 64, 1)
        total = jnp.where(low, turned, mixed) if head % 2 == 0 else jnp.where(low, mixed, turned)
        lse_parts = parts_of(-jnp.log2(total), head, lse_parts)
        return mixed / turned, lse_parts, jnp.minimum(least, total), jnp.maximum(most, total)

    least = jnp.full((size, LANES), 1.0, F32)
    most = least
    for block in range(LEN // size):
        rows = pl.ds(block * size, size)
        waiting, outs = [], []
        lse_parts = jnp.zeros((size, LANES), F32)
        for step in range(HEADS + depth):
            if step < HEADS:
                waiting.append(score(block, step))
            if step >= depth:
                head = step - depth
                out, lse_parts, least, most = finish(head, waiting.pop(0), lse_parts, least, most)
                outs.append(out)
                if head % 2:
                    lanes = pl.ds(head // 2 * LANES, LANES)
                    o_ref[rows, lanes] = jnp.where(low, outs[-2], outs[-1]).astype(BF)
        qal_ref[rows, :] = (qa_ref[rows, :].astype(F32) + lse_parts).astype(BF)
    safe = (jnp.min(least) > safe_least) & (jnp.max(most) < safe_most)

    @pl.when(jnp.logical_not(safe))
    def _():
        for block in range(BLOCKS):
            rows = pl.ds(block * ROWS, ROWS)
            keys = (block + 1) * ROWS if causal else LEN
            qa = qa_ref[rows, :]

            def one_pair(pair, lse_parts):
                lanes = pl.ds(pl.multiple_of(pair * LANES, LANES), LANES)
                k_cat = jnp.concatenate([kt_ref[lanes, :keys], kat_ref[:, :keys]], axis=0)
                outs = []
                for parity in range(2):
                    half = half_row(parity)
                    scores = nn(jnp.concatenate([q_ref[rows, lanes] * half, qa], axis=1), k_cat)
                    if causal:
                        diag = scores[:, keys - ROWS :] + bias
                        scores = (
                            jnp.concatenate([scores[:, : keys - ROWS], diag], axis=1) if block else diag
                        )
                    top = jnp.max(scores, axis=1, keepdims=True)
                    probs = jnp.exp2(scores - top).astype(BF)
                    mixed = nn(probs, v_ref[:keys, lanes] * half + (1.0 - half).astype(BF))
                    turned = pltpu.roll(mixed, 64, 1)
                    outs.append(mixed / turned)
                    lse = -(top + jnp.log2(turned if parity == 0 else mixed))
                    lse_parts = parts_of(lse, pair * 2 + parity, lse_parts)
                lower = lax.broadcasted_iota(jnp.int32, (ROWS, LANES), 1) < 64
                o_ref[rows, lanes] = jnp.where(lower, outs[0], outs[1]).astype(BF)
                return lse_parts

            lse_parts = lax.fori_loop(0, PAIRS, one_pair, jnp.zeros((ROWS, LANES), F32))
            qal_ref[rows, :] = (qa.astype(F32) + lse_parts).astype(BF)

    moves.done(o_ref)
    moves.done(qal_ref)


def attend_backward(
    q_ref, k_ref, v_ref, do_ref, qal_ref, del_ref, ka_ref, dq_ref, dk_ref, dv_ref, p_ref, s_ref, kt_ref, dqt_ref,
    causal,
):
    bias = causal_bias(True) if causal else None
    kt_ref[...] = k_ref[...].T

    def score(head, block):
        lanes = pl.ds(head // 2 * LANES, LANES)
        half = half_row(head % 2)
        rows = pl.ds(block * ROWS, ROWS)
        keys = (block + 1) * ROWS if causal else LEN
        marks = ka_ref[:keys, :] + lane_row(head * 3, 3)
        k_cat = jnp.concatenate([k_ref[:keys, lanes] * half, marks], axis=1)
        ones = jnp.broadcast_to(lane_row(head * 2, 2), (keys, LANES))
        v_cat = jnp.concatenate([v_ref[:keys, lanes] * half, ones], axis=1)
        q_cat = jnp.concatenate([q_ref[rows, lanes], qal_ref[rows, :]], axis=1)
        do_cat = jnp.concatenate([do_ref[rows, lanes], del_ref[rows, :]], axis=1)
        return nt(k_cat, q_cat), nt(v_cat, do_cat)

    def finish(head, block, scores, grads):
        rows = pl.ds(block * ROWS, ROWS)
        keys = scores.shape[0]
        if causal:
            diag = scores[keys - ROWS :] + bias
            scores = jnp.concatenate([scores[: keys - ROWS], diag], axis=0) if block else diag
        probs = jnp.exp2(scores)
        p_ref[head % 2, :keys, rows] = probs.astype(BF)
        inner = (probs * grads).astype(BF)
        s_ref[head % 2, :keys, rows] = inner
        own = pl.ds(head * 64, 64)
        dqt_ref[own, rows] = nn(kt_ref[own, :keys], inner)

    def pair_end(pair):
        lanes = pl.ds(pair * LANES, LANES)
        for kb in range(BLOCKS):
            rows = pl.ds(kb * ROWS, ROWS)
            first = kb * ROWS if causal else 0
            tail = pl.ds(first, LEN - first)
            do_pair = do_ref[tail, lanes]
            q_pair = q_ref[tail, lanes]
            dv = nn(p_ref[0, rows, tail], do_pair * half_row(0))
            dv = dv + nn(p_ref[1, rows, tail], do_pair * half_row(1))
            dv_ref[rows, lanes] = dv.astype(BF)
            dk = nn(s_ref[0, rows, tail], q_pair * half_row(0))
            dk = dk + nn(s_ref[1, rows, tail], q_pair * half_row(1))
            dk_ref[rows, lanes] = (dk * key_scale).astype(BF)

    steps = [(h, b) for h in range(HEADS) for b in range(BLOCKS)]
    waiting = score(*steps[0])
    for place, (head, block) in enumerate(steps):
        current = waiting
        if place + 1 < len(steps):
            waiting = score(*steps[place + 1])
        finish(head, block, *current)
        if head % 2 and block == BLOCKS - 1:
            pair_end(head // 2)
    for block in range(BLOCKS):
        rows = pl.ds(block * ROWS, ROWS)
        dq_ref[rows, :] = (dqt_ref[:, rows] * 0.125).T.astype(BF)


def mix_gradient(g_ref, w_out, o_ref, do_ref, del_ref):
    lane = lax.broadcasted_iota(jnp.int32, (LEN, LANES), 1)
    even = lane % 2 == 0
    col = lax.broadcasted_iota(jnp.int32, (D, LANES), 0) // 64
    pick = jnp.where(lax.broadcasted_iota(jnp.int32, (D, LANES), 1) // 2 == col, -1.0, 0.0).astype(BF)
    for qb in range(1):
        rows = pl.ds(qb * LEN, LEN)
        do = nt(g_ref[rows, :], w_out).astype(BF)
        do_ref[rows, :] = do
        prod = do.astype(F32) * o_ref[rows, :].astype(F32)
        high = prod.astype(BF)
        inner = nn(high, pick) + nn((prod - high.astype(F32)).astype(BF), pick)
        first = inner.astype(BF).astype(F32)
        del_ref[rows, :] = jnp.where(even, first, inner - first).astype(BF)


def vec_row(vec_ref, index):
    return vec_ref[index : index + 1, :]


class Moves:
    def __init__(self, sems):
        self.sems, self.used = sems, 0
        self.asked, self.inward, self.outward = {}, {}, []

    def copy(self, source, target):
        move = pltpu.make_async_copy(source, target, self.sems.at[self.used])
        self.used += 1
        move.start()
        return move

    def bring(self, source, target, key):
        self.asked.setdefault(id(key), []).append((source, target))

    def start(self, keys):
        for key in keys:
            for source, target in self.asked.pop(key, []):
                self.inward.setdefault(key, []).append(self.copy(source, target))

    def first(self, *refs):
        self.start([id(ref) for ref in refs])
        self.need(*refs)
        self.start(list(self.asked))

    def need(self, *refs):
        for ref in refs:
            for move in self.inward.pop(id(ref), []):
                move.wait()

    def pair(self, scratch, out):
        self.outs = getattr(self, "outs", {})
        self.outs[id(scratch)] = out

    def done(self, ref, *where):
        out = self.outs[id(ref)]
        if where:
            ref, out = ref.at[where], out.at[where]
        self.outward.append(self.copy(ref, out))

    def finish(self):
        for moves in self.inward.values():
            for move in moves:
                move.wait()
        for move in self.outward:
            move.wait()


def fetch(moves, core_ref, parts, w_ref, rows=ROWS, first=0):
    core, chip = core_ref[0], core_ref[1]
    near, far = chip ^ (1 + core), chip ^ (2 - core)
    own, other = core, 1 - core
    places = (
        (0, 0, chip, own),
        (1, 0, chip, other),
        (2, 0, near, own),
        (2, rows, near, other),
        (3, 0, far, other),
        (3, rows, far, own),
        (4, 0, chip ^ 3, own),
        (5, 0, chip ^ 3, other),
    )
    for part, start, place, half in places:
        source = parts[part].at[pl.ds(start + first, ROWS)]
        moves.bring(source, w_ref.at[2 * place + half], w_ref)


def square(w_ref, matrix):
    return w_ref[2 * matrix : 2 * matrix + 2].reshape(D, D)


def put_square(mine_ref, other_ref, core, matrix, turned_ref, grad, place=0):
    halves = [turned_ref[pl.ds(pl.multiple_of(h * ROWS, ROWS), ROWS), :] for h in (core, 1 - core)]
    both = nn(jnp.concatenate(halves, axis=0), grad).astype(BF)
    mine_ref[matrix ^ place, :ROWS, :] = both[:ROWS]
    other_ref[matrix ^ place, :ROWS, :] = both[ROWS:]


def put_square_tn(mine_ref, other_ref, core, matrix, left_ref, grad, place=0):
    halves = [left_ref[:, pl.ds(pl.multiple_of(h * ROWS, ROWS), ROWS)] for h in (core, 1 - core)]
    both = tn(jnp.concatenate(halves, axis=1), grad).astype(BF)
    mine_ref[matrix ^ place, :ROWS, :] = both[:ROWS]
    other_ref[matrix ^ place, :ROWS, :] = both[ROWS:]


def self_forward_kernel(
    moves, core_ref, parts, x_ref, vec_ref, qa_ref, ka_ref,
    q_ref, k_ref, v_ref, o_ref, qal_ref, n_ref, r_ref,
    w_ref, kt_ref, kat_ref,
):
    fetch(moves, core_ref, parts, w_ref, FIRST_ROWS)
    moves.first(x_ref, vec_ref, w_ref)
    for qb in range(TALLS):
        rows = pl.ds(qb * TALL, TALL)
        x = x_ref[rows, :]
        q_ref[rows, :] = ((nn(x, square(w_ref, 0)) + vec_row(vec_ref, 6)) * query_scale).astype(BF)
        k_ref[rows, :] = nn(x, square(w_ref, 1)).astype(BF)
        v_ref[rows, :] = (nn(x, square(w_ref, 2)) + vec_row(vec_ref, 7)).astype(BF)
    moves.need(qa_ref, ka_ref)
    for ref in (q_ref, k_ref, v_ref):
        moves.done(ref)
    attend_forward(moves, q_ref, k_ref, v_ref, qa_ref, ka_ref, o_ref, qal_ref, kt_ref, kat_ref, True)
    for qb in range(TALLS):
        rows = pl.ds(qb * TALL, TALL)
        resid = x_ref[rows, :].astype(F32) + nn(o_ref[rows, :], square(w_ref, 3)) + vec_row(vec_ref, 8)
        normed, inv_std = layer_norm(resid)
        n_ref[rows, :] = normed
        r_ref[rows, :] = jnp.broadcast_to(inv_std, (TALL, LANES))
        moves.done(n_ref, rows)
    moves.done(r_ref)


def cross_forward_kernel(
    moves, core_ref, parts, n1_ref, vec_ref, m_ref, qa_ref, ka_ref,
    q_ref, k_ref, v_ref, o_ref, qal_ref, n_ref, r_ref,
    w_ref, kt_ref, kat_ref,
):
    fetch(moves, core_ref, parts, w_ref)
    moves.first(m_ref, vec_ref, w_ref)
    for qb in range(TALLS):
        rows = pl.ds(qb * TALL, TALL)
        m = m_ref[rows, :]
        k_ref[rows, :] = nn(m, square(w_ref, 1)).astype(BF)
        v_ref[rows, :] = (nn(m, square(w_ref, 2)) + vec_row(vec_ref, 10)).astype(BF)
    moves.need(n1_ref)
    for qb in range(TALLS):
        rows = pl.ds(qb * TALL, TALL)
        h = (n1_ref[rows, :] * vec_row(vec_ref, 0) + vec_row(vec_ref, 1)).astype(BF)
        q_ref[rows, :] = ((nn(h, square(w_ref, 0)) + vec_row(vec_ref, 9)) * query_scale).astype(BF)
    moves.need(qa_ref, ka_ref)
    for ref in (q_ref, k_ref, v_ref):
        moves.done(ref)
    attend_forward(moves, q_ref, k_ref, v_ref, qa_ref, ka_ref, o_ref, qal_ref, kt_ref, kat_ref, False)
    for qb in range(TALLS):
        rows = pl.ds(qb * TALL, TALL)
        h = n1_ref[rows, :] * vec_row(vec_ref, 0) + vec_row(vec_ref, 1)
        resid = h + nn(o_ref[rows, :], square(w_ref, 3)) + vec_row(vec_ref, 11)
        normed, inv_std = layer_norm(resid)
        n_ref[rows, :] = normed
        r_ref[rows, :] = jnp.broadcast_to(inv_std, (TALL, LANES))
        moves.done(n_ref, rows)
    moves.done(r_ref)


def col_sum(x):
    return jnp.sum(x.astype(F32), axis=0, keepdims=True)


def ffn_kernel(
    moves, core_ref, parts, n2_ref, vec_ref, cot_ref, r2_ref,
    out_ref, mine_ref, other_ref, dr_ref, vg_ref,
    w1_ref, w2_ref, u_ref, da_ref, h_ref, dz_ref, f_ref, ht_ref,
):
    fetch(moves, core_ref, parts, w1_ref, 2 * ROWS)
    fetch(moves, core_ref, parts, w2_ref, 2 * ROWS, ROWS)

    def w1_block(j):
        return w1_ref[:, 64 * j : 64 * j + 64].reshape(D, D)

    def w2_block(j):
        return square(w2_ref, j)

    vg_ref[...] = jnp.zeros_like(vg_ref)
    moves.first(n2_ref, vec_ref, w1_ref, w2_ref)
    for tile in range(TALLS):
        rows = pl.ds(tile * TALL, TALL)
        n2 = n2_ref[rows, :]
        h2 = n2 * vec_row(vec_ref, 2) + vec_row(vec_ref, 3)
        h2_low = h2.astype(BF)
        h_ref[rows, :] = h2_low
        resid = h2 + vec_row(vec_ref, 16)
        for j in range(4):
            a = nn(h2_low, w1_block(j)) + vec_row(vec_ref, 12 + j)
            s = 0.5 * jnp.tanh(0.5 * a) + 0.5
            u = (a * s).astype(BF)
            u_ref[rows, j * D : (j + 1) * D] = u
            f_ref[:, j * D : (j + 1) * D] = s * (1.0 + a * (1.0 - s))
            moves.need(w2_ref)
            resid = resid + nn(u, w2_block(j))
        n3, inv3 = layer_norm(resid)
        gain3 = vec_row(vec_ref, 4)
        out_ref[rows, :] = (n3 * gain3 + vec_row(vec_ref, 5)).astype(BF)
        moves.done(out_ref, rows)
        moves.need(cot_ref)
        cot = cot_ref[rows, :].astype(F32)
        dr3 = norm_back(cot, n3, inv3, gain3)
        dz = dr3.astype(BF)
        dz_ref[rows, :] = dz
        vg_ref[4:5, :] += col_sum(cot * n3)
        vg_ref[5:6, :] += col_sum(cot)
        vg_ref[16:17, :] += col_sum(dz)
        dh = dr3
        for j in range(4):
            da = (nt(dz, w2_block(j)) * f_ref[:, j * D : (j + 1) * D]).astype(BF)
            da_ref[rows, j * D : (j + 1) * D] = da
            vg_ref[12 + j : 13 + j, :] += col_sum(da)
            dh = dh + nt(da, w1_block(j))
        vg_ref[2:3, :] += col_sum(dh * n2)
        vg_ref[3:4, :] += col_sum(dh)
        moves.need(r2_ref)
        dr2 = norm_back(dh, n2, r2_ref[rows, 0:1], vec_row(vec_ref, 2))
        dr_ref[rows, :] = dr2
        moves.done(dr_ref, rows)
        vg_ref[11:12, :] += col_sum(dr2.astype(BF))
    moves.done(vg_ref)
    core = core_ref[0]
    ht_ref[...] = jnp.swapaxes(h_ref[...].T.reshape(4, 2, 64, LEN), 0, 1).reshape(2, ROWS, LEN)
    dz = dz_ref[...]
    turned = jnp.concatenate([ht_ref[1 - core], ht_ref[core]], axis=0)
    for j in range(4):
        starts = [pl.multiple_of(j * D + h * ROWS, ROWS) for h in (1 - core, core)]
        cols = jnp.concatenate([u_ref[:, pl.ds(start, ROWS)] for start in starts], axis=1)
        dw1 = nn(turned, da_ref[:, j * D : (j + 1) * D]).astype(BF)
        dw2 = tn(cols, dz).astype(BF)
        for place, ref in enumerate((other_ref, mine_ref)):
            half = slice(place * ROWS, place * ROWS + ROWS)
            ref[:, 64 * j : 64 * j + 64, :] = dw1[half].reshape(4, 64, D)
            ref[j, ROWS:, :] = dw2[half]
            moves.done(ref, j, pl.ds(ROWS, ROWS))
    for j in range(4):
        for ref in (other_ref, mine_ref):
            moves.done(ref, j, pl.ds(0, ROWS))


def cross_backward_kernel(
    moves, core_ref, parts, dr2_ref, o_ref, q_ref, k_ref, v_ref, qal_ref, ka_ref, mt_ref, n1_ref, vec_ref, vf_ref, r1_ref,
    mine_ref, other_ref, dr1_ref, dk_ref, dv_ref,
    g_ref, do_ref, del_ref, dq_ref, p_ref, s_ref, h_ref, w_ref, vg_ref, kt_ref, dqt_ref,
):
    core = core_ref[0]
    fetch(moves, core_ref, parts, w_ref)
    moves.first(dr2_ref, w_ref, o_ref)
    for qb in range(1):
        rows = pl.ds(qb * LEN, LEN)
        g_ref[rows, :] = dr2_ref[rows, :].astype(BF)
    mix_gradient(g_ref, square(w_ref, 3), o_ref, do_ref, del_ref)
    put_square_tn(mine_ref, other_ref, core, 3, o_ref, g_ref[...])
    moves.need(q_ref, k_ref, v_ref, qal_ref, ka_ref)
    attend_backward(
        q_ref, k_ref, v_ref, do_ref, qal_ref, del_ref, ka_ref, dq_ref, dk_ref, dv_ref, p_ref, s_ref, kt_ref, dqt_ref, False
    )
    moves.done(dk_ref)
    moves.done(dv_ref)
    moves.need(n1_ref, vec_ref, vf_ref, r1_ref, mt_ref)
    vg_ref[...] = vf_ref[...]
    for qb in range(1):
        rows = pl.ds(qb * LEN, LEN)
        dq = dq_ref[rows, :]
        vg_ref[9:10, :] += col_sum(dq)
        vg_ref[10:11, :] += col_sum(dv_ref[rows, :])
        dh = dr2_ref[rows, :] + nt(dq, square(w_ref, 0))
        n1 = n1_ref[rows, :]
        vg_ref[0:1, :] += col_sum(dh * n1)
        vg_ref[1:2, :] += col_sum(dh)
        dr1 = norm_back(dh, n1, r1_ref[rows, 0:1], vec_row(vec_ref, 0))
        dr1_ref[rows, :] = dr1
        moves.done(dr1_ref, rows)
        vg_ref[8:9, :] += col_sum(dr1.astype(BF))
        h_ref[rows, :] = (n1 * vec_row(vec_ref, 0) + vec_row(vec_ref, 1)).astype(BF)
    blank = jnp.zeros((12, D), F32)
    for ref, half in ((mine_ref, core), (other_ref, 1 - core)):
        for xy in range(4):
            low, high = vg_ref[8 * xy : 8 * xy + 4, :], vg_ref[8 * xy + 4 : 8 * xy + 8, :]
            rows = jnp.where(half == 0, low, high)
            ref[xy, ROWS:, :] = jnp.concatenate([rows, blank], axis=0).astype(BF)
        moves.done(ref, 3)
    put_square(mine_ref, other_ref, core, 1, mt_ref, dk_ref[...])
    put_square(mine_ref, other_ref, core, 2, mt_ref, dv_ref[...])
    for ref in (mine_ref, other_ref):
        moves.done(ref, 1)
        moves.done(ref, 2)
    put_square_tn(mine_ref, other_ref, core, 0, h_ref, dq_ref[...])
    for ref in (mine_ref, other_ref):
        moves.done(ref, 0)


def self_backward_kernel(
    moves, core_ref, parts, dr1_ref, o_ref, q_ref, k_ref, v_ref, qal_ref, ka_ref, xt_ref,
    mine_ref, other_ref, dq_ref, dk_ref, dv_ref,
    g_ref, do_ref, del_ref, p_ref, s_ref, w_ref, late_ref, kt_ref, dqt_ref,
):
    core, chip = core_ref[0], core_ref[1]
    fetch(moves, core_ref, parts, w_ref, FIRST_ROWS)
    moves.first(dr1_ref, w_ref, o_ref)
    for qb in range(1):
        rows = pl.ds(qb * LEN, LEN)
        g_ref[rows, :] = dr1_ref[rows, :].astype(BF)
    mix_gradient(g_ref, square(w_ref, 3), o_ref, do_ref, del_ref)
    put_square_tn(mine_ref, other_ref, core, 3, o_ref, g_ref[...], chip)
    moves.need(q_ref, k_ref, v_ref, qal_ref, ka_ref)
    attend_backward(
        q_ref, k_ref, v_ref, do_ref, qal_ref, del_ref, ka_ref, dq_ref, dk_ref, dv_ref, p_ref, s_ref, kt_ref, dqt_ref, True
    )
    for ref in (dq_ref, dk_ref, dv_ref):
        moves.done(ref)
    moves.need(xt_ref)
    late_ref[0:1, :] = col_sum(dq_ref[...])
    late_ref[1:2, :] = col_sum(dv_ref[...])
    for ref, half in ((mine_ref, core), (other_ref, 1 - core)):
        for xy in range(4):
            place = pl.multiple_of((2 * (xy % 2) + half) * LANES, LANES)
            piece = late_ref[xy // 2 : xy // 2 + 1, pl.ds(place, LANES)]
            after = lax.broadcasted_iota(jnp.int32, (16, LANES), 0) >= 4
            ref[xy ^ chip, ROWS:, :] = jnp.zeros((16, D), BF)
            ref[xy ^ chip, ROWS:, :LANES] = jnp.where(after, piece, 0.0).astype(BF)
        moves.done(ref, 3 ^ chip)
    for matrix, source in ((0, dq_ref), (1, dk_ref), (2, dv_ref)):
        put_square(mine_ref, other_ref, core, matrix, xt_ref, source[...], chip)
        moves.done(mine_ref, matrix ^ chip)
        moves.done(other_ref, matrix ^ chip)


def input_grads_kernel(
    moves, core_ref, parts, parts2, dr1_ref, dqs_ref, dks_ref, dvs_ref, dkc_ref, dvc_ref,
    ig_ref, mg_ref,
    w_ref, wc_ref,
):
    fetch(moves, core_ref, parts, w_ref, FIRST_ROWS)
    fetch(moves, core_ref, parts2, wc_ref)
    moves.first(w_ref, dr1_ref, dqs_ref, dks_ref, dvs_ref)
    for qb in range(TALLS):
        rows = pl.ds(qb * TALL, TALL)
        total = dr1_ref[rows, :] + nt(dqs_ref[rows, :], square(w_ref, 0))
        total = total + nt(dks_ref[rows, :], square(w_ref, 1))
        ig_ref[rows, :] = (total + nt(dvs_ref[rows, :], square(w_ref, 2))).astype(BF)
        moves.done(ig_ref, rows)
    moves.need(wc_ref, dkc_ref, dvc_ref)
    for qb in range(TALLS):
        rows = pl.ds(qb * TALL, TALL)
        total = nt(dkc_ref[rows, :], square(wc_ref, 1))
        mg_ref[rows, :] = (total + nt(dvc_ref[rows, :], square(wc_ref, 2))).astype(BF)
        moves.done(mg_ref, rows)


def call(kernel, outs, scratch, flops, core, parts, args):
    sds = [jax.ShapeDtypeStruct(shape, dtype) for shape, dtype in outs]
    arrays = [block for group in parts for block in group]
    moved = sum(a.size * a.dtype.itemsize for a in arrays + list(args))
    spaces = [pltpu.SMEM] + [pl.ANY] * (len(arrays) + len(args))
    memory = [pltpu.VMEM(a.shape, a.dtype) for a in args]
    memory += [pltpu.VMEM(shape, dtype) for shape, dtype in list(outs) + scratch]
    memory += [pltpu.SemaphoreType.DMA((64,))]

    def body(core_ref, *refs):
        groups = [refs[6 * i : 6 * i + 6] for i in range(len(parts))]
        refs = refs[6 * len(parts) :]
        given, refs = refs[: len(args)], refs[len(args) :]
        results, refs = refs[: len(outs)], refs[len(outs) :]
        held, refs = refs[: len(args)], refs[len(args) :]
        moves = Moves(refs[-1])
        for source, target in zip(given, held):
            moves.bring(source, target, target)
        for place, result in zip(refs, results):
            moves.pair(place, result)
        kernel(moves, core_ref, *groups, *held, *refs[:-1])
        moves.finish()

    return pl.pallas_call(
        body,
        out_shape=sds,
        in_specs=[pl.BlockSpec(memory_space=space) for space in spaces],
        out_specs=[pl.BlockSpec(memory_space=pl.ANY)] * len(outs),
        scratch_shapes=memory,
        compiler_params=pltpu.CompilerParams(vmem_limit_bytes=VMEM_BYTES),
        cost_estimate=pl.CostEstimate(flops=flops, bytes_accessed=moved, transcendentals=0),
    )(core, *arrays, *args)


TOK = (LEN, D)
STAT = (LEN, LANES)
OCT = (8, ROWS, D)
unit = 2 * LEN * D * D
FORWARD_OUTS = [(TOK, BF)] * 4 + [(STAT, BF), (TOK, F32), (STAT, F32)]
HALVES = ((4, ROWS + 16, D), BF)
TOKB = (TOK, BF)
PROBS = ((2, LEN, LEN), BF)
TURN = ((D, LEN), BF)
TURN32 = ((D, LEN), F32)
FORWARD_SCRATCH = [(OCT, BF), TURN, ((LANES, LEN), BF)]


def self_forward(core, w, *args):
    return call(self_forward_kernel, FORWARD_OUTS, FORWARD_SCRATCH, 20 * unit, core, [w], args)


def cross_forward(core, w, *args):
    return call(cross_forward_kernel, FORWARD_OUTS, FORWARD_SCRATCH, 25 * unit, core, [w], args)


def ffn(core, w, *args):
    outs = [TOKB, ((4, 2 * ROWS, D), BF), ((4, 2 * ROWS, D), BF), (TOK, F32), ((32, D), F32)]
    scratch = [(OCT, BF), (OCT, BF), ((LEN, FF), BF), ((LEN, FF), BF), TOKB, TOKB]
    scratch += [((TALL, FF), F32), ((2, ROWS, LEN), BF)]
    return call(ffn_kernel, outs, scratch, 26 * unit, core, [w], args)


def cross_backward(core, w, *args):
    outs = [HALVES, HALVES, (TOK, F32), TOKB, TOKB]
    scratch = [TOKB, TOKB, (STAT, BF), TOKB, PROBS, PROBS, TOKB, (OCT, BF), ((32, D), F32), TURN, TURN32]
    return call(cross_backward_kernel, outs, scratch, 50 * unit, core, [w], args)


def self_backward(core, w, *args):
    outs = [HALVES, HALVES, TOKB, TOKB, TOKB]
    scratch = [TOKB, TOKB, (STAT, BF), PROBS, PROBS, (OCT, BF), ((8, D), F32), TURN, TURN32]
    return call(self_backward_kernel, outs, scratch, 37 * unit, core, [w], args)


def input_grads(core, ws, wc, *args):
    scratch = [(OCT, BF), (OCT, BF)]
    return call(input_grads_kernel, [TOKB, TOKB], scratch, 6 * unit, core, [ws, wc], args)


SQUARES = 8 * D * D
VEC_ROWS = 17
VEC_LEN = VEC_ROWS * D


def groups_xy():
    return [[z * 8 + c * 2 + core for c in range(4)] for z in range(4) for core in range(2)]


def groups_z():
    return [[z * 8 + p for z in range(4)] for p in range(8)]


def swap(x, bit):
    return lax.ppermute(x, "dp", [(i, i ^ bit) for i in range(32)])


def turn_w1(chunk, here, out_first):
    if out_first:
        alt = chunk.reshape(64, 4, D).transpose(1, 0, 2).reshape(ROWS, D)
    else:
        alt = chunk.reshape(4, 64, D).transpose(1, 0, 2).reshape(ROWS, D)
    return jnp.where(here, alt, chunk)


def along_z(x, moves):
    return lax.ppermute(x, "dp", [(8 * a + p, 8 * b + p) for a, b in moves for p in range(8)])


def gather_blocks(params, index, others):
    low = params.astype(BF)
    share = low.shape[0]
    shift = share - ROWS * D
    z = index // 8
    prev = lax.ppermute(low[share - VEC_LEN :], "dp", [(i, (i + 1) % 32) for i in range(32)])
    flat = lax.dynamic_slice(jnp.concatenate([prev, low]), (VEC_LEN - shift * index,), (ROWS * D,))
    chunk = turn_w1(flat.reshape(ROWS, D), z == 2, True)
    vec = jnp.pad(prev.reshape(VEC_ROWS, D), ((0, 15), (0, 0)))
    mine = jnp.concatenate([chunk, vec])
    first = along_z(mine, ((0, 2), (1, 0), (2, 3), (3, 1)))
    first, others = lax.optimization_barrier((first, others))
    second = along_z(jnp.where(z == 2, first, mine), ((0, 1), (1, 2), (2, 3)))
    third = along_z(jnp.where(z == 1, first, mine)[:ROWS], ((3, 2), (2, 1), (1, 0)))
    second, third = lax.optimization_barrier((second, third))
    block0 = jnp.where(z == 0, mine, jnp.where(z == 2, first, second))
    fourth = along_z(jnp.where(z == 1, third, second[:ROWS]), ((1, 0), (2, 3)))
    pair0, near0 = to_sides(block0)
    near0, fourth = lax.optimization_barrier((near0, fourth))
    first, second = first[:ROWS], second[:ROWS]

    def pick(*blocks):
        return jnp.where(z < 2, jnp.where(z == 0, *blocks[:2]), jnp.where(z == 2, *blocks[2:]))

    block1 = pick(first, chunk, second, fourth)
    block2 = pick(fourth, third, chunk, first)
    block3 = pick(third, first, third, chunk)
    across0 = to_corners(near0)
    pair1, near1 = to_sides(block1)
    part0 = finish_block(pair0, near0, across0)
    across1 = to_corners(near1)
    pair2, near2 = to_sides(jnp.concatenate([block2, block3]))
    core, chip = index % 2, index % 8 // 2
    rows = [part0[0], part0[1], part0[2], part0[2], part0[3], part0[3], part0[4], part0[5]]
    starts = [ROWS, ROWS, ROWS, 2 * ROWS + 32, ROWS, 2 * ROWS + 32, ROWS, ROWS]
    rows = jnp.stack([lax.slice_in_dim(a, s, s + 32) for a, s in zip(rows, starts)])
    place = jnp.where(chip == 0, core, jnp.where(chip == 3, 6 + core, jnp.where(chip == 1 + core, 2 + core, 5 - core)))
    source = lax.dynamic_index_in_dim(rows, place, 0, keepdims=False)
    return part0, (pair1, near1, across1), (pair2, near2), source.astype(F32), others


def sides(first, second):
    return [(i, i ^ (first if i % 2 == 0 else second)) for i in range(32)]


def to_sides(block):
    pair = (block, swap(block, 1))
    return pair, lax.ppermute(jnp.concatenate(pair), "dp", sides(2, 4))


def to_corners(near):
    return lax.ppermute(near[: near.shape[0] // 2], "dp", sides(4, 2))


def finish_block(pair, near, across):
    return [*pair, near, swap(near, 1), across, swap(across, 1)]


def gather_plain(params, index, others):
    flat = lax.all_gather(params.astype(BF), "dp", axis=0, tiled=True)
    end = SQUARES + D * FF
    w1 = flat[SQUARES:end].reshape(8, 64, 4, D).transpose(0, 2, 1, 3).reshape(8, ROWS, D)
    w2 = flat[end : end + D * FF].reshape(8, ROWS, D)
    vec = flat[end + D * FF :].reshape(VEC_ROWS, D).astype(F32)
    mats = flat[:SQUARES].reshape(2, 4, 2, ROWS, D)

    core = index % 2

    def parts(pairs, rows):
        pairs = jnp.pad(pairs, ((0, 0), (0, 0), (0, rows - pairs.shape[2]), (0, 0)))
        own = lax.dynamic_index_in_dim(pairs, core, 1, keepdims=False)
        other = lax.dynamic_index_in_dim(pairs, 1 - core, 1, keepdims=False)
        one, two = jnp.concatenate([own, other], axis=1), jnp.concatenate([other, own], axis=1)
        near = lax.dynamic_index_in_dim(one, 1 + core, 0, keepdims=False)
        far = lax.dynamic_index_in_dim(two, 2 - core, 0, keepdims=False)
        return [own[0], other[0], near, far, own[3], other[3]]

    vec = jnp.pad(vec, ((0, 15), (0, 0)))
    wide = jnp.concatenate([w1.reshape(4, 2, ROWS, D), w2.reshape(4, 2, ROWS, D)], axis=2)
    return parts(mats[0], FIRST_ROWS), parts(mats[1], ROWS), parts(wide, 2 * ROWS), vec, others


def plane_parts(mine, other):
    pair = (mine.astype(F32) + swap(other, 1).astype(F32)).astype(BF)
    return lax.all_to_all(pair, "dp", 0, 0, tiled=True, axis_index_groups=groups_xy())


def summed(parts):
    return jnp.sum(parts.astype(F32), axis=0).astype(BF)


def add(a, b):
    return (a.astype(F32) + b.astype(F32)).astype(BF)


def first_round(parts_c, part_f, z):
    part_c = summed(parts_c)
    extra = part_c[ROWS:]
    part_1 = jnp.concatenate([part_f[:ROWS], extra])
    part_2 = jnp.concatenate([part_f[ROWS:], extra])
    return (part_c, part_1, part_2), jnp.where(z == 0, part_1, part_c)


def finish_blocks(mine, other, blocks, grads, index):
    z = index // 8
    got = swap(other, 1)
    pairs = [(mine[j].astype(F32) + got[j].astype(F32)).astype(BF) for j in range(4)]
    part_c, part_1, part_2, early = blocks
    part = pairs[0].astype(F32) + swap(pairs[1], 2).astype(F32) + swap(pairs[2], 4).astype(F32)
    part = part + swap(pairs[3], 6).astype(F32)
    part, grads = lax.optimization_barrier((part, grads))
    part = (part + jnp.pad(part_c[ROWS:].astype(F32), ((ROWS, 0), (0, 0)))).astype(BF)
    left = jnp.where(z == 2, add(part_c, early), part)
    right = jnp.where(z == 1, add(part_1, early), part_2)
    got_left = along_z(left, ((1, 0), (2, 1), (3, 2)))
    got_right = along_z(right, ((0, 1), (1, 2), (2, 3)))
    last = jnp.where(z < 2, jnp.where(z == 0, part_c, add(part_2, got_right)), jnp.where(z == 2, add(part, got_left), part_1))
    got = along_z(last, ((2, 0), (0, 1), (3, 2), (1, 3)))
    own = jnp.where(z < 2, jnp.where(z == 0, part, part_c), jnp.where(z == 2, part_1, part_2)).astype(F32)
    own = own + jnp.where(z < 2, got_left, got_right).astype(F32) + got.astype(F32)
    chunk = own[:ROWS]
    flat = turn_w1(chunk, z == 2, False).reshape(ROWS * D)
    after = lax.ppermute(flat[:VEC_LEN], "dp", [(i + 1, i) for i in range(31)])
    pieces = jnp.concatenate(
        [
            lax.dynamic_index_in_dim(own[ROWS : ROWS + 4], z, 0, keepdims=False).reshape(4, LANES),
            own[ROWS + 4 : ROWS + 5, :LANES],
            jnp.full((3, LANES), jnp.sum(chunk * chunk)),
        ]
    )
    pieces = jnp.broadcast_to(pieces[None], (32, 8, LANES))
    pieces = lax.all_to_all(pieces, "dp", 0, 0, tiled=True)
    vec = pieces[:, :4].reshape(4, 8, D).transpose(1, 0, 2).reshape(32, D)
    late = jnp.pad(pieces[:8, 4].reshape(2, D), ((6, 9), (0, 0)))
    vec = (vec[:VEC_ROWS] + late).reshape(VEC_LEN)
    square = jnp.sum(pieces[:, 5, 0]) + jnp.sum(vec * vec)
    after = jnp.where(index == 31, vec, after)
    share = lax.dynamic_slice(jnp.concatenate([flat, after]), (272 * index,), (ROWS * D + 272,))
    return share, vec, square, grads


def share_plain(pairs, index, share_len):
    def joined(mine, other):
        low = jnp.where(index % 2 == 0, mine, other).astype(F32)
        return jnp.stack([low, jnp.where(index % 2 == 0, other, mine).astype(F32)], axis=1)

    self_g, cross_g, ffn_g = (joined(*pair) for pair in pairs)
    dw1 = ffn_g[:, :, :ROWS].reshape(8, 4, 64, D).transpose(0, 2, 1, 3)
    vec = cross_g[:, :, ROWS : ROWS + 4].reshape(32, D)
    late = jnp.pad(self_g[:, :, ROWS + 4, :LANES].reshape(2, D), ((6, 9), (0, 0)))
    vec = vec[:VEC_ROWS] + late
    parts = (self_g[:, :, :ROWS], cross_g[:, :, :ROWS], dw1, ffn_g[:, :, ROWS:], vec)
    flat = lax.psum(jnp.concatenate([g.reshape(-1) for g in parts]), "dp")
    share = lax.dynamic_slice(flat, (index * share_len,), (share_len,))
    return share, flat[-VEC_LEN:], jnp.sum(flat * flat)


def shards(count, targets, memory, target_ids, memory_ids, cotangent, params, first_moment, second_moment):
    index = lax.axis_index("dp")
    blocked = count == 32
    place = jnp.where(blocked, index % 8 // 2, 0)
    core = jnp.stack([index % 2, place]).astype(jnp.int32)
    lane = jnp.arange(LANES)[None, :] - MASK_LANE
    live = (lane >= 0) & (lane < 8)
    same_t = lane == target_ids[:, None]
    same_m = lane == memory_ids[:, None]
    others = (
        jnp.where(live & ~same_t, masked_value, 0.0).astype(BF),
        jnp.where(same_t, 1.0, 0.0).astype(BF),
        jnp.where(same_m, 1.0, 0.0).astype(BF),
        memory.T,
        targets.T,
        core,
    )
    gather = gather_blocks if blocked else gather_plain
    ws, wc, wide, vec, others = gather(params, index, others)
    qa, ka_self, ka_cross, memory_turn, targets_turn, core = others
    qs, ks, vs, os, qal_s, n1, r1 = self_forward(core, ws, targets, vec, qa, ka_self)
    if blocked:
        wc, wide, n1 = lax.optimization_barrier((wc, wide, n1))
        wc = finish_block(*wc)
        across = to_corners(wide[1])
    qc, kc, vc, oc, qal_c, n2, r2 = cross_forward(core, wc, n1, vec, memory, qa, ka_cross)
    if blocked:
        across, n2 = lax.optimization_barrier((across, n2))
        wide = finish_block(*wide, across)
    out, mine_f, other_f, dr2, vg_f = ffn(core, wide, n2, vec, cotangent, r2)
    mine_c, other_c, dr1, dkc, dvc = cross_backward(
        core, wc, dr2, oc, qc, kc, vc, qal_c, ka_cross, memory_turn, n1, vec, vg_f, r1
    )
    if blocked:
        part_f = plane_parts(mine_f, other_f)
        part_f, mine_c, other_c, dr1 = lax.optimization_barrier((part_f, mine_c, other_c, dr1))
        part_c = plane_parts(mine_c, other_c)
        part_f, dr1 = lax.optimization_barrier((summed(part_f), dr1))
    mine_s, other_s, dqs, dks, dvs = self_backward(
        core, ws, dr1, os, qs, ks, vs, qal_s, ka_self, targets_turn
    )
    if blocked:
        part_c, part_f, mine_s = lax.optimization_barrier((part_c, part_f, mine_s))
        blocks, first_sent = first_round(part_c, part_f, index // 8)
        first_sent, dr1 = lax.optimization_barrier((first_sent, dr1))
        blocks += (along_z(first_sent, ((0, 1), (3, 2))),)
    input_grad, memory_grad = input_grads(core, ws, wc, dr1, dqs, dks, dvs, dkc, dvc)
    if blocked:
        grads = (input_grad, memory_grad)
        grad, vec_total, square, grads = finish_blocks(mine_s, other_s, blocks, grads, index)
        input_grad, memory_grad = grads
    else:
        pairs = ((mine_s, other_s), (mine_c, other_c), (mine_f, other_f))
        grad, vec_total, square = share_plain(pairs, index, params.shape[0])
    norm_value = jnp.sqrt(square)
    factor = jnp.minimum(1.0, clip_limit / (norm_value + 1e-06))
    clipped = grad * factor
    new_first = beta_one * first_moment + (1.0 - beta_one) * clipped
    new_second = beta_two * second_moment + (1.0 - beta_two) * clipped * clipped
    first_hat = new_first / (1.0 - beta_one**STEP)
    second_hat = new_second / (1.0 - beta_two**STEP)
    new_params = params - step_rate * (
        first_hat / (jnp.sqrt(second_hat) + adam_eps) + weight_decay * params
    )
    return (
        out,
        input_grad,
        memory_grad,
        norm_value,
        grad,
        vec_total,
        new_params,
        new_first,
        new_second,
        new_params.astype(BF),
    )


def solution(mesh):
    rows, flat = P("dp", None), P("dp")
    return jax.shard_map(
        functools.partial(shards, mesh.shape["dp"]),
        mesh=mesh,
        in_specs=(rows, rows, flat, flat, rows, flat, flat, flat),
        out_specs=(rows, rows, rows, P(), flat, P(), flat, flat, flat, flat),
        check_vma=False,
    )
```
